256 devices in a mesh: gx: 4 (over x), gy: 8 (over y, core), gz: 8 (over z).
Axes of the slice: x: 4, y: 4, z: 8, core: 2. Of those that a mesh axis runs over, the one named last changes fastest.
Arguments:
- right_side: float32 [64, 256, 1024], P('gx', 'gy', 'gz'), may hold values from -6 to 6
- coefficient: float32 [64, 256, 1024], P('gx', 'gy', 'gz'), may hold values from 0.1 to 10
Outputs:
- solution: float32 [64, 256, 1024], P('gx', 'gy', 'gz')
The draws below stay inside these ranges and needn't reach their ends.
All inputs are finite; a program needn't handle non-finite values.
Results may differ from the reference program's by a relative error of at most 0.0003.
Values sent between devices are 32-bit elements; how exact they have to be, the bound alone decides.
No kernel may reach another device: no remote copies, remote signals or barrier semaphores. Data moves between devices by JAX's collectives and lax.ppermute only.
A program may use at most 192 MiB of HBM per device.

```python
import math
import jax
import jax.numpy as jnp
from jax import lax

FINE_LEVELS = 3
SWEEPS = 2
ITERS = 20
NX = 64
NY = 256
NZ = 1024


def draw_right_side(key, part):
    key = jax.random.fold_in(key, 11)
    extent = (NX, NY, NZ)
    rough = 1.5 * jax.random.normal(key, extent, jnp.float32)
    return jnp.clip(rough, -6.0, 6.0)


def level_of(rng, shape, cuts, smallest, high):
    gain, own = 1.0, jax.random.fold_in(rng, 6)
    for position, shards_of in cuts:
        draws = jnp.exp(jax.random.uniform(jax.random.fold_in(own, position), (shards_of,), jnp.float32, smallest / len(cuts), high / len(cuts)))
        gain = gain * jnp.repeat(draws, shape[position] // shards_of).reshape([-1 if axis == position else 1 for axis in range(len(shape))])
    return gain


def setup_inputs(seed: int = 0) -> dict:
    keys = jax.random.split(jax.random.key(seed), 3)
    right_side = draw_right_side(jax.random.fold_in(keys[2], 71), 0)
    coefficient = jnp.clip(jnp.exp(math.log(10.0) - 4.6051702 * jax.random.uniform(keys[1], (NX, NY, NZ), jnp.float32) ** level_of(keys[1], (NX, NY, NZ), ((0, 4), (1, 8), (2, 8)), -0.2, 0.2)), 0.1, 10.0)
    return dict(right_side=right_side, coefficient=coefficient)


SHIFTS = ((0, 1), (0, -1), (1, 1), (1, -1), (2, 1), (2, -1))


def window(values, margin, direction=0, offset=0):
    selector = [slice(margin, values.shape[dimension] - margin) for dimension in range(3)]
    selector[direction] = slice(margin + offset, values.shape[direction] - margin + offset)
    return values[tuple(selector)]


def coefficients(conduct):
    padded = jnp.pad(conduct, 1)
    present_all = jnp.pad(jnp.ones(conduct.shape, jnp.float32), 1)
    weights = []
    diagonal = jnp.zeros(conduct.shape, jnp.float32)
    for direction, offset in SHIFTS:
        beside = window(padded, 1, direction, offset)
        present = window(present_all, 1, direction, offset) > 0.5
        face_weight = jnp.where(present, 2.0 * conduct * beside / (conduct + beside), 0.0)
        weights.append(face_weight)
        diagonal = diagonal + jnp.where(present, face_weight, 2.0 * conduct)
    return weights, diagonal


def neighbours(padded, weights):
    summed = jnp.zeros(window(padded, 1).shape, padded.dtype)
    for (direction, offset), face_weight in zip(SHIFTS, weights):
        summed = summed + face_weight * window(padded, 1, direction, offset)
    return summed


def parity(extent):
    total = lax.broadcasted_iota(jnp.int32, extent, 0) + lax.broadcasted_iota(jnp.int32, extent, 1)
    total = total + lax.broadcasted_iota(jnp.int32, extent, 2)
    return total % 2


def half_sweep(potential, source, weights, diagonal, colour, colour_value, factor):
    summed = neighbours(jnp.pad(potential, 1), weights)
    update = (factor * source + summed) / diagonal
    return jnp.where(colour == colour_value, update, potential)


def restrict(values):
    a, b, c = values.shape
    return values.reshape(a // 2, 2, b // 2, 2, c // 2, 2).mean(axis=(1, 3, 5))


def prolong(values):
    return jnp.repeat(jnp.repeat(jnp.repeat(values, 2, 0), 2, 1), 2, 2)


def smooth(potential, source, weights, diagonal, colour, factor, sweeps):
    for _ in range(sweeps):
        for colour_value in (0, 1):
            potential = half_sweep(potential, source, weights, diagonal, colour, colour_value, factor)
    return potential


def reference(right_side, coefficient):
    source, conduct = right_side, coefficient
    stored = []
    for height in range(FINE_LEVELS + 1):
        factor = 4.0 ** height
        weights, diagonal = coefficients(conduct)
        colour = parity(source.shape)
        potential = smooth(jnp.zeros(source.shape, jnp.float32), source, weights, diagonal, colour, factor, SWEEPS)
        stored.append((potential, source, weights, diagonal, colour, factor))
        remainder = source - (diagonal * potential - neighbours(jnp.pad(potential, 1), weights)) / factor
        source = restrict(remainder)
        conduct = restrict(conduct)
    factor = 4.0 ** (FINE_LEVELS + 1)
    weights, diagonal = coefficients(conduct)
    colour = parity(source.shape)

    def coarse_step(_, potential):
        return smooth(potential, source, weights, diagonal, colour, factor, 1)

    correction = lax.fori_loop(0, ITERS, coarse_step, jnp.zeros(source.shape, jnp.float32))
    for potential, source, weights, diagonal, colour, factor in reversed(stored):
        potential = potential + prolong(correction)
        correction = smooth(potential, source, weights, diagonal, colour, factor, SWEEPS)
    return correction
```

```python
import functools

import jax
import jax.numpy as jnp
from jax import lax
from jax.experimental import pallas as pl
from jax.experimental.pallas import tpu as pltpu
from jax.sharding import PartitionSpec as P

SWEEPS = 2
ITERS = 20
F32 = jnp.float32
VMEM = pl.BlockSpec(memory_space=pltpu.VMEM)
SMEM = pl.BlockSpec(memory_space=pltpu.SMEM)


def lanes(rows):
    return lax.broadcasted_iota(jnp.int32, (rows, 128), 1)


def rows_of(rows):
    return lax.broadcasted_iota(jnp.int32, (rows, 128), 0)


def pick(values, index):
    return jnp.take_along_axis(values, index, axis=1, mode="promise_in_bounds")


def turn(values, shift):
    shift = shift % 128
    return pltpu.roll(values, shift, 1) if shift else values


def up(values):
    return pltpu.roll(values, values.shape[0] - 1, 0)


def down(values):
    return pltpu.roll(values, 1, 0)


def beside(other, x, q, colour, a):
    mid = other[x + 1, q]
    across = other[x + 1, 1 - q]
    back = (colour == 0) == ((a + q) % 2 == 0)
    return [
        other[x + 2, q],
        other[x, q],
        across if q == 0 else up(across),
        down(across) if q == 0 else across,
        mid,
        pltpu.roll(mid, 1 if back else 127, 1),
    ]


def planes(count, body):
    def pair(i, carry):
        for a in (0, 1):
            for q in (0, 1):
                body(2 * i + a, a, q)
        return carry

    lax.fori_loop(0, count // 2, pair, 0)


def set_up(count, rows, cond, src, wd, fd, dd):
    row = rows_of(rows)
    zero = jnp.zeros((2, rows, 128), F32)
    for colour in (0, 1):
        cond[colour, 0] = zero
        cond[colour, count + 1] = zero

    def body(x, a, q):
        for colour in (0, 1):
            other = cond.at[1 - colour]
            own = cond[colour, x + 1, q]
            near = beside(other, x, q, colour, a)
            if q == 0:
                near[3] = jnp.where(row > 0, near[3], 0.0)
            else:
                near[2] = jnp.where(row < rows - 1, near[2], 0.0)
            total = jnp.zeros((rows, 128), F32)
            faces = []
            for value in near:
                face = 2.0 * own * value / jnp.maximum(own + value, 1e-30)
                faces.append(face)
                total = total + jnp.where(value > 0.0, face, 2.0 * own)
            total = jnp.where(total > 0.0, total, 1.0)
            inverse = 1.0 / total
            for i, face in enumerate(faces):
                wd[colour, i, x, q] = face * inverse
            fd[colour, x, q] = src[colour, x, q] * inverse
            if colour == 0:
                dd[x, q] = total

    planes(count, body)


def relaxed(colour, x, a, q, v, wd, fd):
    near = beside(v.at[1 - colour], x, q, colour, a)
    total = fd[colour, x, q]
    for i, value in enumerate(near):
        total = total + wd[colour, i, x, q] * value
    return total


def half_sweep(colour, count, v, wd, fd):
    def body(x, a, q):
        v[colour, x + 1, q] = relaxed(colour, x, a, q, v, wd, fd)

    planes(count, body)


def clear_ends(count, rows, v):
    zero = jnp.zeros((2, rows, 128), F32)
    for colour in (0, 1):
        v[colour, 0] = zero
        v[colour, count + 1] = zero


def first_half(count, v, fd):
    def body(x, a, q):
        v[0, x + 1, q] = fd[0, x, q]

    planes(count, body)


def descend(count, rows, v, wd, fd, dd, cond, out_f, out_b):
    clear_ends(count, rows, v)
    first_half(count, v, fd)
    half_sweep(1, count, v, wd, fd)
    half_sweep(0, count, v, wd, fd)
    half_sweep(1, count, v, wd, fd)

    def body(i, carry):
        left = jnp.zeros((rows, 128), F32)
        mean = jnp.zeros((rows, 128), F32)
        for a in (0, 1):
            for q in (0, 1):
                x = 2 * i + a
                left = left + dd[x, q] * (relaxed(0, x, a, q, v, wd, fd) - v[0, x + 1, q])
                mean = mean + (cond[0, x + 1, q] + cond[1, x + 1, q])
        out_f[i] = 0.5 * left
        out_b[i] = 0.125 * mean
        return carry

    lax.fori_loop(0, count // 2, body, 0)


def ascend(count, v, wd, fd):
    for _ in range(SWEEPS):
        half_sweep(0, count, v, wd, fd)
        half_sweep(1, count, v, wd, fd)


def natural(v, x, a, q, shift, index):
    red, black = v[0, x + 1, q], v[1, x + 1, q]
    even, odd = (red, black) if (a + q) % 2 == 0 else (black, red)
    packed = jnp.where(lanes(even.shape[0]) < shift, even, turn(odd, shift))
    return pick(packed, index)


def split_kernel(f_ref, b_ref, lo_ref, hi_ref, zl_ref, zr_ref):
    lane = lanes(16)
    whole = 2 * (lane % 64) + lane // 64
    slot = lane // 8
    within = lane % 8
    first = 2 * (within % 4) + within // 4
    last = 120 + first
    for half, out in enumerate((lo_ref, hi_ref)):
        for q in (0, 1):
            left = jnp.zeros((16, 128), F32)
            right = jnp.zeros((16, 128), F32)
            for x in range(8):
                for arr, ref in enumerate((f_ref, b_ref)):
                    cells = ref[8 * half + x, pl.ds(q, 16, stride=2), :]
                    out[8 * arr + x, q] = pick(cells, whole)
                    here = slot == 2 * x + arr
                    left = jnp.where(here, pick(cells, first), left)
                    right = jnp.where(here, pick(cells, last), right)
            zl_ref[half, q] = left
            zr_ref[half, q] = right


def edge_kernel(a_ref, b_ref, c_ref, d_ref, lo_ref, hi_ref):
    for t, ref in enumerate((a_ref, b_ref, c_ref, d_ref)):
        def body(i, carry):
            for q in (0, 1):
                cells = ref[i, q]
                lo_ref[18 * t + i, 4 * q : 4 * q + 4] = cells[0:4]
                hi_ref[18 * t + i, 4 * q : 4 * q + 4] = cells[12:16]
            return carry

        lax.fori_loop(0, 18, body, 0)


def level0_down_kernel(
    scal, a_ref, b_ref, c_ref, d_ref, yl_ref, yr_ref,
    own_ref, zl_ref, zr_ref, black_ref, wd, fd,
    cond, src, v, dd, nat_f, nat_b,
):
    gx, gy, gz = scal[0], scal[1], scal[2]
    lane = lanes(24)
    row = rows_of(24)
    inside = (lane < 68) | (lane >= 124)
    inside = inside & ((gz > 0) | (lane < 124)) & ((gz < 7) | (lane < 64) | (lane >= 124))
    inside = inside & ((gy > 0) | (row >= 4)) & ((gy < 7) | (row < 20))
    keep = jnp.where(inside, 1.0, 0.0)
    for t, ref in enumerate((a_ref, b_ref, c_ref, d_ref)):
        here = keep
        if t == 0:
            here = keep * jnp.where(gx > 0, 1.0, 0.0)
        if t == 3:
            here = keep * jnp.where(gx < 3, 1.0, 0.0)

        def wide(i, q):
            return jnp.concatenate(
                [yl_ref[18 * t + i, 4 * q : 4 * q + 4], ref[i, q], yr_ref[18 * t + i, 4 * q : 4 * q + 4]], axis=0
            )

        ends = [(wide(16, q), wide(17, q)) for q in (0, 1)]
        for x in range(8):
            for q in (0, 1):
                from_left, from_right = ends[q]
                for arr in (0, 1):
                    s = 8 * (2 * x + arr)
                    main = wide(8 * arr + x, q)
                    even = jnp.where(
                        lane < 64, main,
                        jnp.where(lane < 96, turn(from_right, 64 - s), turn(from_left, 124 - s)),
                    )
                    odd = jnp.where(
                        lane < 64, turn(main, 64),
                        jnp.where(lane < 96, turn(from_right, 60 - s), turn(from_left, 120 - s)),
                    )
                    red, black = (even, odd) if (x + q) % 2 == 0 else (odd, even)
                    if arr == 0:
                        src[0, 8 * t + x, q] = red
                        src[1, 8 * t + x, q] = black
                    else:
                        cond[0, 8 * t + x + 1, q] = red * here
                        cond[1, 8 * t + x + 1, q] = black * here
    set_up(32, 24, cond, src, wd, fd, dd)
    descend(32, 24, v, wd, fd, dd, cond, nat_f, nat_b)
    black_ref[...] = v[1]
    lane8 = lanes(8)
    index = 2 * (lane8 % 32) + (lane8 // 32) % 2
    group = 32 * ((lane8 % 64) // 16) + lane8 % 16
    for x in range(0, 8, 2):
        for q in (0, 1):
            own = []
            for a in (0, 1):
                f = nat_f[4 + x + a, pl.ds(4 + q, 8, stride=2), :]
                b = nat_b[4 + x + a, pl.ds(4 + q, 8, stride=2), :]
                cells = jnp.where(lane8 < 64, pick(f, index), pick(b, index))
                own_ref[x + a, q] = cells
                own.append(cells)
            zl_ref[x // 2, q] = jnp.where(lane8 < 64, pick(own[0], group), pick(own[1], group))
            zr_ref[x // 2, q] = jnp.where(lane8 < 64, pick(own[0], group + 16), pick(own[1], group + 16))


def level1_down_kernel(
    scal, own_ref, yl_ref, yr_ref,
    out_ref, black_ref, wd, fd,
    cond, src, v, dd, nat_f, nat_b,
):
    gx, gy, gz = scal[0], scal[1], scal[2]
    lane = lanes(8)
    inside = (lane < 64) & ((gz > 0) | (lane >= 16)) & ((gz < 7) | (lane < 48))
    keep = jnp.where(inside, 1.0, 0.0)
    for block, ref in enumerate((yl_ref, own_ref, yr_ref)):
        here = keep
        if block == 0:
            here = keep * jnp.where(gy > 0, 1.0, 0.0)
        if block == 2:
            here = keep * jnp.where(gy < 7, 1.0, 0.0)
        rows = pl.ds(8 * block, 8)

        def body(s, carry):
            start = 8 * ((gx + 4 - s) % 4)
            for x in range(8):
                for q in (0, 1):
                    main = ref[16 * s + x, q]
                    from_left = ref[16 * s + 8 + x // 2, q]
                    from_right = ref[16 * s + 12 + x // 2, q]
                    parts = []
                    for g in range(4):
                        far = 64 * (x % 2) + 16 * g
                        parts.append(
                            jnp.where(
                                lane < 16, turn(from_left, -far),
                                jnp.where(lane < 48, turn(main, 16 - 32 * g), turn(from_right, 48 - far)),
                            )
                        )
                    red, black = (0, 1) if (x + q) % 2 == 0 else (1, 0)
                    src[0, start + x, q, rows] = parts[red]
                    src[1, start + x, q, rows] = parts[black]
                    cond[0, start + x + 1, q, rows] = parts[2 + red] * here
                    cond[1, start + x + 1, q, rows] = parts[2 + black] * here
            return carry

        lax.fori_loop(0, 4, body, 0)
    set_up(32, 24, cond, src, wd, fd, dd)
    descend(32, 24, v, wd, fd, dd, cond, nat_f, nat_b)
    black_ref[...] = v[1]
    index = 2 * (lane % 32) + (lane // 32) % 2
    for x in range(16):
        f = pick(nat_f[x, 8:16], index)
        b = pick(nat_b[x, 8:16], index)
        nat_f[x, 0:8] = jnp.where(lane < 64, f, b)
        for q in (0, 1):
            out_ref[x, 4 * q : 4 * q + 4] = nat_f[x, pl.ds(q, 4, stride=2), :]


def level2_down_kernel(
    scal, in_ref,
    out_ref, black_ref, wd, fd,
    cond, src, v, dd, nat_f, nat_b,
):
    gy, gz = scal[1], scal[2]
    chip = gy // 2
    lane = lanes(8)
    inside = (lane < 32) & ((gz > 0) | (lane >= 8)) & ((gz < 7) | (lane < 24))
    keep = jnp.where(inside, 1.0, 0.0)
    for s in range(4):
        rows = pl.ds(pl.multiple_of(8 * ((chip + 4 - s) % 4), 8), 8)

        def body(i, carry):
            for a in (0, 1):
                x = 2 * i + a
                for q in (0, 1):
                    main = jnp.concatenate(
                        [in_ref[0, s, x, 4 * q : 4 * q + 4], in_ref[1, s, x, 4 * q : 4 * q + 4]], axis=0
                    )
                    parts = [turn(main, -32 * g) for g in range(4)]
                    red, black = (0, 1) if (a + q) % 2 == 0 else (1, 0)
                    src[0, x, q, rows] = parts[red]
                    src[1, x, q, rows] = parts[black]
                    cond[0, x + 1, q, rows] = parts[2 + red] * keep
                    cond[1, x + 1, q, rows] = parts[2 + black] * keep
            return carry

        lax.fori_loop(0, 8, body, 0)
    set_up(16, 32, cond, src, wd, fd, dd)
    descend(16, 32, v, wd, fd, dd, cond, nat_f, nat_b)
    black_ref[...] = v[1]
    lane = lanes(16)
    index = 8 + 2 * (lane % 8) + (lane // 8) % 2
    for xg in (0, 1):
        for q in (0, 1):
            packed = jnp.zeros((16, 128), F32)
            for xi in range(4):
                f = pick(nat_f[4 * xg + xi, pl.ds(q, 16, stride=2), :], index)
                b = pick(nat_b[4 * xg + xi, pl.ds(q, 16, stride=2), :], index)
                packed = jnp.where(lane // 32 == xi, jnp.where(lane % 32 < 16, f, b), packed)
            for r in range(8):
                out_ref[r, xg, q] = packed


def coarse_kernel(
    scal, in_ref, out_ref,
    cond3, src3, v3, dd3, wd3, fd3, nat_f, nat_b,
    cond4, src4, v4, dd4, wd4, fd4, nat4, nat3,
):
    gz = scal[2]
    lane = lanes(16)
    for xg in (0, 1):
        for xi in range(4):
            x = 4 * xg + xi
            for q in (0, 1):
                parts = []
                for g in range(4):
                    cells = jnp.zeros((16, 128), F32)
                    for r in range(8):
                        cells = jnp.where(lane // 8 == r, turn(in_ref[r, xg, q], 8 * r - 32 * xi - 8 * g), cells)
                    parts.append(cells)
                red, black = (0, 1) if (x + q) % 2 == 0 else (1, 0)
                src3[0, x, q] = parts[red]
                src3[1, x, q] = parts[black]
                cond3[0, x + 1, q] = parts[2 + red]
                cond3[1, x + 1, q] = parts[2 + black]
    set_up(8, 16, cond3, src3, wd3, fd3, dd3)
    descend(8, 16, v3, wd3, fd3, dd3, cond3, nat_f, nat_b)
    lane8 = lanes(8)
    even = 2 * (lane8 % 32)
    on_grid = lane8 < 32
    for x in range(4):
        for q in (0, 1):
            f = nat_f[x, pl.ds(q, 8, stride=2), :]
            b = nat_b[x, pl.ds(q, 8, stride=2), :]
            for e in (0, 1):
                colour = (x + q + e) % 2
                src4[colour, x, q] = pick(f, even + e)
                cond4[colour, x + 1, q] = jnp.where(on_grid, pick(b, even + e), 0.0)
    set_up(4, 8, cond4, src4, wd4, fd4, dd4)
    clear_ends(4, 8, v4)
    first_half(4, v4, fd4)
    half_sweep(1, 4, v4, wd4, fd4)

    def step(_, carry):
        half_sweep(0, 4, v4, wd4, fd4)
        half_sweep(1, 4, v4, wd4, fd4)
        return carry

    lax.fori_loop(0, ITERS - 1, step, 0)
    index = (lane8 % 2) * 32 + (lane8 // 2) % 32
    for x in range(4):
        for q in (0, 1):
            nat4[x, pl.ds(q, 8, stride=2), :] = natural(v4, x, x % 2, q, 32, index)

    def add(x, a, q):
        v3[1, x + 1, q] = v3[1, x + 1, q] + nat4[x // 2]

    planes(8, add)
    ascend(8, v3, wd3, fd3)
    place = jnp.clip(16 * gz - 8 + lane, 0, 127)
    index = (place % 2) * 64 + place // 2
    for x in range(8):
        for q in (0, 1):
            nat3[x, pl.ds(q, 16, stride=2), :] = natural(v3, x, x % 2, q, 64, index)
    out_ref[...] = nat3[...]


def level2_up_kernel(scal, black_ref, wd, fd, add_ref, out_ref, v, nat):
    gy = scal[1]
    clear_ends(16, 32, v)

    def add(x, a, q):
        v[1, x + 1, q] = black_ref[x + 1, q] + add_ref[x // 2]

    planes(16, add)
    ascend(16, v, wd, fd)
    lane = lanes(32)
    index = (lane % 2) * 32 + (lane // 2) % 32

    def store(x, a, q):
        nat[x, pl.ds(8 + q, 32, stride=2), :] = natural(v, x, a, q, 32, index)

    planes(16, store)
    start = pl.multiple_of(8 * gy, 8)

    def hand_on(x, carry):
        out_ref[x] = nat[x, pl.ds(start, 24), :]
        return carry

    lax.fori_loop(0, 16, hand_on, 0)


def level1_up_kernel(scal, black_ref, wd, fd, add_ref, out_ref, v, nat):
    gx = scal[0]
    clear_ends(32, 24, v)

    def add(x, a, q):
        v[1, x + 1, q] = black_ref[x + 1, q] + add_ref[x // 2]

    planes(32, add)
    ascend(32, v, wd, fd)
    lane = lanes(24)
    place = jnp.where(lane < 96, lane, lane - 128) + 32
    index = (place % 2) * 64 + jnp.clip(place // 2, 0, 63)

    def store(x, a, q):
        nat[x + 4, pl.ds(q, 24, stride=2), :] = natural(v, x, a, q, 64, index)

    planes(32, store)

    def hand_on(x, carry):
        out_ref[x] = nat[8 * gx + x, 12:36]
        return carry

    lax.fori_loop(0, 16, hand_on, 0)


def level0_up_kernel(black_ref, wd, fd, add_ref, out_ref, v):
    clear_ends(32, 24, v)

    def add(x, a, q):
        v[1, x + 1, q] = black_ref[x + 1, q] + add_ref[x // 2]

    planes(32, add)
    ascend(32, v, wd, fd)
    lane = lanes(24)
    index = (lane % 2) * 64 + lane // 2

    def store(i, carry):
        for a in (0, 1):
            for q in (0, 1):
                x = 2 * i + a
                cells = natural(v, x + 8, a, q, 64, index)
                out_ref[x, pl.ds(q, 16, stride=2), :] = cells[4:20]
        return carry

    lax.fori_loop(0, 8, store, 0)


def arr(*shape):
    return jax.ShapeDtypeStruct(shape, F32)


def level_scratch(count, rows, nat_rows=None):
    return [
        pltpu.VMEM((2, count + 2, 2, rows, 128), F32),
        pltpu.VMEM((2, count, 2, rows, 128), F32),
        pltpu.VMEM((2, count + 2, 2, rows, 128), F32),
        pltpu.VMEM((count, 2, rows, 128), F32),
    ]


def nat_scratch(count, rows):
    return [pltpu.VMEM((count // 2, rows, 128), F32)] * 2


def weights_shape(count, rows):
    return [(2, 6, count, 2, rows, 128), (2, count, 2, rows, 128)]


def call(kernel, outs, scratch, *args, scal=None):
    specs = [VMEM] * len(args)
    if scal is not None:
        specs = [SMEM] + specs
        args = (scal,) + args
    return pl.pallas_call(
        kernel,
        out_shape=outs,
        in_specs=specs,
        out_specs=jax.tree.map(lambda _: VMEM, outs),
        scratch_shapes=scratch,
        compiler_params=pltpu.CompilerParams(vmem_limit_bytes=48 * 1024 * 1024),
    )(*args)


def ring(values, axis, step):
    count = lax.axis_size(axis)
    return lax.ppermute(values, axis, [(i, (i + step) % count) for i in range(count)])


def on_device(right_side, coefficient):
    scal = jnp.stack([lax.axis_index("gx"), lax.axis_index("gy"), lax.axis_index("gz")]).astype(jnp.int32)
    half = arr(16, 2, 16, 128)
    strip = arr(2, 2, 16, 128)
    lo, hi, zl, zr = call(split_kernel, [half, half, strip, strip], [], right_side, coefficient)
    from_left, from_right = ring(zr, "gz", 1), ring(zl, "gz", -1)
    lo = jnp.concatenate([lo, from_left[0:1], from_right[0:1]])
    hi = jnp.concatenate([hi, from_left[1:2], from_right[1:2]])
    before, after = ring(hi, "gx", 1), ring(lo, "gx", -1)
    bundles = (before, lo, hi, after)
    yl, yr = call(edge_kernel, [arr(72, 8, 128)] * 2, [], *bundles)
    from_left, from_right = ring(yr, "gy", 1), ring(yl, "gy", -1)
    own, zl, zr, black0, wd0, fd0 = call(
        level0_down_kernel,
        [arr(8, 2, 8, 128), arr(4, 2, 8, 128), arr(4, 2, 8, 128), arr(34, 2, 24, 128)]
        + [arr(*s) for s in weights_shape(32, 24)],
        level_scratch(32, 24) + nat_scratch(32, 24),
        *bundles, from_left, from_right, scal=scal,
    )
    from_left, from_right = ring(zr, "gz", 1), ring(zl, "gz", -1)
    bundle = jnp.concatenate([own, from_left, from_right])
    column = jnp.concatenate([bundle] + [ring(bundle, "gx", s) for s in (1, 2, 3)])
    from_left, from_right = ring(column, "gy", 1), ring(column, "gy", -1)
    own, black1, wd1, fd1 = call(
        level1_down_kernel,
        [arr(16, 8, 128), arr(34, 2, 24, 128)] + [arr(*s) for s in weights_shape(32, 24)],
        level_scratch(32, 24) + nat_scratch(32, 24),
        column, from_left, from_right, scal=scal,
    )
    own = own[None]
    sheet = jnp.concatenate([own] + [ring(own, "gy", 2 * s) for s in (1, 2, 3)])
    sheet = lax.all_gather(sheet, "gy", axis=0, axis_index_groups=[[0, 1], [2, 3], [4, 5], [6, 7]])
    own, black2, wd2, fd2 = call(
        level2_down_kernel,
        [arr(8, 2, 2, 16, 128), arr(18, 2, 32, 128)] + [arr(*s) for s in weights_shape(16, 32)],
        level_scratch(16, 32) + nat_scratch(16, 32),
        sheet, scal=scal,
    )
    whole = lax.all_to_all(own, "gz", 0, 0, tiled=True)
    correction = call(
        coarse_kernel,
        arr(8, 32, 128),
        level_scratch(8, 16) + [pltpu.VMEM(s, F32) for s in weights_shape(8, 16)] + nat_scratch(8, 16)
        + level_scratch(4, 8) + [pltpu.VMEM(s, F32) for s in weights_shape(4, 8)]
        + [pltpu.VMEM((4, 16, 128), F32), pltpu.VMEM((8, 32, 128), F32)],
        whole, scal=scal,
    )
    correction = call(
        level2_up_kernel, arr(16, 24, 128),
        [pltpu.VMEM((2, 18, 2, 32, 128), F32), pltpu.VMEM((16, 80, 128), F32)],
        black2, wd2, fd2, correction, scal=scal,
    )
    correction = call(
        level1_up_kernel, arr(16, 24, 128),
        [pltpu.VMEM((2, 34, 2, 24, 128), F32), pltpu.VMEM((40, 48, 128), F32)],
        black1, wd1, fd1, correction, scal=scal,
    )
    return call(
        level0_up_kernel, arr(16, 32, 128),
        [pltpu.VMEM((2, 34, 2, 24, 128), F32)],
        black0, wd0, fd0, correction,
    )


def solution(mesh):
    spec = P("gx", "gy", "gz")
    return jax.shard_map(on_device, mesh=mesh, in_specs=(spec, spec), out_specs=spec, check_vma=False)
```

```python
import functools

import jax
import jax.numpy as jnp
from jax import lax
from jax.experimental import pallas as pl
from jax.experimental.pallas import tpu as pltpu
from jax.sharding import PartitionSpec as P

SWEEPS = 2
ITERS = 20
F32 = jnp.float32
OFF = 1e30
VMEM = pl.BlockSpec(memory_space=pltpu.VMEM)
SMEM = pl.BlockSpec(memory_space=pltpu.SMEM)


class Level:
    def __init__(self, count, rows, group, fold):
        self.count, self.rows, self.group, self.fold = count, rows, group, fold

    def wide(self):
        return (self.count + 2, 2, self.rows, 128)

    def own(self):
        return (self.count, 2, self.rows, 128)


L0 = Level(32, 24, 128, None)
L1 = Level(16, 24, 64, "x")
L2 = Level(16, 8, 32, "y")
L3 = Level(8, 8, 64, "y")
L4 = Level(4, 8, 128, None)


def lanes(rows):
    return lax.broadcasted_iota(jnp.int32, (rows, 128), 1)


def rows_of(rows):
    return lax.broadcasted_iota(jnp.int32, (rows, 128), 0)


def pick(values, index):
    return jnp.take_along_axis(values, index, axis=1, mode="promise_in_bounds")


def turn(values, shift):
    shift = shift % 128
    return pltpu.roll(values, shift, 1) if shift else values


def inverse_of(values):
    guess = pl.reciprocal(values, approx=True)
    guess = guess * (2.0 - values * guess)
    return guess * (2.0 - values * guess)


def up(level, values):
    rolled = pltpu.roll(values, level.rows - 1, 0)
    if level.fold == "y":
        rolled = jnp.where(rows_of(level.rows) == level.rows - 1, turn(rolled, -level.group), rolled)
    return rolled


def down(level, values):
    rolled = pltpu.roll(values, 1, 0)
    if level.fold == "y":
        rolled = jnp.where(rows_of(level.rows) == 0, turn(rolled, level.group), rolled)
    return rolled


def goes_back(colour, a, q):
    return (colour == 0) == ((a + q) % 2 == 0)


def beside(level, other, x, q, colour, a):
    mid = other[x + 1, q]
    across = other[x + 1, 1 - q]
    return [
        other[x + 2, q],
        other[x, q],
        across if q == 0 else up(level, across),
        down(level, across) if q == 0 else across,
        mid,
        turn(mid, 1 if goes_back(colour, a, q) else -1),
    ]


def planes(first, last, unroll, body):
    pairs = (last - first) // 2
    unroll = min(unroll, pairs)
    while pairs % unroll:
        unroll -= 1

    def step(i, carry):
        for u in range(unroll):
            for a in (0, 1):
                for q in (0, 1):
                    body(first + 2 * (unroll * i + u) + a, a, q)
        return carry

    if pairs == unroll:
        step(0, 0)
    else:
        lax.fori_loop(0, pairs // unroll, step, 0)


def fill_ends(level, values, rest=0.0):
    lane = lanes(level.rows)
    for q in (0, 1):
        if level.fold == "x":
            values[0, q] = jnp.where(lane < 64, rest, turn(values[level.count, q], 64))
            values[level.count + 1, q] = jnp.where(lane < 64, turn(values[1, q], 64), rest)
        else:
            values[0, q] = jnp.full((level.rows, 128), rest, F32)
            values[level.count + 1, q] = jnp.full((level.rows, 128), rest, F32)


def set_up(level, cond, rec, wd, fd, dd):
    rows = level.rows
    row, lane = rows_of(rows), lanes(rows)
    for colour in (0, 1):
        fill_ends(level, rec[colour], OFF)

    def body(x, a, q):
        for colour in (0, 1):
            own = cond[colour][x, q]
            own_rec = rec[colour][x + 1, q]
            near = beside(level, rec[1 - colour], x, q, colour, a)
            if level.fold == "y":
                if q == 0:
                    near[3] = jnp.where((row == 0) & (lane < level.group), OFF, near[3])
                else:
                    near[2] = jnp.where((row == rows - 1) & (lane >= 128 - level.group), OFF, near[2])
            elif level is L4:
                if q == 0:
                    near[3] = jnp.where(row == 0, OFF, near[3])
                else:
                    near[2] = jnp.where(row == rows - 1, OFF, near[2])
            if level.group < 128:
                end = 0 if goes_back(colour, a, q) else level.group - 1
                near[5] = jnp.where(lane % level.group == end, OFF, near[5])
            total = None
            faces = []
            for value in near:
                off = value > 0.5 * OFF
                face = inverse_of(own_rec + value)
                faces.append(jnp.where(off, 0.0, face))
                part = jnp.where(off, own, face)
                total = part if total is None else total + part
            total = jnp.where(own_rec > 0.5 * OFF, 1.0, total)
            inverse = inverse_of(total)
            for i, face in enumerate(faces):
                wd[colour][i, x, q] = face * inverse
            fd[colour][x, q] = fd[colour][x, q] * (0.5 * inverse)
            if colour == 0:
                dd[x, q] = total

    planes(0, level.count, 1, body)


def relaxed(level, colour, x, a, q, v, wd, fd):
    near = beside(level, v[1 - colour], x, q, colour, a)
    weight = wd[colour]
    one = fd[colour][x, q] + weight[0, x, q] * near[0]
    two = weight[4, x, q] * near[4] + weight[1, x, q] * near[1]
    one = one + weight[2, x, q] * near[2]
    two = two + weight[3, x, q] * near[3]
    return one + (two + weight[5, x, q] * near[5])


def half_sweep(level, colour, v, wd, fd, first=0, last=None):
    def body(x, a, q):
        v[colour][x + 1, q] = relaxed(level, colour, x, a, q, v, wd, fd)

    planes(first, level.count if last is None else last, 8 if level.rows == 8 else 4, body)
    if level.fold == "x":
        fill_ends(level, v[colour])


def first_half(level, v, fd):
    for colour in (0, 1):
        fill_ends(level, v[colour])

    def body(x, a, q):
        v[0][x + 1, q] = fd[0][x, q]

    planes(0, level.count, 4, body)
    if level.fold == "x":
        fill_ends(level, v[0])


def descend(level, v, wd, fd, dd, cond, out_f, out_b, ranges=None):
    ranges = ranges or [(0, level.count)] * 4
    first_half(level, v, fd)
    half_sweep(level, 1, v, wd, fd, *ranges[0])
    half_sweep(level, 0, v, wd, fd, *ranges[1])
    half_sweep(level, 1, v, wd, fd, *ranges[2])
    first, last = ranges[3]

    def body(i, carry):
        for u in (0, 1):
            left = jnp.zeros((level.rows, 128), F32)
            mean = jnp.zeros((level.rows, 128), F32)
            for a in (0, 1):
                for q in (0, 1):
                    x = first + 4 * i + 2 * u + a
                    left = left + dd[x, q] * (relaxed(level, 0, x, a, q, v, wd, fd) - v[0][x + 1, q])
                    mean = mean + (cond[0][x, q] + cond[1][x, q])
            out_f[2 * i + u] = left
            out_b[2 * i + u] = 0.125 * mean
        return carry

    lax.fori_loop(0, (last - first) // 4, body, 0)


def ascend(level, v, wd, fd, ranges=None):
    ranges = ranges or [(0, level.count)] * 4
    for step in range(2 * SWEEPS):
        half_sweep(level, step % 2, v, wd, fd, *ranges[step])


def correct(level, v, black, add):
    for colour in (0, 1):
        fill_ends(level, v[colour])

    def body(x, a, q):
        v[1][x + 1, q] = black[x, q] + add[x // 2]

    planes(0, level.count, 4, body)
    if level.fold == "x":
        fill_ends(level, v[1])


def keep_black(level, v, black):
    def body(x, a, q):
        black[x, q] = v[1][x + 1, q]

    planes(0, level.count, 4, body)


def even_odd(v, x, a, q):
    red, black = v[0][x + 1, q], v[1][x + 1, q]
    return (red, black) if (a + q) % 2 == 0 else (black, red)


def split_kernel(f_ref, b_ref, lo_ref, hi_ref, zl_ref, zr_ref):
    lane = lanes(16)
    whole = 2 * (lane % 64) + lane // 64
    slot = lane // 8
    within = lane % 8
    first = 2 * (within % 4) + within // 4
    last = 120 + first
    for half, out in enumerate((lo_ref, hi_ref)):
        for q in (0, 1):
            left = jnp.zeros((16, 128), F32)
            right = jnp.zeros((16, 128), F32)
            for x in range(8):
                for arr, ref in enumerate((f_ref, b_ref)):
                    cells = ref[8 * half + x, pl.ds(q, 16, stride=2), :]
                    out[8 * arr + x, q] = pick(cells, whole)
                    here = slot == 2 * x + arr
                    left = jnp.where(here, pick(cells, first), left)
                    right = jnp.where(here, pick(cells, last), right)
            zl_ref[half, q] = left
            zr_ref[half, q] = turn(right, 60)


def edge_kernel(a_ref, b_ref, c_ref, d_ref, lo_ref, hi_ref):
    for t, ref in enumerate((a_ref, b_ref, c_ref, d_ref)):
        for i in range(18):
            for q in (0, 1):
                cells = ref[i, q]
                lo_ref[18 * t + i, 4 * q : 4 * q + 4] = cells[0:4]
                hi_ref[18 * t + i, 4 - 4 * q : 8 - 4 * q] = cells[12:16]


def level0_down_kernel(
    scal, a_ref, b_ref, c_ref, d_ref, yl_ref, yr_ref,
    own_ref, zl_ref, zr_ref, black_ref, wd0, wd1, fd0, fd1,
    cond0, cond1, rec0, rec1, v0, v1, dd, nat_f, nat_b,
):
    cond, rec, v, wd, fd = (cond0, cond1), (rec0, rec1), (v0, v1), (wd0, wd1), (fd0, fd1)
    gx, gy, gz = scal[0], scal[1], scal[2]
    lane, row = lanes(24), rows_of(24)
    inside = (lane < 68) | (lane >= 124)
    inside = inside & ((gz > 0) | (lane < 124)) & ((gz < 7) | (lane < 64) | (lane >= 124))
    inside = inside & ((gy > 0) | (row < 20)) & ((gy < 7) | (row < 16) | (row >= 20))
    keep = jnp.where(inside, 1.0, 0.0)
    low = rows_of(8) < 4
    for t, ref in enumerate((a_ref, b_ref, c_ref, d_ref)):
        here = keep
        if t == 0:
            here = keep * jnp.where(gx > 0, 1.0, 0.0)
        if t == 3:
            here = keep * jnp.where(gx < 3, 1.0, 0.0)

        def wide(i, q):
            right, left = yr_ref[18 * t + i], yl_ref[18 * t + i]
            edge = jnp.where(low, right, left) if q == 0 else pltpu.roll(jnp.where(low, left, right), 4, 0)
            return jnp.concatenate([ref[i, q], edge], axis=0)

        ends = [(wide(16, q), wide(17, q)) for q in (0, 1)]
        for x in range(8):
            for q in (0, 1):
                from_left, from_right = ends[q]
                for arr in (0, 1):
                    s = 2 * x + arr
                    main = wide(8 * arr + x, q)
                    edge = jnp.where(lane // 8 == s, from_right, from_left)
                    even = jnp.where(lane < 64, main, turn(edge, 64 - 8 * s))
                    odd = jnp.where(lane < 64, turn(main, 64), turn(edge, 60 - 8 * s))
                    cells = (even, odd) if (x + q) % 2 == 0 else (odd, even)
                    for colour in (0, 1):
                        if arr == 0:
                            fd[colour][8 * t + x, q] = cells[colour]
                        else:
                            on_grid = cells[colour] * here
                            cond[colour][8 * t + x, q] = on_grid
                            rec[colour][8 * t + x + 1, q] = jnp.where(
                                here > 0.0, inverse_of(cells[colour]), OFF
                            )
    set_up(L0, cond, rec, wd, fd, dd)
    descend(L0, v, wd, fd, dd, cond, nat_f, nat_b, [(2, 30), (2, 30), (4, 28), (8, 24)])
    keep_black(L0, v, black_ref)
    lane8 = lanes(8)
    index = 2 * (lane8 % 32) + (lane8 // 32) % 2
    group = 32 * ((lane8 % 64) // 16) + lane8 % 16
    for x in range(0, 8, 2):
        for q in (0, 1):
            own = []
            for a in (0, 1):
                f = nat_f[x + a, pl.ds(q, 8, stride=2), :]
                b = nat_b[x + a, pl.ds(q, 8, stride=2), :]
                cells = jnp.where(lane8 < 64, pick(f, index), pick(b, index))
                own_ref[x + a, q] = cells
                own.append(cells)
            left = jnp.where(lane8 < 64, pick(own[0], group), pick(own[1], group))
            zl_ref[x // 2, q] = turn(left, 48)
            zr_ref[x // 2, q] = jnp.where(lane8 < 64, pick(own[0], group + 16), pick(own[1], group + 16))


def level1_down_kernel(
    scal, own_ref, yl_ref, yr_ref,
    out_ref, black_ref, wd0, wd1, fd0, fd1,
    cond0, cond1, rec0, rec1, v0, v1, dd, nat_f, nat_b,
):
    cond, rec, v, wd, fd = (cond0, cond1), (rec0, rec1), (v0, v1), (wd0, wd1), (fd0, fd1)
    gx, gy, gz = scal[0], scal[1], scal[2]
    lane = lanes(8)
    k = lane % 64
    inside = ((gz > 0) | (k >= 16)) & ((gz < 7) | (k < 48))
    keep = jnp.where(inside, 1.0, 0.0)
    for block, ref in enumerate((yl_ref, own_ref, yr_ref)):
        here = keep
        if block == 0:
            here = keep * jnp.where(gy > 0, 1.0, 0.0)
        if block == 2:
            here = keep * jnp.where(gy < 7, 1.0, 0.0)
        rows = pl.ds(8 * block, 8)

        def body(j, carry):
            slots = [16 * ((gx + 4 - j) % 4), 16 * ((gx + 6 - j) % 4)]
            for x in range(8):
                for q in (0, 1):
                    parts = []
                    for g in range(4):
                        far = 64 * (x % 2) + 16 * g
                        made = []
                        for h, slot in enumerate(slots):
                            main = ref[slot + x, q]
                            from_left = ref[slot + 8 + x // 2, q]
                            from_right = ref[slot + 12 + x // 2, q]
                            edge = jnp.where(lane // 16 == far // 16, from_left, from_right)
                            made.append((turn(main, 64 * h + 16 - 32 * g), turn(edge, 64 * h - far)))
                        main = jnp.where(lane < 64, made[0][0], made[1][0])
                        edge = jnp.where(lane < 64, made[0][1], made[1][1])
                        parts.append(jnp.where((k >= 16) & (k < 48), main, edge))
                    for colour in (0, 1):
                        odd = (x + q + colour) % 2
                        fd[colour][8 * j + x, q, rows] = parts[odd]
                        cond[colour][8 * j + x, q, rows] = parts[2 + odd] * here
                        rec[colour][8 * j + x + 1, q, rows] = jnp.where(
                            here > 0.0, inverse_of(parts[2 + odd]), OFF
                        )
            return carry

        lax.fori_loop(0, 2, body, 0)
    set_up(L1, cond, rec, wd, fd, dd)
    descend(L1, v, wd, fd, dd, cond, nat_f, nat_b)
    keep_black(L1, v, black_ref)
    for h in (0, 1):
        index = 64 * h + 2 * (lane % 32) + (lane // 32) % 2
        for x in range(8):
            f = pick(nat_f[x, 8:16], index)
            b = pick(nat_b[x, 8:16], index)
            nat_f[x, 0:8] = jnp.where(lane < 64, f, b)
            for q in (0, 1):
                out_ref[8 * h + x, 4 * q : 4 * q + 4] = nat_f[x, pl.ds(q, 4, stride=2), :]


def level2_down_kernel(
    scal, in_ref,
    out_ref, black_ref, wd0, wd1, fd0, fd1,
    cond0, cond1, rec0, rec1, v0, v1, dd, nat_f, nat_b,
):
    cond, rec, v, wd, fd = (cond0, cond1), (rec0, rec1), (v0, v1), (wd0, wd1), (fd0, fd1)
    gy, gz = scal[1], scal[2]
    chip = gy // 2
    lane = lanes(8)
    k = lane % 32
    inside = ((gz > 0) | (k >= 8)) & ((gz < 7) | (k < 24))
    slots = [(chip + 4 - j) % 4 for j in range(4)]

    def body(x, a, q):
        mains = []
        for slot in slots:
            both = [in_ref[c, slot, x, 4 * q : 4 * q + 4] for c in (0, 1)]
            mains.append(jnp.concatenate(both, axis=0))
        parts = []
        for g in range(4):
            part = turn(mains[0], -32 * g)
            for j in (1, 2, 3):
                part = jnp.where(lane // 32 == j, turn(mains[j], 32 * (j - g)), part)
            parts.append(part)
        for colour in (0, 1):
            odd = (a + q + colour) % 2
            fd[colour][x, q] = parts[odd]
            cond[colour][x, q] = jnp.where(inside, parts[2 + odd], 0.0)
            rec[colour][x + 1, q] = jnp.where(inside, inverse_of(parts[2 + odd]), OFF)

    planes(0, 16, 2, body)
    set_up(L2, cond, rec, wd, fd, dd)
    descend(L2, v, wd, fd, dd, cond, nat_f, nat_b)
    keep_black(L2, v, black_ref)
    index = 32 * (lane // 32) + 8 + 2 * (lane % 8) + (lane // 8) % 2
    for x in range(8):
        packed = jnp.where(lane % 32 < 16, pick(nat_f[x], index), pick(nat_b[x], index))
        for r in range(8):
            out_ref[r, x] = packed


def unfold(ref, x, q, group):
    cells = ref[x, pl.ds(q, 8, stride=2), :]
    for j in range(1, 128 // group):
        more = ref[x, pl.ds(16 * j + q, 8, stride=2), :]
        cells = jnp.where(lanes(8) // group == j, turn(more, group * j), cells)
    return cells


def coarse_kernel(
    scal, in_ref, out_ref,
    cond30, cond31, rec30, rec31, v30, v31, dd3, wd30, wd31, fd30, fd31, nat_f, nat_b,
    cond40, cond41, rec40, rec41, v40, v41, dd4, wd40, wd41, fd40, fd41, whole, nat4, nat3,
):
    cond3, rec3, v3, wd3, fd3 = (cond30, cond31), (rec30, rec31), (v30, v31), (wd30, wd31), (fd30, fd31)
    cond4, rec4, v4, wd4, fd4 = (cond40, cond41), (rec40, rec41), (v40, v41), (wd40, wd41), (fd40, fd41)
    gz = scal[2]
    lane = lanes(8)

    def collect(x, carry):
        for g in range(4):
            for mq in range(4):
                cells = turn(in_ref[0, x], -32 * mq - 8 * g)
                for r in range(1, 8):
                    cells = jnp.where(lane // 8 == r, turn(in_ref[r, x], 8 * r - 32 * mq - 8 * g), cells)
                whole[g, x, 8 * mq : 8 * mq + 8] = cells
        return carry

    lax.fori_loop(0, 8, collect, 0)

    def place3(x, a, q):
        for colour in (0, 1):
            odd = (a + q + colour) % 2
            fd3[colour][x, q] = unfold(whole.at[odd], x, q, 64)
            cells = unfold(whole.at[2 + odd], x, q, 64)
            cond3[colour][x, q] = cells
            rec3[colour][x + 1, q] = inverse_of(cells)

    planes(0, 8, 2, place3)
    set_up(L3, cond3, rec3, wd3, fd3, dd3)
    descend(L3, v3, wd3, fd3, dd3, cond3, nat_f, nat_b)
    on_grid = lane < 32
    for x in range(4):
        f_plane, b_plane = nat_f[x], nat_b[x]
        for half in (0, 1):
            nat4[x, 8 * half : 8 * half + 8] = turn(f_plane, 64 * half)
            whole[0, x, 8 * half : 8 * half + 8] = turn(b_plane, 64 * half)
        for q in (0, 1):
            f = nat4[x, pl.ds(q, 8, stride=2), :]
            b = whole[0, x, pl.ds(q, 8, stride=2), :]
            for e in (0, 1):
                colour = (x + q + e) % 2
                index = 2 * (lane % 32) + e
                fd4[colour][x, q] = pick(f, index)
                cells = pick(b, index)
                cond4[colour][x, q] = jnp.where(on_grid, cells, 0.0)
                rec4[colour][x + 1, q] = jnp.where(on_grid, inverse_of(cells), OFF)
    set_up(L4, cond4, rec4, wd4, fd4, dd4)

    def half(colour, other):
        made = {}
        for x in range(4):
            for q in (0, 1):
                mid, across = other[x, q], other[x, 1 - q]
                weight = lambda i: wd4[colour][i, x, q]
                total = fd4[colour][x, q] + weight(4) * mid
                total = total + weight(2) * (across if q == 0 else up(L4, across))
                total = total + weight(3) * (down(L4, across) if q == 0 else across)
                rest = weight(5) * turn(mid, 1 if goes_back(colour, x, q) else -1)
                if x < 3:
                    rest = rest + weight(0) * other[x + 1, q]
                if x > 0:
                    rest = rest + weight(1) * other[x - 1, q]
                made[x, q] = total + rest
        return made

    keys = [(x, q) for x in range(4) for q in (0, 1)]
    black = half(1, {key: fd4[0][key] for key in keys})

    def step(_, carry):
        after = half(1, half(0, dict(zip(keys, carry))))
        return tuple(after[key] for key in keys)

    final = lax.fori_loop(0, ITERS - 2, step, tuple(black[key] for key in keys))
    red = half(0, dict(zip(keys, final)))
    black = half(1, red)
    index = (lane % 2) * 32 + (lane // 2) % 32
    for x, q in keys:
        even, odd = (red[x, q], black[x, q]) if (x + q) % 2 == 0 else (black[x, q], red[x, q])
        nat4[x, pl.ds(q, 8, stride=2), :] = pick(jnp.where(lane < 32, even, turn(odd, 32)), index)
    for x in range(4):
        nat_f[x] = jnp.where(lane < 64, nat4[x, 0:8], turn(nat4[x, 8:16], 64))

    def add(x, a, q):
        v3[1][x + 1, q] = v3[1][x + 1, q] + nat_f[x // 2]

    planes(0, 8, 4, add)
    ascend(L3, v3, wd3, fd3)
    z = jnp.clip(16 * gz - 8 + lane % 32, 0, 127)
    index = (z % 2) * 64 + z // 2
    for x in range(8):
        for q in (0, 1):
            even, odd = even_odd(v3, x, x, q)
            first = pick(jnp.where(lane < 64, even, turn(odd, 64)), index)
            second = pick(jnp.where(lane < 64, turn(even, 64), odd), index)
            nat3[x, pl.ds(q, 8, stride=2), :] = first
            nat3[x, pl.ds(16 + q, 8, stride=2), :] = second
        cells = nat3[x, 0:8]
        for j in (1, 2, 3):
            cells = jnp.where(lane // 32 == j, nat3[x, 8 * j : 8 * j + 8], cells)
        out_ref[x] = cells


def level2_up_kernel(scal, black_ref, wd0, wd1, fd0, fd1, add_ref, out_ref, v0, v1, nat):
    v, wd, fd = (v0, v1), (wd0, wd1), (fd0, fd1)
    gy = scal[1]
    correct(L2, v, black_ref, add_ref)
    ascend(L2, v, wd, fd)
    lane = lanes(8)
    k = lane % 64
    start = pl.multiple_of(8 * gy, 8)
    for x in range(16):
        nat[x, 0:8] = jnp.zeros((8, 128), F32)
        nat[x, 72:80] = jnp.zeros((8, 128), F32)

    def store(x, a, q):
        even, odd = even_odd(v, x, a, q)
        for mq in range(4):
            packed = jnp.where(lane < 32, turn(even, -32 * mq), turn(odd, 32 - 32 * mq))
            nat[x, pl.ds(8 + 16 * mq + q, 8, stride=2), :] = pick(packed, (k % 2) * 32 + k // 2)

    planes(0, 16, 2, store)
    side = lanes(24) < 64
    for x in range(8):
        out_ref[x] = jnp.where(side, nat[x, pl.ds(start, 24), :], nat[8 + x, pl.ds(start, 24), :])


def level1_up_kernel(scal, black_ref, wd0, wd1, fd0, fd1, add_ref, out_ref, v0, v1, nat):
    v, wd, fd = (v0, v1), (wd0, wd1), (fd0, fd1)
    gx = scal[0]
    correct(L1, v, black_ref, add_ref)
    ascend(L1, v, wd, fd)
    lane = lanes(24)
    z = jnp.where(lane < 96, lane, lane - 128) + 32
    index = (z % 2) * 64 + jnp.clip(z // 2, 0, 63)
    for x in range(4):
        nat[x] = jnp.zeros((48, 128), F32)
        nat[36 + x] = jnp.zeros((48, 128), F32)

    def store(x, a, q):
        even, odd = even_odd(v, x, a, q)
        first = jnp.where(lane < 64, even, turn(odd, 64))
        second = jnp.where(lane < 64, turn(even, 64), odd)
        nat[x + 4, pl.ds(q, 24, stride=2), :] = pick(first, index)
        nat[x + 20, pl.ds(q, 24, stride=2), :] = pick(second, index)

    planes(0, 16, 2, store)

    def hand_on(x, carry):
        out_ref[x, 0:16] = nat[8 * gx + x, 16:32]
        out_ref[x, 16:20] = nat[8 * gx + x, 32:36]
        out_ref[x, 20:24] = nat[8 * gx + x, 12:16]
        return carry

    lax.fori_loop(0, 16, hand_on, 0)


def level0_up_kernel(black_ref, wd0, wd1, fd0, fd1, add_ref, out_ref, v0, v1):
    v, wd, fd = (v0, v1), (wd0, wd1), (fd0, fd1)
    correct(L0, v, black_ref, add_ref)
    ascend(L0, v, wd, fd, [(4, 28), (6, 26), (6, 26), (8, 24)])
    lane = lanes(16)
    index = (lane % 2) * 64 + lane // 2

    def store(x, a, q):
        even, odd = even_odd(v, x, a, q)
        packed = jnp.where(lane < 64, even[0:16], turn(odd[0:16], 64))
        out_ref[x - 8, pl.ds(q, 16, stride=2), :] = pick(packed, index)

    planes(8, 24, 4, store)


def arr(*shape):
    return jax.ShapeDtypeStruct(shape, F32)


def scratch(*shape):
    return pltpu.VMEM(shape, F32)


def level_scratch(level):
    shapes = [level.own()] * 2 + [level.wide()] * 4 + [level.own()]
    return [scratch(*s) for s in shapes]


def nat_scratch(level, count=None):
    return [scratch(count or level.count // 2, level.rows, 128)] * 2


def weights(level):
    return [(6,) + level.own()] * 2 + [level.own()] * 2


def call(kernel, outs, temps, *args, scal=None, limit=28):
    specs = [VMEM] * len(args)
    if scal is not None:
        specs = [SMEM] + specs
        args = (scal,) + args
    return pl.pallas_call(
        kernel,
        out_shape=outs,
        in_specs=specs,
        out_specs=jax.tree.map(lambda _: VMEM, outs),
        scratch_shapes=temps,
        compiler_params=pltpu.CompilerParams(vmem_limit_bytes=limit * 1024 * 1024),
    )(*args)


def ring(values, axis, step):
    count = lax.axis_size(axis)
    return lax.ppermute(values, axis, [(i, (i + step) % count) for i in range(count)])


def on_device(right_side, coefficient):
    scal = jnp.stack([lax.axis_index("gx"), lax.axis_index("gy"), lax.axis_index("gz")]).astype(jnp.int32)
    half = arr(16, 2, 16, 128)
    strip = arr(2, 2, 16, 128)
    lo, hi, zl, zr = call(split_kernel, [half, half, strip, strip], [], right_side, coefficient)
    from_left, from_right = ring(zr, "gz", 1), ring(zl, "gz", -1)
    lo = jnp.concatenate([lo, from_left[0:1], from_right[0:1]])
    hi = jnp.concatenate([hi, from_left[1:2], from_right[1:2]])
    before, after = ring(hi, "gx", 1), ring(lo, "gx", -1)
    bundles = (before, lo, hi, after)
    yl, yr = call(edge_kernel, [arr(72, 8, 128)] * 2, [], *bundles)
    from_left, from_right = ring(yr, "gy", 1), ring(yl, "gy", -1)
    own, zl, zr, black0, *set0 = call(
        level0_down_kernel,
        [arr(8, 2, 8, 128), arr(4, 2, 8, 128), arr(4, 2, 8, 128), arr(*L0.own())]
        + [arr(*s) for s in weights(L0)],
        level_scratch(L0) + nat_scratch(L0, 8),
        *bundles, from_left, from_right, scal=scal,
    )
    from_left, from_right = ring(zr, "gz", 1), ring(zl, "gz", -1)
    bundle = jnp.concatenate([own, from_left, from_right])
    column = jnp.concatenate([bundle] + [ring(bundle, "gx", s) for s in (1, 2, 3)])
    from_left, from_right = ring(column, "gy", 1), ring(column, "gy", -1)
    own, black1, *set1 = call(
        level1_down_kernel,
        [arr(16, 8, 128), arr(*L1.own())] + [arr(*s) for s in weights(L1)],
        level_scratch(L1) + nat_scratch(L1),
        column, from_left, from_right, scal=scal,
    )
    own = own[None]
    sheet = jnp.concatenate([own] + [ring(own, "gy", 2 * s) for s in (1, 2, 3)])
    sheet = lax.all_gather(sheet, "gy", axis=0, axis_index_groups=[[0, 1], [2, 3], [4, 5], [6, 7]])
    own, black2, *set2 = call(
        level2_down_kernel,
        [arr(8, 8, 8, 128), arr(*L2.own())] + [arr(*s) for s in weights(L2)],
        level_scratch(L2) + nat_scratch(L2),
        sheet, scal=scal,
    )
    whole = lax.all_to_all(own, "gz", 0, 0, tiled=True)
    correction = call(
        coarse_kernel,
        arr(8, 8, 128),
        level_scratch(L3) + [scratch(*s) for s in weights(L3)] + nat_scratch(L3)
        + level_scratch(L4) + [scratch(*s) for s in weights(L4)]
        + [scratch(4, 8, 32, 128), scratch(4, 16, 128), scratch(8, 32, 128)],
        whole, scal=scal,
    )
    correction = call(
        level2_up_kernel, arr(8, 24, 128),
        [scratch(*L2.wide())] * 2 + [scratch(16, 80, 128)],
        black2, *set2, correction, scal=scal,
    )
    correction = call(
        level1_up_kernel, arr(16, 24, 128),
        [scratch(*L1.wide())] * 2 + [scratch(40, 48, 128)],
        black1, *set1, correction, scal=scal,
    )
    return call(
        level0_up_kernel, arr(16, 32, 128),
        [scratch(*L0.wide())] * 2,
        black0, *set0, correction,
    )


def solution(mesh):
    spec = P("gx", "gy", "gz")
    return jax.shard_map(on_device, mesh=mesh, in_specs=(spec, spec), out_specs=spec, check_vma=False)
```

```python
import functools

import jax
import jax.numpy as jnp
from jax import lax
from jax.experimental import pallas as pl
from jax.experimental.pallas import tpu as pltpu
from jax.sharding import PartitionSpec as P

SWEEPS = 2
ITERS = 20
F32 = jnp.float32
OFF = 1e-20
VMEM = pl.BlockSpec(memory_space=pltpu.VMEM)
SMEM = pl.BlockSpec(memory_space=pltpu.SMEM)


class Level:
    def __init__(self, count, rows, group, fold):
        self.count, self.rows, self.group, self.fold = count, rows, group, fold

    def wide(self):
        return (self.count + 2, 2, self.rows, 128)

    def own(self):
        return (self.count, 2, self.rows, 128)


L0 = Level(32, 24, 128, None)
L1 = Level(16, 24, 64, "x")
L2 = Level(16, 8, 32, "y")
L3 = Level(8, 8, 64, "y")
L4 = Level(4, 8, 128, None)


def lanes(rows):
    return lax.broadcasted_iota(jnp.int32, (rows, 128), 1)


def rows_of(rows):
    return lax.broadcasted_iota(jnp.int32, (rows, 128), 0)


def pick(values, index):
    return jnp.take_along_axis(values, index, axis=1, mode="promise_in_bounds")


def turn(values, shift):
    shift = shift % 128
    return pltpu.roll(values, shift, 1) if shift else values


def inverse_of(values):
    return pl.reciprocal(values, approx=True)


def up(level, values):
    rolled = pltpu.roll(values, level.rows - 1, 0)
    if level.fold == "y":
        rolled = jnp.where(rows_of(level.rows) == level.rows - 1, turn(rolled, -level.group), rolled)
    return rolled


def down(level, values):
    rolled = pltpu.roll(values, 1, 0)
    if level.fold == "y":
        rolled = jnp.where(rows_of(level.rows) == 0, turn(rolled, level.group), rolled)
    return rolled


def goes_back(colour, a, q):
    return (colour == 0) == ((a + q) % 2 == 0)


def beside(level, other, x, q, colour, a):
    mid = other[x + 1, q]
    across = other[x + 1, 1 - q]
    return [
        other[x + 2, q],
        other[x, q],
        across if q == 0 else up(level, across),
        down(level, across) if q == 0 else across,
        mid,
        turn(mid, 1 if goes_back(colour, a, q) else -1),
    ]


def planes(first, last, unroll, body):
    pairs = (last - first) // 2
    unroll = min(unroll, pairs)
    while pairs % unroll:
        unroll -= 1

    def step(i, carry):
        for u in range(unroll):
            for a in (0, 1):
                for q in (0, 1):
                    body(first + 2 * (unroll * i + u) + a, a, q)
        return carry

    if pairs == unroll:
        step(0, 0)
    else:
        lax.fori_loop(0, pairs // unroll, step, 0)


def fill_ends(level, values, rest=0.0):
    lane = lanes(level.rows)
    for q in (0, 1):
        if level.fold == "x":
            values[0, q] = jnp.where(lane < 64, rest, turn(values[level.count, q], 64))
            values[level.count + 1, q] = jnp.where(lane < 64, turn(values[1, q], 64), rest)
        else:
            values[0, q] = jnp.full((level.rows, 128), rest, F32)
            values[level.count + 1, q] = jnp.full((level.rows, 128), rest, F32)


def set_up(level, cond, rec, wd, fd, dd):
    rows = level.rows
    row, lane = rows_of(rows), lanes(rows)
    for colour in (0, 1):
        fill_ends(level, rec[colour], OFF)

    def body(x, a, q):
        for colour in (0, 1):
            own_rec = rec[colour][x + 1, q]
            near = beside(level, rec[1 - colour], x, q, colour, a)
            walls = {}
            if level.fold == "y" or level is L4:
                width = level.group if level.fold == "y" else 128
                if q == 0:
                    walls[3] = (row == 0) & (lane < width)
                else:
                    walls[2] = (row == rows - 1) & (lane >= 128 - width)
            if level.group < 128:
                end = 0 if goes_back(colour, a, q) else level.group - 1
                walls[5] = lane % level.group == end
            total = None
            faces = []
            for i, value in enumerate(near):
                if i in walls:
                    value = jnp.where(walls[i], OFF, value)
                face = inverse_of(own_rec + value)
                faces.append(face)
                total = face if total is None else total + face
            inverse = jnp.where(own_rec > 1e-10, inverse_of(total), 0.0)
            for i, face in enumerate(faces):
                weight = face * inverse
                wd[colour][i, x, q] = jnp.where(walls[i], 0.0, weight) if i in walls else weight
            fd[colour][x, q] = fd[colour][x, q] * (0.5 * inverse)
            if colour == 0:
                dd[x, q] = total

    planes(0, level.count, 4 if level.rows == 8 else 1, body)


def relaxed(level, colour, x, a, q, v, wd, fd):
    near = beside(level, v[1 - colour], x, q, colour, a)
    weight = wd[colour]
    one = fd[colour][x, q] + weight[0, x, q] * near[0]
    two = weight[4, x, q] * near[4] + weight[1, x, q] * near[1]
    one = one + weight[2, x, q] * near[2]
    two = two + weight[3, x, q] * near[3]
    return one + (two + weight[5, x, q] * near[5])


def half_sweep(level, colour, v, wd, fd, first=0, last=None):
    def body(x, a, q):
        v[colour][x + 1, q] = relaxed(level, colour, x, a, q, v, wd, fd)

    planes(first, level.count if last is None else last, 8 if level.rows == 8 else 4, body)
    if level.fold == "x":
        fill_ends(level, v[colour])


def first_half(level, v, fd):
    for colour in (0, 1):
        fill_ends(level, v[colour])

    def body(x, a, q):
        v[0][x + 1, q] = fd[0][x, q]

    planes(0, level.count, 4, body)
    if level.fold == "x":
        fill_ends(level, v[0])


def descend(level, v, wd, fd, dd, cond, out_f, out_b, ranges=None):
    ranges = ranges or [(0, level.count)] * 4
    first_half(level, v, fd)
    half_sweep(level, 1, v, wd, fd, *ranges[0])
    half_sweep(level, 0, v, wd, fd, *ranges[1])
    half_sweep(level, 1, v, wd, fd, *ranges[2])
    first, last = ranges[3]

    def body(i, carry):
        for u in (0, 1):
            left = jnp.zeros((level.rows, 128), F32)
            mean = jnp.zeros((level.rows, 128), F32)
            for a in (0, 1):
                for q in (0, 1):
                    x = first + 4 * i + 2 * u + a
                    left = left + dd[x, q] * (relaxed(level, 0, x, a, q, v, wd, fd) - v[0][x + 1, q])
                    mean = mean + (cond[0][x, q] + cond[1][x, q])
            out_f[2 * i + u] = left
            out_b[2 * i + u] = 0.125 * mean
        return carry

    lax.fori_loop(0, (last - first) // 4, body, 0)


def ascend(level, v, wd, fd, ranges=None):
    ranges = ranges or [(0, level.count)] * 4
    for step in range(2 * SWEEPS):
        half_sweep(level, step % 2, v, wd, fd, *ranges[step])


def correct(level, v, black, add):
    for colour in (0, 1):
        fill_ends(level, v[colour])

    def body(x, a, q):
        v[1][x + 1, q] = black[x, q] + add[x // 2]

    planes(0, level.count, 4, body)
    if level.fold == "x":
        fill_ends(level, v[1])


def keep_black(level, v, black):
    def body(x, a, q):
        black[x, q] = v[1][x + 1, q]

    planes(0, level.count, 4, body)


def even_odd(v, x, a, q):
    red, black = v[0][x + 1, q], v[1][x + 1, q]
    return (red, black) if (a + q) % 2 == 0 else (black, red)


def exchange(blocks, width):
    group = lanes(8) // width
    step = len(blocks) // 2
    while step:
        swapped = list(blocks)
        for i in range(len(blocks)):
            if not i & step:
                a, b = blocks[i], blocks[i + step]
                low = group & step == 0
                swapped[i] = jnp.where(low, a, turn(b, width * step))
                swapped[i + step] = jnp.where(low, turn(a, -width * step), b)
        blocks = swapped
        step //= 2
    return blocks


def split_kernel(f_ref, b_ref, lo_ref, hi_ref, zl_ref, zr_ref):
    lane = lanes(16)
    whole = 2 * (lane % 64) + lane // 64
    slot = lane // 8
    within = lane % 8
    first = 2 * (within % 4) + within // 4
    last = 120 + first
    for half, out in enumerate((lo_ref, hi_ref)):
        for q in (0, 1):
            left = jnp.zeros((16, 128), F32)
            right = jnp.zeros((16, 128), F32)
            for x in range(8):
                for arr, ref in enumerate((f_ref, b_ref)):
                    cells = ref[8 * half + x, pl.ds(q, 16, stride=2), :]
                    out[8 * arr + x, q] = pick(cells, whole)
                    here = slot == 2 * x + arr
                    left = jnp.where(here, pick(cells, first), left)
                    right = jnp.where(here, pick(cells, last), right)
            zl_ref[half, q] = left
            zr_ref[half, q] = turn(right, 60)


def edge_kernel(a_ref, b_ref, c_ref, d_ref, lo_ref, hi_ref):
    low = rows_of(8) < 4
    for t, ref in enumerate((a_ref, b_ref, c_ref, d_ref)):
        for i in range(18):
            lo_ref[18 * t + i] = jnp.where(low, ref[i, 0, 0:8], pltpu.roll(ref[i, 1, 0:8], 4, 0))
            hi_ref[18 * t + i] = jnp.where(low, pltpu.roll(ref[i, 1, 8:16], 4, 0), ref[i, 0, 8:16])


def level0_down_kernel(
    scal, a_ref, b_ref, c_ref, d_ref, yl_ref, yr_ref,
    own_ref, zl_ref, zr_ref, black_ref, wd0, wd1, fd0, fd1,
    cond0, cond1, rec0, rec1, v0, v1, dd, nat_f, nat_b,
):
    cond, rec, v, wd, fd = (cond0, cond1), (rec0, rec1), (v0, v1), (wd0, wd1), (fd0, fd1)
    gx, gy, gz = scal[0], scal[1], scal[2]
    lane, row = lanes(24), rows_of(24)
    inside = (lane < 68) | (lane >= 124)
    inside = inside & ((gz > 0) | (lane < 124)) & ((gz < 7) | (lane < 64) | (lane >= 124))
    inside = inside & ((gy > 0) | (row < 20)) & ((gy < 7) | (row < 16) | (row >= 20))
    keep = jnp.where(inside, 1.0, 0.0)
    low = rows_of(8) < 4
    for t, ref in enumerate((a_ref, b_ref, c_ref, d_ref)):
        here = keep
        if t == 0:
            here = keep * jnp.where(gx > 0, 1.0, 0.0)
        if t == 3:
            here = keep * jnp.where(gx < 3, 1.0, 0.0)

        def wide(i, q):
            right, left = yr_ref[18 * t + i], yl_ref[18 * t + i]
            edge = jnp.where(low, right, left) if q == 0 else pltpu.roll(jnp.where(low, left, right), 4, 0)
            return jnp.concatenate([ref[i, q], edge], axis=0)

        ends = [(wide(16, q), wide(17, q)) for q in (0, 1)]
        for x in range(8):
            for q in (0, 1):
                from_left, from_right = ends[q]
                for arr in (0, 1):
                    s = 2 * x + arr
                    main = wide(8 * arr + x, q)
                    edge = jnp.where(lane // 8 == s, from_right, from_left)
                    even = jnp.where(lane < 64, main, turn(edge, 64 - 8 * s))
                    odd = jnp.where(lane < 64, turn(main, 64), turn(edge, 60 - 8 * s))
                    cells = (even, odd) if (x + q) % 2 == 0 else (odd, even)
                    for colour in (0, 1):
                        if arr == 0:
                            fd[colour][8 * t + x, q] = cells[colour]
                        else:
                            on_grid = cells[colour] * here
                            cond[colour][8 * t + x, q] = on_grid
                            rec[colour][8 * t + x + 1, q] = jnp.where(
                                here > 0.0, inverse_of(cells[colour]), OFF
                            )
    set_up(L0, cond, rec, wd, fd, dd)
    descend(L0, v, wd, fd, dd, cond, nat_f, nat_b, [(2, 30), (2, 30), (4, 28), (8, 24)])
    keep_black(L0, v, black_ref)
    lane8 = lanes(8)
    k = lane8 % 64
    spread = 2 * jnp.clip(k - 16, 0, 31) + lane8 // 64
    near = 2 * (lane8 % 16) + (lane8 // 16) % 2
    for x in range(0, 8, 2):
        for q in (0, 1):
            left, right = [], []
            for a in (0, 1):
                f = nat_f[x + a, pl.ds(q, 8, stride=2), :]
                b = nat_b[x + a, pl.ds(q, 8, stride=2), :]
                own_ref[x + a, q] = pick(f, spread)
                own_ref[8 + x + a, q] = pick(b, spread)
                here = lane8 % 64 < 32
                left.append(jnp.where(here, pick(f, near), pick(b, near)))
                right.append(jnp.where(here, pick(f, near + 32), pick(b, near + 32)))
            zl_ref[x // 2, q] = jnp.where(lane8 < 64, left[0], left[1])
            zr_ref[x // 2, q] = jnp.where(lane8 < 64, right[0], right[1])


def widen_kernel(own_ref, left_ref, right_ref, out_ref):
    lane = lanes(8)
    k = lane % 64
    index = lane % 16 + 16 * (lane // 64)
    for x in range(8):
        for q in (0, 1):
            for arr in (0, 1):
                there = index + 64 * (x % 2) + 32 * arr
                edge = jnp.where(k < 16, pick(left_ref[x // 2, q], there), pick(right_ref[x // 2, q], there))
                out_ref[8 * arr + x, q] = jnp.where((k >= 16) & (k < 48), own_ref[8 * arr + x, q], edge)


def strip_kernel(a_ref, b_ref, c_ref, d_ref, lo_ref, hi_ref):
    low = rows_of(8) < 4
    for t, ref in enumerate((a_ref, b_ref, c_ref, d_ref)):
        for i in range(16):
            zero, one = ref[i, 0], ref[i, 1]
            lo_ref[20 * t + i] = jnp.where(low, zero, pltpu.roll(one, 4, 0))
            hi_ref[20 * t + i] = jnp.where(low, pltpu.roll(zero, 4, 0), one)
            for q in (0, 1):
                row = 2 * (i % 4) + q
                lo_ref[20 * t + 16 + i // 4, row : row + 1] = ref[i, q, 4:5]
                hi_ref[20 * t + 16 + i // 4, row : row + 1] = ref[i, q, 3:4]


def level1_down_kernel(
    scal, a_ref, b_ref, c_ref, d_ref, yl_ref, yr_ref,
    out_ref, black_ref, wd0, wd1, fd0, fd1,
    cond0, cond1, rec0, rec1, v0, v1, dd, nat_f, nat_b, own,
):
    cond, rec, v, wd, fd = (cond0, cond1), (rec0, rec1), (v0, v1), (wd0, wd1), (fd0, fd1)
    gx, gy, gz = scal[0], scal[1], scal[2]
    lane = lanes(8)
    k = lane % 64
    inside = ((gz > 0) | (k >= 16)) & ((gz < 7) | (k < 48))
    keep = jnp.where(inside, 1.0, 0.0)
    row = rows_of(8)
    for i, ref in enumerate((a_ref, b_ref, c_ref, d_ref)):
        own[i] = ref[...]
    for block in range(3):
        here = keep
        if block == 0:
            here = jnp.where(row >= 3, keep, 0.0) * jnp.where(gy > 0, 1.0, 0.0)
        if block == 2:
            here = jnp.where(row < 5, keep, 0.0) * jnp.where(gy < 7, 1.0, 0.0)
        rows = pl.ds(8 * block, 8)

        def cells_of(slot, i, q):
            if block == 1:
                return own[slot, i, q]
            ref = yl_ref if block == 0 else yr_ref
            cells = ref[20 * slot + i]
            if (block == 0) == (q == 0):
                cells = pltpu.roll(cells, 4, 0)
            at = 2 * (i % 4) + q
            single = ref[20 * slot + 16 + i // 4, at : at + 1]
            return jnp.where(row == (3 if block == 0 else 4), single, cells)

        def body(j, carry):
            slots = [(gx + 4 - j) % 4, (gx + 6 - j) % 4]
            for x in range(8):
                for q in (0, 1):
                    parts = []
                    for arr in (0, 8):
                        first, second = [cells_of(slot, arr + x, q) for slot in slots]
                        parts.append(jnp.where(lane < 64, first, turn(second, 64)))
                        parts.append(jnp.where(lane < 64, turn(first, 64), second))
                    for colour in (0, 1):
                        odd = (x + q + colour) % 2
                        fd[colour][8 * j + x, q, rows] = parts[odd]
                        cond[colour][8 * j + x, q, rows] = parts[2 + odd] * here
                        rec[colour][8 * j + x + 1, q, rows] = jnp.where(
                            here > 0.0, inverse_of(parts[2 + odd]), OFF
                        )
            return carry

        lax.fori_loop(0, 2, body, 0)
    set_up(L1, cond, rec, wd, fd, dd)
    descend(L1, v, wd, fd, dd, cond, nat_f, nat_b)
    keep_black(L1, v, black_ref)
    for h in (0, 1):
        index = 64 * h + 2 * (lane % 32) + (lane // 32) % 2
        for x in range(8):
            f = pick(nat_f[x, 8:16], index)
            b = pick(nat_b[x, 8:16], index)
            nat_f[x, 0:8] = jnp.where(lane < 64, f, b)
            for q in (0, 1):
                out_ref[8 * h + x, 4 * q : 4 * q + 4] = nat_f[x, pl.ds(q, 4, stride=2), :]


def level2_down_kernel(
    scal, in_ref,
    out_ref, black_ref, wd0, wd1, fd0, fd1,
    cond0, cond1, rec0, rec1, v0, v1, dd, nat_f, nat_b,
):
    cond, rec, v, wd, fd = (cond0, cond1), (rec0, rec1), (v0, v1), (wd0, wd1), (fd0, fd1)
    gy, gz = scal[1], scal[2]
    chip = gy // 2
    lane = lanes(8)
    k = lane % 32
    inside = ((gz > 0) | (k >= 8)) & ((gz < 7) | (k < 24))
    slots = [(chip + 4 - j) % 4 for j in range(4)]

    def body(x, a, q):
        mains = []
        for slot in slots:
            both = [in_ref[c, slot, x, 4 * q : 4 * q + 4] for c in (0, 1)]
            mains.append(jnp.concatenate(both, axis=0))
        parts = exchange(mains, 32)
        for colour in (0, 1):
            odd = (a + q + colour) % 2
            fd[colour][x, q] = parts[odd]
            cond[colour][x, q] = jnp.where(inside, parts[2 + odd], 0.0)
            rec[colour][x + 1, q] = jnp.where(inside, inverse_of(parts[2 + odd]), OFF)

    planes(0, 16, 4, body)
    set_up(L2, cond, rec, wd, fd, dd)
    descend(L2, v, wd, fd, dd, cond, nat_f, nat_b)
    keep_black(L2, v, black_ref)
    index = 32 * (lane // 32) + 8 + 2 * (lane % 8) + (lane // 8) % 2
    for x in range(8):
        packed = jnp.where(lane % 32 < 16, pick(nat_f[x], index), pick(nat_b[x], index))
        out_ref[x] = packed


def coarse_kernel(
    scal, own_ref, pair_ref, far_ref, out_ref,
    cond30, cond31, rec30, rec31, v30, v31, dd3, wd30, wd31, fd30, fd31, nat_f, nat_b,
    cond40, cond41, rec40, rec41, v40, v41, dd4, wd40, wd41, fd40, fd41, slabs, whole, nat4, nat3,
):
    cond3, rec3, v3, wd3, fd3 = (cond30, cond31), (rec30, rec31), (v30, v31), (wd30, wd31), (fd30, fd31)
    cond4, rec4, v4, wd4, fd4 = (cond40, cond41), (rec40, rec41), (v40, v41), (wd40, wd41), (fd40, fd41)
    gz = scal[2]
    lane = lanes(8)

    slabs[gz] = own_ref[...]
    slabs[(gz + 4) % 8] = far_ref[...]
    for j in range(3):
        slabs[(gz + 7 - j) % 8] = pair_ref[0, j]
        slabs[(gz + 1 + j) % 8] = pair_ref[1, j]

    for x in range(8):
        for c, cells in enumerate(exchange([slabs[r, x] for r in range(8)], 8)):
            whole[c % 4, x, 8 * (c // 4) : 8 * (c // 4) + 8] = cells

    def place3(x, a, q):
        for colour in (0, 1):
            odd = (a + q + colour) % 2
            fd3[colour][x, q] = whole[odd, x, pl.ds(q, 8, stride=2), :]
            cells = whole[2 + odd, x, pl.ds(q, 8, stride=2), :]
            cond3[colour][x, q] = cells
            rec3[colour][x + 1, q] = inverse_of(cells)

    planes(0, 8, 4, place3)
    set_up(L3, cond3, rec3, wd3, fd3, dd3)
    descend(L3, v3, wd3, fd3, dd3, cond3, nat_f, nat_b)
    on_grid = lane < 32
    for x in range(4):
        f_plane, b_plane = nat_f[x], nat_b[x]
        for half in (0, 1):
            nat4[x, 8 * half : 8 * half + 8] = turn(f_plane, 64 * half)
            whole[0, x, 8 * half : 8 * half + 8] = turn(b_plane, 64 * half)
        for q in (0, 1):
            f = nat4[x, pl.ds(q, 8, stride=2), :]
            b = whole[0, x, pl.ds(q, 8, stride=2), :]
            for e in (0, 1):
                colour = (x + q + e) % 2
                index = 2 * (lane % 32) + e
                fd4[colour][x, q] = pick(f, index)
                cells = pick(b, index)
                cond4[colour][x, q] = jnp.where(on_grid, cells, 0.0)
                rec4[colour][x + 1, q] = jnp.where(on_grid, inverse_of(cells), OFF)
    set_up(L4, cond4, rec4, wd4, fd4, dd4)

    def half(colour, other):
        made = {}
        for x in range(4):
            for q in (0, 1):
                mid, across = other[x, q], other[x, 1 - q]
                weight = lambda i: wd4[colour][i, x, q]
                total = fd4[colour][x, q] + weight(4) * mid
                total = total + weight(2) * (across if q == 0 else up(L4, across))
                total = total + weight(3) * (down(L4, across) if q == 0 else across)
                rest = weight(5) * turn(mid, 1 if goes_back(colour, x, q) else -1)
                if x < 3:
                    rest = rest + weight(0) * other[x + 1, q]
                if x > 0:
                    rest = rest + weight(1) * other[x - 1, q]
                made[x, q] = total + rest
        return made

    keys = [(x, q) for x in range(4) for q in (0, 1)]
    black = half(1, {key: fd4[0][key] for key in keys})

    def step(_, carry):
        after = half(1, half(0, dict(zip(keys, carry))))
        return tuple(after[key] for key in keys)

    final = lax.fori_loop(0, ITERS - 2, step, tuple(black[key] for key in keys))
    red = half(0, dict(zip(keys, final)))
    black = half(1, red)
    index = (lane % 2) * 32 + (lane // 2) % 32
    for x, q in keys:
        even, odd = (red[x, q], black[x, q]) if (x + q) % 2 == 0 else (black[x, q], red[x, q])
        nat4[x, pl.ds(q, 8, stride=2), :] = pick(jnp.where(lane < 32, even, turn(odd, 32)), index)
    for x in range(4):
        nat_f[x] = jnp.where(lane < 64, nat4[x, 0:8], turn(nat4[x, 8:16], 64))

    def add(x, a, q):
        v3[1][x + 1, q] = v3[1][x + 1, q] + nat_f[x // 2]

    planes(0, 8, 4, add)
    ascend(L3, v3, wd3, fd3)
    place = 16 * gz - 8 + lane % 32
    z = jnp.clip(place, 0, 127)
    index = (z % 2) * 64 + z // 2
    for x in range(8):
        for q in (0, 1):
            even, odd = even_odd(v3, x, x, q)
            first = pick(jnp.where(lane < 64, even, turn(odd, 64)), index)
            second = pick(jnp.where(lane < 64, turn(even, 64), odd), index)
            nat3[x, pl.ds(q, 8, stride=2), :] = first
            nat3[x, pl.ds(16 + q, 8, stride=2), :] = second
        cells = nat3[x, 0:8]
        for j in (1, 2, 3):
            cells = jnp.where(lane // 32 == j, nat3[x, 8 * j : 8 * j + 8], cells)
        out_ref[x] = jnp.where(place == z, cells, 0.0)


def level2_up_kernel(scal, black_ref, wd0, wd1, fd0, fd1, add_ref, out_ref, v0, v1, nat):
    v, wd, fd = (v0, v1), (wd0, wd1), (fd0, fd1)
    gy = scal[1]
    correct(L2, v, black_ref, add_ref)
    ascend(L2, v, wd, fd)
    lane = lanes(8)
    k = lane % 64
    base = (gy + 1) // 2 - 1
    groups = [base, base + 1]

    def store(x, a, q):
        even, odd = even_odd(v, x, a, q)
        for i, mq in enumerate(groups):
            index = 32 * jnp.clip(mq, 0, 3) + k // 2
            cells = jnp.where(lane % 2 == 0, pick(even, index), pick(odd, index))
            nat[x, pl.ds(16 * i + q, 8, stride=2), :] = jnp.where((mq >= 0) & (mq < 4), cells, 0.0)

    planes(0, 16, 4, store)
    start = pl.multiple_of(8 - 8 * (gy % 2), 8)
    side = lanes(24) < 64
    for x in range(8):
        out_ref[x] = jnp.where(side, nat[x, pl.ds(start, 24), :], nat[8 + x, pl.ds(start, 24), :])


def level1_up_kernel(scal, black_ref, wd0, wd1, fd0, fd1, add_ref, out_ref, v0, v1, nat):
    v, wd, fd = (v0, v1), (wd0, wd1), (fd0, fd1)
    gx = scal[0]
    correct(L1, v, black_ref, add_ref)
    ascend(L1, v, wd, fd)
    lane = lanes(24)
    z = jnp.where(lane < 96, lane, lane - 128) + 32
    index = jnp.clip(z // 2, 0, 63)

    def store(i, carry):
        for u in range(4):
            x = 8 * gx - 4 + 4 * i + u
            inside = (x >= 0) & (x < 32)
            x = jnp.clip(x, 0, 31)
            there = 64 * (x // 16) + index
            for q in (0, 1):
                even, odd = even_odd(v, x % 16, u, q)
                cells = jnp.where(lane % 2 == 0, pick(even, there), pick(odd, there))
                nat[4 * i + u, pl.ds(q, 24, stride=2), :] = jnp.where(inside, cells, 0.0)
        return carry

    lax.fori_loop(0, 4, store, 0)
    for x in range(16):
        out_ref[x, 0:16] = nat[x, 16:32]
        out_ref[x, 16:20] = nat[x, 32:36]
        out_ref[x, 20:24] = nat[x, 12:16]


def level0_up_kernel(black_ref, wd0, wd1, fd0, fd1, add_ref, out_ref, v0, v1):
    v, wd, fd = (v0, v1), (wd0, wd1), (fd0, fd1)
    correct(L0, v, black_ref, add_ref)
    ascend(L0, v, wd, fd, [(4, 28), (6, 26), (6, 26), (8, 24)])
    lane = lanes(16)
    index = (lane % 2) * 64 + lane // 2

    def store(x, a, q):
        even, odd = even_odd(v, x, a, q)
        packed = jnp.where(lane < 64, even[0:16], turn(odd[0:16], 64))
        out_ref[x - 8, pl.ds(q, 16, stride=2), :] = pick(packed, index)

    planes(8, 24, 4, store)


def arr(*shape):
    return jax.ShapeDtypeStruct(shape, F32)


def scratch(*shape):
    return pltpu.VMEM(shape, F32)


def level_scratch(level):
    shapes = [level.own()] * 2 + [level.wide()] * 4 + [level.own()]
    return [scratch(*s) for s in shapes]


def nat_scratch(level, count=None):
    return [scratch(count or level.count // 2, level.rows, 128)] * 2


def weights(level):
    return [(6,) + level.own()] * 2 + [level.own()] * 2


def call(kernel, outs, temps, *args, scal=None, limit=28):
    specs = [VMEM] * len(args)
    if scal is not None:
        specs = [SMEM] + specs
        args = (scal,) + args
    return pl.pallas_call(
        kernel,
        out_shape=outs,
        in_specs=specs,
        out_specs=jax.tree.map(lambda _: VMEM, outs),
        scratch_shapes=temps,
        compiler_params=pltpu.CompilerParams(vmem_limit_bytes=limit * 1024 * 1024),
    )(*args)


def ring(values, axis, step):
    count = lax.axis_size(axis)
    return lax.ppermute(values, axis, [(i, (i + step) % count) for i in range(count)])


def both_cores(values):
    count = lax.axis_size("gy")
    return lax.all_gather(values, "gy", axis=0, axis_index_groups=[[i, i + 1] for i in range(0, count, 2)])


def along_z(values, step):
    rows, count = lax.axis_size("gy"), lax.axis_size("gz")
    pairs = []
    for i in range(rows):
        for k in range(count):
            pairs.append((i * count + k, i * count + (k + (-step if i % 2 else step)) % count))
    return lax.ppermute(values, ("gy", "gz"), pairs)


def on_device(right_side, coefficient):
    scal = jnp.stack([lax.axis_index("gx"), lax.axis_index("gy"), lax.axis_index("gz")]).astype(jnp.int32)
    half = arr(16, 2, 16, 128)
    strip = arr(2, 2, 16, 128)
    lo, hi, zl, zr = call(split_kernel, [half, half, strip, strip], [], right_side, coefficient)
    from_left, from_right = ring(zr, "gz", 1), ring(zl, "gz", -1)
    lo = jnp.concatenate([lo, from_left[0:1], from_right[0:1]])
    hi = jnp.concatenate([hi, from_left[1:2], from_right[1:2]])
    before, after = ring(hi, "gx", 1), ring(lo, "gx", -1)
    bundles = (before, lo, hi, after)
    yl, yr = call(edge_kernel, [arr(72, 8, 128)] * 2, [], *bundles)
    from_left, from_right = ring(yr, "gy", 1), ring(yl, "gy", -1)
    own, zl, zr, black0, *set0 = call(
        level0_down_kernel,
        [arr(16, 2, 8, 128), arr(4, 2, 8, 128), arr(4, 2, 8, 128), arr(*L0.own())]
        + [arr(*s) for s in weights(L0)],
        level_scratch(L0) + nat_scratch(L0, 8),
        *bundles, from_left, from_right, scal=scal,
    )
    from_left, from_right = ring(zr, "gz", 1), ring(zl, "gz", -1)
    bundle = call(widen_kernel, arr(16, 2, 8, 128), [], own, from_left, from_right)
    column = [bundle] + [ring(bundle, "gx", s) for s in (1, 2, 3)]
    yl, yr = call(strip_kernel, [arr(80, 8, 128)] * 2, [], *column)
    own, black1, *set1 = call(
        level1_down_kernel,
        [arr(16, 8, 128), arr(*L1.own())] + [arr(*s) for s in weights(L1)],
        level_scratch(L1) + nat_scratch(L1) + [scratch(4, 16, 2, 8, 128)],
        *column, ring(yr, "gy", 1), ring(yl, "gy", -1), scal=scal,
    )
    own = own[None]
    sheet = jnp.concatenate([own] + [ring(own, "gy", 2 * s) for s in (1, 2, 3)])
    sheet = both_cores(sheet)
    own, black2, *set2 = call(
        level2_down_kernel,
        [arr(8, 8, 128), arr(*L2.own())] + [arr(*s) for s in weights(L2)],
        level_scratch(L2) + nat_scratch(L2),
        sheet, scal=scal,
    )
    far = along_z(own, 4)
    near = both_cores(jnp.stack([along_z(own, s) for s in (1, 2, 3)]))
    correction = call(
        coarse_kernel,
        arr(8, 8, 128),
        level_scratch(L3) + [scratch(*s) for s in weights(L3)] + nat_scratch(L3)
        + level_scratch(L4) + [scratch(*s) for s in weights(L4)]
        + [scratch(8, 8, 8, 128), scratch(4, 8, 16, 128), scratch(4, 16, 128), scratch(8, 32, 128)],
        own, near, far, scal=scal,
    )
    correction = call(
        level2_up_kernel, arr(8, 24, 128),
        [scratch(*L2.wide())] * 2 + [scratch(16, 32, 128)],
        black2, *set2, correction, scal=scal,
    )
    correction = call(
        level1_up_kernel, arr(16, 24, 128),
        [scratch(*L1.wide())] * 2 + [scratch(16, 48, 128)],
        black1, *set1, correction, scal=scal,
    )
    return call(
        level0_up_kernel, arr(16, 32, 128),
        [scratch(*L0.wide())] * 2,
        black0, *set0, correction,
    )


def solution(mesh):
    spec = P("gx", "gy", "gz")
    return jax.shard_map(on_device, mesh=mesh, in_specs=(spec, spec), out_specs=spec, check_vma=False)
```

```python
import functools

import jax
import jax.numpy as jnp
from jax import lax
from jax.experimental import pallas as pl
from jax.experimental.pallas import tpu as pltpu
from jax.sharding import PartitionSpec as P

SWEEPS = 2
ITERS = 20
F32 = jnp.float32
OFF = 1e-20
VMEM = pl.BlockSpec(memory_space=pltpu.VMEM)
SMEM = pl.BlockSpec(memory_space=pltpu.SMEM)


class Level:
    def __init__(self, count, rows, group, fold):
        self.count, self.rows, self.group, self.fold = count, rows, group, fold

    def wide(self):
        return (self.count + 2, 2, self.rows, 128)

    def own(self):
        return (self.count, 2, self.rows, 128)


L0 = Level(32, 24, 128, None)
L1 = Level(16, 24, 64, "x")
L2 = Level(16, 8, 32, "y")
L3 = Level(8, 8, 64, "y")


def lanes(rows):
    return lax.broadcasted_iota(jnp.int32, (rows, 128), 1)


def rows_of(rows):
    return lax.broadcasted_iota(jnp.int32, (rows, 128), 0)


def pick(values, index):
    return jnp.take_along_axis(values, index, axis=1, mode="promise_in_bounds")


def turn(values, shift):
    shift = shift % 128
    return pltpu.roll(values, shift, 1) if shift else values


def inverse_of(values):
    return pl.reciprocal(values, approx=True)


def up(level, values):
    rolled = pltpu.roll(values, level.rows - 1, 0)
    if level.fold == "y":
        rolled = jnp.where(rows_of(level.rows) == level.rows - 1, turn(rolled, -level.group), rolled)
    return rolled


def down(level, values):
    rolled = pltpu.roll(values, 1, 0)
    if level.fold == "y":
        rolled = jnp.where(rows_of(level.rows) == 0, turn(rolled, level.group), rolled)
    return rolled


def goes_back(colour, a, q):
    return (colour == 0) == ((a + q) % 2 == 0)


def beside(level, other, x, q, colour, a):
    mid = other[x + 1, q]
    across = other[x + 1, 1 - q]
    return [
        other[x + 2, q],
        other[x, q],
        across if q == 0 else up(level, across),
        down(level, across) if q == 0 else across,
        mid,
        turn(mid, 1 if goes_back(colour, a, q) else -1),
    ]


def planes(first, last, unroll, body):
    pairs = (last - first) // 2
    unroll = min(unroll, pairs)
    while pairs % unroll:
        unroll -= 1

    def step(i, carry):
        for u in range(unroll):
            for a in (0, 1):
                for q in (0, 1):
                    body(first + 2 * (unroll * i + u) + a, a, q)
        return carry

    if pairs == unroll:
        step(0, 0)
    else:
        lax.fori_loop(0, pairs // unroll, step, 0)


def fill_ends(level, values, rest=0.0):
    lane = lanes(level.rows)
    for q in (0, 1):
        if level.fold == "x":
            values[0, q] = jnp.where(lane < 64, rest, turn(values[level.count, q], 64))
            values[level.count + 1, q] = jnp.where(lane < 64, turn(values[1, q], 64), rest)
        else:
            values[0, q] = jnp.full((level.rows, 128), rest, F32)
            values[level.count + 1, q] = jnp.full((level.rows, 128), rest, F32)


def set_up(level, cond, rec, wd, fd, dd):
    rows = level.rows
    row, lane = rows_of(rows), lanes(rows)
    for colour in (0, 1):
        fill_ends(level, rec[colour], OFF)

    def body(x, a, q):
        for colour in (0, 1):
            own_rec = rec[colour][x + 1, q]
            near = beside(level, rec[1 - colour], x, q, colour, a)
            walls = {}
            if level.fold == "y":
                if q == 0:
                    walls[3] = (row == 0) & (lane < level.group)
                else:
                    walls[2] = (row == rows - 1) & (lane >= 128 - level.group)
            if level.group < 128:
                end = 0 if goes_back(colour, a, q) else level.group - 1
                walls[5] = lane % level.group == end
            total = None
            faces = []
            for i, value in enumerate(near):
                if i in walls:
                    value = jnp.where(walls[i], OFF, value)
                face = inverse_of(own_rec + value)
                faces.append(face)
                total = face if total is None else total + face
            inverse = jnp.where(own_rec > 1e-10, inverse_of(total), 0.0)
            for i, face in enumerate(faces):
                weight = face * inverse
                wd[colour][i, x, q] = jnp.where(walls[i], 0.0, weight) if i in walls else weight
            fd[colour][x, q] = fd[colour][x, q] * (0.5 * inverse)
            if colour == 0:
                dd[x, q] = total

    planes(0, level.count, 4 if level.rows == 8 else 1, body)


def relaxed(level, colour, x, a, q, v, wd, fd):
    near = beside(level, v[1 - colour], x, q, colour, a)
    weight = wd[colour]
    one = fd[colour][x, q] + weight[0, x, q] * near[0]
    two = weight[4, x, q] * near[4] + weight[1, x, q] * near[1]
    one = one + weight[2, x, q] * near[2]
    two = two + weight[3, x, q] * near[3]
    return one + (two + weight[5, x, q] * near[5])


def half_sweep(level, colour, v, wd, fd, first=0, last=None):
    def body(x, a, q):
        v[colour][x + 1, q] = relaxed(level, colour, x, a, q, v, wd, fd)

    planes(first, level.count if last is None else last, 8 if level.rows == 8 else 4, body)
    if level.fold == "x":
        fill_ends(level, v[colour])


def first_half(level, v, fd):
    for colour in (0, 1):
        fill_ends(level, v[colour])

    def body(x, a, q):
        v[0][x + 1, q] = fd[0][x, q]

    planes(0, level.count, 4, body)
    if level.fold == "x":
        fill_ends(level, v[0])


def descend(level, v, wd, fd, dd, cond, out_f, out_b, ranges=None):
    ranges = ranges or [(0, level.count)] * 4
    first_half(level, v, fd)
    half_sweep(level, 1, v, wd, fd, *ranges[0])
    half_sweep(level, 0, v, wd, fd, *ranges[1])
    half_sweep(level, 1, v, wd, fd, *ranges[2])
    first, last = ranges[3]

    def body(i, carry):
        for u in (0, 1):
            left = jnp.zeros((level.rows, 128), F32)
            mean = jnp.zeros((level.rows, 128), F32)
            for a in (0, 1):
                for q in (0, 1):
                    x = first + 4 * i + 2 * u + a
                    left = left + dd[x, q] * (relaxed(level, 0, x, a, q, v, wd, fd) - v[0][x + 1, q])
                    mean = mean + (cond[0][x, q] + cond[1][x, q])
            out_f[2 * i + u] = left
            out_b[2 * i + u] = 0.125 * mean
        return carry

    lax.fori_loop(0, (last - first) // 4, body, 0)


def ascend(level, v, wd, fd, ranges=None):
    ranges = ranges or [(0, level.count)] * 4
    for step in range(2 * SWEEPS):
        half_sweep(level, step % 2, v, wd, fd, *ranges[step])


def correct(level, v, black, add):
    for colour in (0, 1):
        fill_ends(level, v[colour])

    def body(x, a, q):
        v[1][x + 1, q] = black[x, q] + add[x // 2]

    planes(0, level.count, 4, body)
    if level.fold == "x":
        fill_ends(level, v[1])


def keep_black(level, v, black):
    def body(x, a, q):
        black[x, q] = v[1][x + 1, q]

    planes(0, level.count, 4, body)


def even_odd(v, x, a, q):
    red, black = v[0][x + 1, q], v[1][x + 1, q]
    return (red, black) if (a + q) % 2 == 0 else (black, red)


def exchange(blocks, width):
    group = lanes(8) // width
    step = len(blocks) // 2
    while step:
        swapped = list(blocks)
        for i in range(len(blocks)):
            if not i & step:
                a, b = blocks[i], blocks[i + step]
                low = group & step == 0
                swapped[i] = jnp.where(low, a, turn(b, width * step))
                swapped[i + step] = jnp.where(low, turn(a, -width * step), b)
        blocks = swapped
        step //= 2
    return blocks


def split_kernel(f_ref, b_ref, lo_ref, hi_ref, zl_ref, zr_ref):
    lane = lanes(16)
    whole = 2 * (lane % 64) + lane // 64
    slot = lane // 8
    within = lane % 8
    first = 2 * (within % 4) + within // 4
    last = 120 + first
    for half, out in enumerate((lo_ref, hi_ref)):
        for q in (0, 1):
            left = jnp.zeros((16, 128), F32)
            right = jnp.zeros((16, 128), F32)
            for x in range(8):
                for arr, ref in enumerate((f_ref, b_ref)):
                    cells = ref[8 * half + x, pl.ds(q, 16, stride=2), :]
                    out[8 * arr + x, q] = pick(cells, whole)
                    here = slot == 2 * x + arr
                    left = jnp.where(here, pick(cells, first), left)
                    right = jnp.where(here, pick(cells, last), right)
            zl_ref[half, q] = left
            zr_ref[half, q] = turn(right, 60)


def edge_kernel(*refs):
    mains, strips, lo_ref, hi_ref = refs[0:4], refs[4:8], refs[8], refs[9]
    low = rows_of(8) < 4
    for t in range(4):
        for i in range(18):
            ref, at = (mains[t], i) if i < 16 else (strips[t], i - 16)
            lo_ref[18 * t + i] = jnp.where(low, ref[at, 0, 0:8], pltpu.roll(ref[at, 1, 0:8], 4, 0))
            hi_ref[18 * t + i] = jnp.where(low, pltpu.roll(ref[at, 1, 8:16], 4, 0), ref[at, 0, 8:16])


def level0_down_kernel(
    scal, m0, m1, m2, m3, s0, s1, s2, s3, yl_ref, yr_ref,
    own_ref, zl_ref, zr_ref, black_ref, wd0, wd1, fd0, fd1,
    cond0, cond1, rec0, rec1, v0, v1, dd, nat_f, nat_b,
):
    cond, rec, v, wd, fd = (cond0, cond1), (rec0, rec1), (v0, v1), (wd0, wd1), (fd0, fd1)
    gx, gy, gz = scal[0], scal[1], scal[2]
    lane, row = lanes(24), rows_of(24)
    inside = (lane < 68) | (lane >= 124)
    inside = inside & ((gz > 0) | (lane < 124)) & ((gz < 7) | (lane < 64) | (lane >= 124))
    inside = inside & ((gy > 0) | (row < 20)) & ((gy < 7) | (row < 16) | (row >= 20))
    keep = jnp.where(inside, 1.0, 0.0)
    low = rows_of(8) < 4
    for t, (main_ref, strip_ref) in enumerate(((m0, s0), (m1, s1), (m2, s2), (m3, s3))):
        here = keep
        if t == 0:
            here = keep * jnp.where(gx > 0, 1.0, 0.0)
        if t == 3:
            here = keep * jnp.where(gx < 3, 1.0, 0.0)

        def wide(i, q):
            right, left = yr_ref[18 * t + i], yl_ref[18 * t + i]
            edge = jnp.where(low, right, left) if q == 0 else pltpu.roll(jnp.where(low, left, right), 4, 0)
            own = main_ref[i, q] if i < 16 else strip_ref[i - 16, q]
            return jnp.concatenate([own, edge], axis=0)

        ends = [(wide(16, q), wide(17, q)) for q in (0, 1)]
        for x in range(8):
            for q in (0, 1):
                from_left, from_right = ends[q]
                for arr in (0, 1):
                    s = 2 * x + arr
                    main = wide(8 * arr + x, q)
                    edge = jnp.where(lane // 8 == s, from_right, from_left)
                    even = jnp.where(lane < 64, main, turn(edge, 64 - 8 * s))
                    odd = jnp.where(lane < 64, turn(main, 64), turn(edge, 60 - 8 * s))
                    cells = (even, odd) if (x + q) % 2 == 0 else (odd, even)
                    for colour in (0, 1):
                        if arr == 0:
                            fd[colour][8 * t + x, q] = cells[colour]
                        else:
                            on_grid = cells[colour] * here
                            cond[colour][8 * t + x, q] = on_grid
                            rec[colour][8 * t + x + 1, q] = jnp.where(
                                here > 0.0, inverse_of(cells[colour]), OFF
                            )
    set_up(L0, cond, rec, wd, fd, dd)
    descend(L0, v, wd, fd, dd, cond, nat_f, nat_b, [(2, 30), (2, 30), (4, 28), (8, 24)])
    keep_black(L0, v, black_ref)
    lane8 = lanes(8)
    k = lane8 % 64
    spread = 2 * jnp.clip(k - 16, 0, 31) + lane8 // 64
    near = 2 * (lane8 % 16) + (lane8 // 16) % 2
    for x in range(0, 8, 2):
        for q in (0, 1):
            left, right = [], []
            for a in (0, 1):
                f = nat_f[x + a, pl.ds(q, 8, stride=2), :]
                b = nat_b[x + a, pl.ds(q, 8, stride=2), :]
                own_ref[x + a, q] = pick(f, spread)
                own_ref[8 + x + a, q] = pick(b, spread)
                here = lane8 % 64 < 32
                left.append(jnp.where(here, pick(f, near), pick(b, near)))
                right.append(jnp.where(here, pick(f, near + 32), pick(b, near + 32)))
            zl_ref[x // 2, q] = jnp.where(lane8 < 64, left[0], left[1])
            zr_ref[x // 2, q] = jnp.where(lane8 < 64, right[0], right[1])


def widen_kernel(own_ref, left_ref, right_ref, out_ref):
    lane = lanes(8)
    k = lane % 64
    index = lane % 16 + 16 * (lane // 64)
    for x in range(8):
        for q in (0, 1):
            for arr in (0, 1):
                there = index + 64 * (x % 2) + 32 * arr
                edge = jnp.where(k < 16, pick(left_ref[x // 2, q], there), pick(right_ref[x // 2, q], there))
                out_ref[8 * arr + x, q] = jnp.where((k >= 16) & (k < 48), own_ref[8 * arr + x, q], edge)


def strip_kernel(a_ref, b_ref, c_ref, d_ref, lo_ref, hi_ref):
    low = rows_of(8) < 4
    for t, ref in enumerate((a_ref, b_ref, c_ref, d_ref)):
        for i in range(16):
            zero, one = ref[i, 0], ref[i, 1]
            lo_ref[20 * t + i] = jnp.where(low, zero, pltpu.roll(one, 4, 0))
            hi_ref[20 * t + i] = jnp.where(low, pltpu.roll(zero, 4, 0), one)
            for q in (0, 1):
                row = 2 * (i % 4) + q
                lo_ref[20 * t + 16 + i // 4, row : row + 1] = ref[i, q, 4:5]
                hi_ref[20 * t + 16 + i // 4, row : row + 1] = ref[i, q, 3:4]


def level1_down_kernel(
    scal, a_ref, b_ref, c_ref, d_ref, yl_ref, yr_ref,
    out_ref, black_ref, wd0, wd1, fd0, fd1,
    cond0, cond1, rec0, rec1, v0, v1, dd, nat_f, nat_b, own,
):
    cond, rec, v, wd, fd = (cond0, cond1), (rec0, rec1), (v0, v1), (wd0, wd1), (fd0, fd1)
    gx, gy, gz = scal[0], scal[1], scal[2]
    lane = lanes(8)
    k = lane % 64
    inside = ((gz > 0) | (k >= 16)) & ((gz < 7) | (k < 48))
    keep = jnp.where(inside, 1.0, 0.0)
    row = rows_of(8)
    for i, ref in enumerate((a_ref, b_ref, c_ref, d_ref)):
        own[i] = ref[...]
    for block in range(3):
        here = keep
        if block == 0:
            here = jnp.where(row >= 3, keep, 0.0) * jnp.where(gy > 0, 1.0, 0.0)
        if block == 2:
            here = jnp.where(row < 5, keep, 0.0) * jnp.where(gy < 7, 1.0, 0.0)
        rows = pl.ds(8 * block, 8)

        def cells_of(slot, i, q):
            if block == 1:
                return own[slot, i, q]
            ref = yl_ref if block == 0 else yr_ref
            cells = ref[20 * slot + i]
            if (block == 0) == (q == 0):
                cells = pltpu.roll(cells, 4, 0)
            at = 2 * (i % 4) + q
            single = ref[20 * slot + 16 + i // 4, at : at + 1]
            return jnp.where(row == (3 if block == 0 else 4), single, cells)

        def body(j, carry):
            slots = [(gx + 4 - j) % 4, (gx + 6 - j) % 4]
            for x in range(8):
                for q in (0, 1):
                    parts = []
                    for arr in (0, 8):
                        first, second = [cells_of(slot, arr + x, q) for slot in slots]
                        parts.append(jnp.where(lane < 64, first, turn(second, 64)))
                        parts.append(jnp.where(lane < 64, turn(first, 64), second))
                    for colour in (0, 1):
                        odd = (x + q + colour) % 2
                        fd[colour][8 * j + x, q, rows] = parts[odd]
                        cond[colour][8 * j + x, q, rows] = parts[2 + odd] * here
                        rec[colour][8 * j + x + 1, q, rows] = jnp.where(
                            here > 0.0, inverse_of(parts[2 + odd]), OFF
                        )
            return carry

        lax.fori_loop(0, 2, body, 0)
    set_up(L1, cond, rec, wd, fd, dd)
    descend(L1, v, wd, fd, dd, cond, nat_f, nat_b)
    keep_black(L1, v, black_ref)
    for h in (0, 1):
        index = 64 * h + 2 * (lane % 32) + (lane // 32) % 2
        for x in range(8):
            f = pick(nat_f[x, 8:16], index)
            b = pick(nat_b[x, 8:16], index)
            nat_f[x, 0:8] = jnp.where(lane < 64, f, b)
            for q in (0, 1):
                out_ref[8 * h + x, 4 * q : 4 * q + 4] = nat_f[x, pl.ds(q, 4, stride=2), :]


def level2_down_kernel(
    scal, in_ref,
    out_ref, black_ref, wd0, wd1, fd0, fd1,
    cond0, cond1, rec0, rec1, v0, v1, dd, nat_f, nat_b,
):
    cond, rec, v, wd, fd = (cond0, cond1), (rec0, rec1), (v0, v1), (wd0, wd1), (fd0, fd1)
    gy, gz = scal[1], scal[2]
    chip = gy // 2
    lane = lanes(8)
    k = lane % 32
    inside = ((gz > 0) | (k >= 8)) & ((gz < 7) | (k < 24))
    slots = [(chip + 4 - j) % 4 for j in range(4)]

    def body(x, a, q):
        mains = []
        for slot in slots:
            both = [in_ref[c, slot, x, 4 * q : 4 * q + 4] for c in (0, 1)]
            mains.append(jnp.concatenate(both, axis=0))
        parts = exchange(mains, 32)
        for colour in (0, 1):
            odd = (a + q + colour) % 2
            fd[colour][x, q] = parts[odd]
            cond[colour][x, q] = jnp.where(inside, parts[2 + odd], 0.0)
            rec[colour][x + 1, q] = jnp.where(inside, inverse_of(parts[2 + odd]), OFF)

    planes(0, 16, 4, body)
    set_up(L2, cond, rec, wd, fd, dd)
    descend(L2, v, wd, fd, dd, cond, nat_f, nat_b)
    keep_black(L2, v, black_ref)
    index = 32 * (lane // 32) + 8 + 2 * (lane % 8) + (lane // 8) % 2
    for x in range(8):
        packed = jnp.where(lane % 32 < 16, pick(nat_f[x], index), pick(nat_b[x], index))
        out_ref[x] = packed


def coarsest(f, b):
    lane, row = lanes(8), rows_of(8)
    x, k = lane // 32, lane % 32

    def near(values, colour, q):
        back = (x + q + colour) % 2 == 0
        across = values[1 - q]
        return [
            values[q],
            across,
            turn(values[q], -32),
            turn(values[q], 32),
            pltpu.roll(across, 1 if q == 0 else 7, 0),
            pick(values[q], (lane + jnp.where(back, 127, 1)) % 128),
        ]

    rec = [[inverse_of(cells) for cells in pair] for pair in b]
    weights, sources = [], []
    for colour in (0, 1):
        weights.append([])
        sources.append([])
        for q in (0, 1):
            back = (x + q + colour) % 2 == 0
            walls = [
                None, None, x == 3, x == 0, row == (0 if q == 0 else 7), k == jnp.where(back, 0, 31),
            ]
            faces, total = [], None
            for value, wall in zip(near(rec[1 - colour], colour, q), walls):
                if wall is not None:
                    value = jnp.where(wall, OFF, value)
                face = inverse_of(rec[colour][q] + value)
                total = face if total is None else total + face
                faces.append(face if wall is None else jnp.where(wall, 0.0, face))
            inverse = inverse_of(total)
            weights[-1].append([face * inverse for face in faces])
            sources[-1].append(f[colour][q] * (0.5 * inverse))

    def half(colour, other):
        made = []
        for q in (0, 1):
            total = sources[colour][q]
            for weight, value in zip(weights[colour][q], near(other, colour, q)):
                total = total + weight * value
            made.append(total)
        return made

    black = half(1, sources[0])

    def step(_, carry):
        return tuple(half(1, half(0, list(carry))))

    black = lax.fori_loop(0, ITERS - 2, step, tuple(black))
    red = half(0, list(black))
    return red, half(1, red)


def coarse_kernel(
    scal, own_ref, all_ref, out_ref,
    cond30, cond31, rec30, rec31, v30, v31, dd3, wd30, wd31, fd30, fd31, nat_f, nat_b,
    slabs, whole, nat4, nat3,
):
    cond3, rec3, v3, wd3, fd3 = (cond30, cond31), (rec30, rec31), (v30, v31), (wd30, wd31), (fd30, fd31)
    gz = scal[2]
    lane = lanes(8)
    slabs[gz] = own_ref[...]
    for j in range(4):
        slabs[(gz + 7 - j) % 8] = all_ref[0, j]
        slabs[(gz + 1 + j) % 8] = all_ref[1, j]

    for x in range(8):
        for c, cells in enumerate(exchange([slabs[r, x] for r in range(8)], 8)):
            whole[c % 4, x, 8 * (c // 4) : 8 * (c // 4) + 8] = cells

    def place3(x, a, q):
        for colour in (0, 1):
            odd = (a + q + colour) % 2
            fd3[colour][x, q] = whole[odd, x, pl.ds(q, 8, stride=2), :]
            cells = whole[2 + odd, x, pl.ds(q, 8, stride=2), :]
            cond3[colour][x, q] = cells
            rec3[colour][x + 1, q] = inverse_of(cells)

    planes(0, 8, 4, place3)
    set_up(L3, cond3, rec3, wd3, fd3, dd3)
    descend(L3, v3, wd3, fd3, dd3, cond3, nat_f, nat_b)
    f4 = [[None, None], [None, None]]
    b4 = [[None, None], [None, None]]
    for x in range(4):
        for arr, plane in enumerate((nat_f[x], nat_b[x])):
            for part in (0, 1):
                whole[arr, x, 8 * part : 8 * part + 8] = turn(plane, 64 * part)
        for made, arr in ((f4, 0), (b4, 1)):
            for q in (0, 1):
                cells = whole[arr, x, pl.ds(q, 8, stride=2), :]
                for colour in (0, 1):
                    mine = pick(cells, 2 * (lane % 32) + (x + q + colour) % 2)
                    before = made[colour][q]
                    made[colour][q] = mine if x == 0 else jnp.where(lane // 32 == x, mine, before)
    red, black = coarsest(f4, b4)
    for x in range(4):
        for q in (0, 1):
            even, odd = (red[q], black[q]) if (x + q) % 2 == 0 else (black[q], red[q])
            index = 32 * x + (lane % 64) // 2
            nat4[x, pl.ds(q, 8, stride=2), :] = jnp.where(lane % 2 == 0, pick(even, index), pick(odd, index))
    for x in range(4):
        nat_f[x] = jnp.where(lane < 64, nat4[x, 0:8], turn(nat4[x, 8:16], 64))

    def add(x, a, q):
        v3[1][x + 1, q] = v3[1][x + 1, q] + nat_f[x // 2]

    planes(0, 8, 4, add)
    ascend(L3, v3, wd3, fd3)
    place = 16 * gz - 8 + lane % 32
    z = jnp.clip(place, 0, 127)
    index = (z % 2) * 64 + z // 2
    for x in range(8):
        for q in (0, 1):
            even, odd = even_odd(v3, x, x, q)
            first = pick(jnp.where(lane < 64, even, turn(odd, 64)), index)
            second = pick(jnp.where(lane < 64, turn(even, 64), odd), index)
            nat3[x, pl.ds(q, 8, stride=2), :] = first
            nat3[x, pl.ds(16 + q, 8, stride=2), :] = second
        cells = nat3[x, 0:8]
        for j in (1, 2, 3):
            cells = jnp.where(lane // 32 == j, nat3[x, 8 * j : 8 * j + 8], cells)
        out_ref[x] = jnp.where(place == z, cells, 0.0)


def level2_up_kernel(scal, black_ref, wd0, wd1, fd0, fd1, add_ref, out_ref, v0, v1, nat):
    v, wd, fd = (v0, v1), (wd0, wd1), (fd0, fd1)
    gy = scal[1]
    correct(L2, v, black_ref, add_ref)
    ascend(L2, v, wd, fd)
    lane = lanes(8)
    k = lane % 64
    base = (gy + 1) // 2 - 1
    groups = [base, base + 1]

    def store(x, a, q):
        even, odd = even_odd(v, x, a, q)
        for i, mq in enumerate(groups):
            index = 32 * jnp.clip(mq, 0, 3) + k // 2
            cells = jnp.where(lane % 2 == 0, pick(even, index), pick(odd, index))
            nat[x, pl.ds(16 * i + q, 8, stride=2), :] = jnp.where((mq >= 0) & (mq < 4), cells, 0.0)

    planes(0, 16, 4, store)
    start = pl.multiple_of(8 - 8 * (gy % 2), 8)
    side = lanes(24) < 64
    for x in range(8):
        out_ref[x] = jnp.where(side, nat[x, pl.ds(start, 24), :], nat[8 + x, pl.ds(start, 24), :])


def level1_up_kernel(scal, black_ref, wd0, wd1, fd0, fd1, add_ref, out_ref, v0, v1, nat):
    v, wd, fd = (v0, v1), (wd0, wd1), (fd0, fd1)
    gx = scal[0]
    correct(L1, v, black_ref, add_ref)
    ascend(L1, v, wd, fd)
    lane = lanes(24)
    z = jnp.where(lane < 96, lane, lane - 128) + 32
    index = jnp.clip(z // 2, 0, 63)

    def store(i, carry):
        for u in range(4):
            x = 8 * gx - 4 + 4 * i + u
            inside = (x >= 0) & (x < 32)
            x = jnp.clip(x, 0, 31)
            there = 64 * (x // 16) + index
            for q in (0, 1):
                even, odd = even_odd(v, x % 16, u, q)
                cells = jnp.where(lane % 2 == 0, pick(even, there), pick(odd, there))
                nat[4 * i + u, pl.ds(q, 24, stride=2), :] = jnp.where(inside, cells, 0.0)
        return carry

    lax.fori_loop(0, 4, store, 0)
    for x in range(16):
        out_ref[x, 0:16] = nat[x, 16:32]
        out_ref[x, 16:20] = nat[x, 32:36]
        out_ref[x, 20:24] = nat[x, 12:16]


def level0_up_kernel(black_ref, wd0, wd1, fd0, fd1, add_ref, out_ref, v0, v1):
    v, wd, fd = (v0, v1), (wd0, wd1), (fd0, fd1)
    correct(L0, v, black_ref, add_ref)
    ascend(L0, v, wd, fd, [(4, 28), (6, 26), (6, 26), (8, 24)])
    lane = lanes(16)
    index = (lane % 2) * 64 + lane // 2

    def store(x, a, q):
        even, odd = even_odd(v, x, a, q)
        packed = jnp.where(lane < 64, even[0:16], turn(odd[0:16], 64))
        out_ref[x - 8, pl.ds(q, 16, stride=2), :] = pick(packed, index)

    planes(8, 24, 4, store)


def up_kernel(scal, own_ref, all_ref, *refs):
    set2, set1, set0 = refs[0:5], refs[5:10], refs[10:15]
    out_ref, add2, add1, add0, v0, v1, w0, w1, x0, x1, nat2, nat1, *rest = refs[15:]
    coarse_kernel(scal, own_ref, all_ref, add2, *rest)
    level2_up_kernel(scal, *set2, add2, add1, v0, v1, nat2)
    level1_up_kernel(scal, *set1, add1, add0, w0, w1, nat1)
    level0_up_kernel(*set0, add0, out_ref, x0, x1)


def arr(*shape):
    return jax.ShapeDtypeStruct(shape, F32)


def scratch(*shape):
    return pltpu.VMEM(shape, F32)


def level_scratch(level):
    shapes = [level.own()] * 2 + [level.wide()] * 4 + [level.own()]
    return [scratch(*s) for s in shapes]


def nat_scratch(level, count=None):
    return [scratch(count or level.count // 2, level.rows, 128)] * 2


def weights(level):
    return [(6,) + level.own()] * 2 + [level.own()] * 2


def call(kernel, outs, temps, *args, scal=None, limit=28):
    specs = [VMEM] * len(args)
    if scal is not None:
        specs = [SMEM] + specs
        args = (scal,) + args
    return pl.pallas_call(
        kernel,
        out_shape=outs,
        in_specs=specs,
        out_specs=jax.tree.map(lambda _: VMEM, outs),
        scratch_shapes=temps,
        compiler_params=pltpu.CompilerParams(vmem_limit_bytes=limit * 1024 * 1024),
    )(*args)


def ring(values, axis, step):
    count = lax.axis_size(axis)
    return lax.ppermute(values, axis, [(i, (i + step) % count) for i in range(count)])


def both_cores(values):
    count = lax.axis_size("gy")
    return lax.all_gather(values, "gy", axis=0, axis_index_groups=[[i, i + 1] for i in range(0, count, 2)])


def along_z(values, step):
    rows, count = lax.axis_size("gy"), lax.axis_size("gz")
    pairs = []
    for i in range(rows):
        for k in range(count):
            pairs.append((i * count + k, i * count + (k + (-step if i % 2 else step)) % count))
    return lax.ppermute(values, ("gy", "gz"), pairs)


def on_device(right_side, coefficient):
    scal = jnp.stack([lax.axis_index("gx"), lax.axis_index("gy"), lax.axis_index("gz")]).astype(jnp.int32)
    half = arr(16, 2, 16, 128)
    strip = arr(2, 2, 16, 128)
    lo, hi, zl, zr = call(split_kernel, [half, half, strip, strip], [], right_side, coefficient)
    from_left, from_right = ring(zr, "gz", 1), ring(zl, "gz", -1)
    mains = (ring(hi, "gx", 1), lo, hi, ring(lo, "gx", -1))
    low, high = [jnp.concatenate([from_left[i : i + 1], from_right[i : i + 1]]) for i in (0, 1)]
    strips = (ring(high, "gx", 1), low, high, ring(low, "gx", -1))
    yl, yr = call(edge_kernel, [arr(72, 8, 128)] * 2, [], *mains, *strips)
    from_left, from_right = ring(yr, "gy", 1), ring(yl, "gy", -1)
    own, zl, zr, black0, *set0 = call(
        level0_down_kernel,
        [arr(16, 2, 8, 128), arr(4, 2, 8, 128), arr(4, 2, 8, 128), arr(*L0.own())]
        + [arr(*s) for s in weights(L0)],
        level_scratch(L0) + nat_scratch(L0, 8),
        *mains, *strips, from_left, from_right, scal=scal,
    )
    from_left, from_right = ring(zr, "gz", 1), ring(zl, "gz", -1)
    bundle = call(widen_kernel, arr(16, 2, 8, 128), [], own, from_left, from_right)
    column = [bundle] + [ring(bundle, "gx", s) for s in (1, 2, 3)]
    yl, yr = call(strip_kernel, [arr(80, 8, 128)] * 2, [], *column)
    own, black1, *set1 = call(
        level1_down_kernel,
        [arr(16, 8, 128), arr(*L1.own())] + [arr(*s) for s in weights(L1)],
        level_scratch(L1) + nat_scratch(L1) + [scratch(4, 16, 2, 8, 128)],
        *column, ring(yr, "gy", 1), ring(yl, "gy", -1), scal=scal,
    )
    own = own[None]
    sheet = jnp.concatenate([own] + [ring(own, "gy", 2 * s) for s in (1, 2, 3)])
    sheet = both_cores(sheet)
    own, black2, *set2 = call(
        level2_down_kernel,
        [arr(8, 8, 128), arr(*L2.own())] + [arr(*s) for s in weights(L2)],
        level_scratch(L2) + nat_scratch(L2),
        sheet, scal=scal,
    )
    slabs = both_cores(jnp.stack([along_z(own, s) for s in (1, 2, 3, 4)]))
    return call(
        up_kernel, arr(16, 32, 128),
        [scratch(8, 8, 128), scratch(8, 24, 128), scratch(16, 24, 128)]
        + [scratch(*level.wide()) for level in (L2, L2, L1, L1, L0, L0)]
        + [scratch(16, 32, 128), scratch(16, 48, 128)]
        + level_scratch(L3) + [scratch(*s) for s in weights(L3)] + nat_scratch(L3)
        + [scratch(8, 8, 8, 128), scratch(4, 8, 16, 128), scratch(4, 16, 128), scratch(8, 32, 128)],
        own, slabs, black2, *set2, black1, *set1, black0, *set0, scal=scal,
    )


def solution(mesh):
    spec = P("gx", "gy", "gz")
    return jax.shard_map(on_device, mesh=mesh, in_specs=(spec, spec), out_specs=spec, check_vma=False)
```

```python
import functools

import jax
import jax.numpy as jnp
from jax import lax
from jax.experimental import pallas as pl
from jax.experimental.pallas import tpu as pltpu
from jax.sharding import PartitionSpec as P

SWEEPS = 2
ITERS = 20
F32 = jnp.float32
OFF = 1e-20
VMEM = pl.BlockSpec(memory_space=pltpu.VMEM)
SMEM = pl.BlockSpec(memory_space=pltpu.SMEM)


class Level:
    def __init__(self, count, rows, group, fold):
        self.count, self.rows, self.group, self.fold = count, rows, group, fold

    def wide(self):
        return (self.count + 2, 2, self.rows, 128)

    def own(self):
        return (self.count, 2, self.rows, 128)


L0 = Level(32, 24, 128, None)
L1 = Level(16, 24, 64, "x")
L2 = Level(16, 8, 32, "y")
L3 = Level(8, 8, 64, "y")


def lanes(rows):
    return lax.broadcasted_iota(jnp.int32, (rows, 128), 1)


def rows_of(rows):
    return lax.broadcasted_iota(jnp.int32, (rows, 128), 0)


def pick(values, index):
    return jnp.take_along_axis(values, index, axis=1, mode="promise_in_bounds")


def turn(values, shift):
    shift = shift % 128
    return pltpu.roll(values, shift, 1) if shift else values


def inverse_of(values):
    return pl.reciprocal(values, approx=True)


def up(level, values):
    rolled = pltpu.roll(values, level.rows - 1, 0)
    if level.fold == "y":
        rolled = jnp.where(rows_of(level.rows) == level.rows - 1, turn(rolled, -level.group), rolled)
    return rolled


def down(level, values):
    rolled = pltpu.roll(values, 1, 0)
    if level.fold == "y":
        rolled = jnp.where(rows_of(level.rows) == 0, turn(rolled, level.group), rolled)
    return rolled


def goes_back(colour, a, q):
    return (colour == 0) == ((a + q) % 2 == 0)


class Window:
    def __init__(self, ref, first):
        self.ref, self.first, self.kept = ref, first, {}

    def __call__(self, offset, q):
        if (offset, q) not in self.kept:
            self.kept[offset, q] = self.ref[self.first + offset, q]
        return self.kept[offset, q]


def beside(level, other, at, q, colour, a):
    mid = other(at + 1, q)
    across = other(at + 1, 1 - q)
    return [
        other(at + 2, q),
        other(at, q),
        across if q == 0 else up(level, across),
        down(level, across) if q == 0 else across,
        mid,
        turn(mid, 1 if goes_back(colour, a, q) else -1),
    ]


def planes(first, last, unroll, body, *refs):
    pairs = (last - first) // 2
    unroll = min(unroll, pairs)
    while pairs % unroll:
        unroll -= 1

    def step(i, carry):
        start = first + 2 * unroll * i
        windows = [Window(ref, start) for ref in refs]
        for at in range(2 * unroll):
            for q in (0, 1):
                if refs:
                    body(start + at, at, q, windows)
                else:
                    body(start + at, at % 2, q)
        return carry

    if pairs == unroll:
        step(0, 0)
    else:
        lax.fori_loop(0, pairs // unroll, step, 0)


def fill_ends(level, values, rest=0.0):
    lane = lanes(level.rows)
    for q in (0, 1):
        if level.fold == "x":
            values[0, q] = jnp.where(lane < 64, rest, turn(values[level.count, q], 64))
            values[level.count + 1, q] = jnp.where(lane < 64, turn(values[1, q], 64), rest)
        else:
            values[0, q] = jnp.full((level.rows, 128), rest, F32)
            values[level.count + 1, q] = jnp.full((level.rows, 128), rest, F32)


def set_up(level, cond, rec, wd, fd, dd):
    rows = level.rows
    row, lane = rows_of(rows), lanes(rows)
    for colour in (0, 1):
        fill_ends(level, rec[colour], OFF)

    def body(x, at, q, windows):
        a = at % 2
        for colour in (0, 1):
            own_rec = windows[colour](at + 1, q)
            near = beside(level, windows[1 - colour], at, q, colour, a)
            walls = {}
            if level.fold == "y":
                if q == 0:
                    walls[3] = (row == 0) & (lane < level.group)
                else:
                    walls[2] = (row == rows - 1) & (lane >= 128 - level.group)
            if level.group < 128:
                end = 0 if goes_back(colour, a, q) else level.group - 1
                walls[5] = lane % level.group == end
            total = None
            faces = []
            for i, value in enumerate(near):
                if i in walls:
                    value = jnp.where(walls[i], OFF, value)
                face = inverse_of(own_rec + value)
                faces.append(face)
                total = face if total is None else total + face
            inverse = jnp.where(own_rec > 1e-10, inverse_of(total), 0.0)
            for i, face in enumerate(faces):
                weight = face * inverse
                wd[colour][i, x, q] = jnp.where(walls[i], 0.0, weight) if i in walls else weight
            fd[colour][x, q] = fd[colour][x, q] * (0.5 * inverse)
            if colour == 0:
                dd[x, q] = total

    planes(0, level.count, 4 if level.rows == 8 else 1, body, *rec)


def relaxed(level, colour, x, at, q, window, wd, fd):
    near = beside(level, window, at, q, colour, at % 2)
    weight = wd[colour]
    one = fd[colour][x, q] + weight[0, x, q] * near[0]
    two = weight[4, x, q] * near[4] + weight[1, x, q] * near[1]
    one = one + weight[2, x, q] * near[2]
    two = two + weight[3, x, q] * near[3]
    return one + (two + weight[5, x, q] * near[5])


def half_sweep(level, colour, v, wd, fd, first=0, last=None):
    def body(x, at, q, windows):
        v[colour][x + 1, q] = relaxed(level, colour, x, at, q, windows[0], wd, fd)

    planes(first, level.count if last is None else last, 8 if level.rows == 8 else 4, body, v[1 - colour])
    if level.fold == "x":
        fill_ends(level, v[colour])


def first_half(level, v, fd):
    for colour in (0, 1):
        fill_ends(level, v[colour])

    def body(x, a, q):
        v[0][x + 1, q] = fd[0][x, q]

    planes(0, level.count, 4, body)
    if level.fold == "x":
        fill_ends(level, v[0])


def descend(level, v, wd, fd, dd, cond, out_f, out_b, ranges=None):
    ranges = ranges or [(0, level.count)] * 4
    first_half(level, v, fd)
    half_sweep(level, 1, v, wd, fd, *ranges[0])
    half_sweep(level, 0, v, wd, fd, *ranges[1])
    half_sweep(level, 1, v, wd, fd, *ranges[2])
    first, last = ranges[3]

    def body(i, carry):
        window = Window(v[1], first + 4 * i)
        for u in (0, 1):
            left = jnp.zeros((level.rows, 128), F32)
            mean = jnp.zeros((level.rows, 128), F32)
            for a in (0, 1):
                for q in (0, 1):
                    at = 2 * u + a
                    x = first + 4 * i + at
                    left = left + dd[x, q] * (relaxed(level, 0, x, at, q, window, wd, fd) - v[0][x + 1, q])
                    mean = mean + (cond[0][x, q] + cond[1][x, q])
            out_f[2 * i + u] = left
            out_b[2 * i + u] = 0.125 * mean
        return carry

    lax.fori_loop(0, (last - first) // 4, body, 0)


def ascend(level, v, wd, fd, ranges=None):
    ranges = ranges or [(0, level.count)] * 4
    for step in range(2 * SWEEPS):
        half_sweep(level, step % 2, v, wd, fd, *ranges[step])


def correct(level, v, black, add):
    for colour in (0, 1):
        fill_ends(level, v[colour])

    def body(x, a, q):
        v[1][x + 1, q] = black[x, q] + add[x // 2]

    planes(0, level.count, 4, body)
    if level.fold == "x":
        fill_ends(level, v[1])


def keep_black(level, v, black):
    def body(x, a, q):
        black[x, q] = v[1][x + 1, q]

    planes(0, level.count, 4, body)


def even_odd(v, x, a, q):
    red, black = v[0][x + 1, q], v[1][x + 1, q]
    return (red, black) if (a + q) % 2 == 0 else (black, red)


def exchange(blocks, width):
    group = lanes(8) // width
    step = len(blocks) // 2
    while step:
        swapped = list(blocks)
        for i in range(len(blocks)):
            if not i & step:
                a, b = blocks[i], blocks[i + step]
                low = group & step == 0
                swapped[i] = jnp.where(low, a, turn(b, width * step))
                swapped[i + step] = jnp.where(low, turn(a, -width * step), b)
        blocks = swapped
        step //= 2
    return blocks


def split_kernel(f_ref, b_ref, lo_ref, hi_ref, zl_ref, zr_ref):
    lane = lanes(16)
    whole = 2 * (lane % 64) + lane // 64
    slot = lane // 8
    within = lane % 8
    first = 2 * (within % 4) + within // 4
    last = 120 + first
    for half, out in enumerate((lo_ref, hi_ref)):
        for q in (0, 1):
            left = jnp.zeros((16, 128), F32)
            right = jnp.zeros((16, 128), F32)
            for x in range(8):
                for arr, ref in enumerate((f_ref, b_ref)):
                    cells = ref[8 * half + x, pl.ds(q, 16, stride=2), :]
                    out[8 * arr + x, q] = pick(cells, whole)
                    here = slot == 2 * x + arr
                    left = jnp.where(here, pick(cells, first), left)
                    right = jnp.where(here, pick(cells, last), right)
            zl_ref[half, q] = left
            zr_ref[half, q] = turn(right, 60)


def edge_kernel(*refs):
    mains, strips, lo_ref, hi_ref = refs[0:4], refs[4:8], refs[8], refs[9]
    low = rows_of(8) < 4
    for t in range(4):
        for i in range(18):
            ref, at = (mains[t], i) if i < 16 else (strips[t], i - 16)
            lo_ref[18 * t + i] = jnp.where(low, ref[at, 0, 0:8], pltpu.roll(ref[at, 1, 0:8], 4, 0))
            hi_ref[18 * t + i] = jnp.where(low, pltpu.roll(ref[at, 1, 8:16], 4, 0), ref[at, 0, 8:16])


def level0_down_kernel(
    scal, m0, m1, m2, m3, s0, s1, s2, s3, yl_ref, yr_ref,
    own_ref, zl_ref, zr_ref, black_ref, wd0, wd1, fd0, fd1,
    cond0, cond1, rec0, rec1, v0, v1, dd, nat_f, nat_b,
):
    cond, rec, v, wd, fd = (cond0, cond1), (rec0, rec1), (v0, v1), (wd0, wd1), (fd0, fd1)
    gx, gy, gz = scal[0], scal[1], scal[2]
    lane, row = lanes(24), rows_of(24)
    inside = (lane < 68) | (lane >= 124)
    inside = inside & ((gz > 0) | (lane < 124)) & ((gz < 7) | (lane < 64) | (lane >= 124))
    inside = inside & ((gy > 0) | (row < 20)) & ((gy < 7) | (row < 16) | (row >= 20))
    keep = jnp.where(inside, 1.0, 0.0)
    low = rows_of(8) < 4
    for t, (main_ref, strip_ref) in enumerate(((m0, s0), (m1, s1), (m2, s2), (m3, s3))):
        here = keep
        if t == 0:
            here = keep * jnp.where(gx > 0, 1.0, 0.0)
        if t == 3:
            here = keep * jnp.where(gx < 3, 1.0, 0.0)

        def wide(i, q):
            right, left = yr_ref[18 * t + i], yl_ref[18 * t + i]
            edge = jnp.where(low, right, left) if q == 0 else pltpu.roll(jnp.where(low, left, right), 4, 0)
            own = main_ref[i, q] if i < 16 else strip_ref[i - 16, q]
            return jnp.concatenate([own, edge], axis=0)

        ends = [(wide(16, q), wide(17, q)) for q in (0, 1)]
        for x in range(8):
            for q in (0, 1):
                from_left, from_right = ends[q]
                for arr in (0, 1):
                    s = 2 * x + arr
                    main = wide(8 * arr + x, q)
                    edge = jnp.where(lane // 8 == s, from_right, from_left)
                    even = jnp.where(lane < 64, main, turn(edge, 64 - 8 * s))
                    odd = jnp.where(lane < 64, turn(main, 64), turn(edge, 60 - 8 * s))
                    cells = (even, odd) if (x + q) % 2 == 0 else (odd, even)
                    for colour in (0, 1):
                        if arr == 0:
                            fd[colour][8 * t + x, q] = cells[colour]
                        else:
                            on_grid = cells[colour] * here
                            cond[colour][8 * t + x, q] = on_grid
                            rec[colour][8 * t + x + 1, q] = jnp.where(
                                here > 0.0, inverse_of(cells[colour]), OFF
                            )
    set_up(L0, cond, rec, wd, fd, dd)
    descend(L0, v, wd, fd, dd, cond, nat_f, nat_b, [(2, 30), (2, 30), (4, 28), (8, 24)])
    keep_black(L0, v, black_ref)
    lane8 = lanes(8)
    k = lane8 % 64
    spread = 2 * jnp.clip(k - 16, 0, 31) + lane8 // 64
    near = 2 * (lane8 % 16) + (lane8 // 16) % 2
    for x in range(0, 8, 2):
        for q in (0, 1):
            left, right = [], []
            for a in (0, 1):
                f = nat_f[x + a, pl.ds(q, 8, stride=2), :]
                b = nat_b[x + a, pl.ds(q, 8, stride=2), :]
                own_ref[x + a, q] = pick(f, spread)
                own_ref[8 + x + a, q] = pick(b, spread)
                here = lane8 % 64 < 32
                left.append(jnp.where(here, pick(f, near), pick(b, near)))
                right.append(jnp.where(here, pick(f, near + 32), pick(b, near + 32)))
            zl_ref[x // 2, q] = jnp.where(lane8 < 64, left[0], left[1])
            zr_ref[x // 2, q] = jnp.where(lane8 < 64, right[0], right[1])


def widen_kernel(own_ref, left_ref, right_ref, out_ref):
    lane = lanes(8)
    k = lane % 64
    index = lane % 16 + 16 * (lane // 64)
    for x in range(8):
        for q in (0, 1):
            for arr in (0, 1):
                there = index + 64 * (x % 2) + 32 * arr
                edge = jnp.where(k < 16, pick(left_ref[x // 2, q], there), pick(right_ref[x // 2, q], there))
                out_ref[8 * arr + x, q] = jnp.where((k >= 16) & (k < 48), own_ref[8 * arr + x, q], edge)


def strip_kernel(a_ref, b_ref, c_ref, d_ref, lo_ref, hi_ref):
    low = rows_of(8) < 4
    for t, ref in enumerate((a_ref, b_ref, c_ref, d_ref)):
        for i in range(16):
            zero, one = ref[i, 0], ref[i, 1]
            lo_ref[20 * t + i] = jnp.where(low, zero, pltpu.roll(one, 4, 0))
            hi_ref[20 * t + i] = jnp.where(low, pltpu.roll(zero, 4, 0), one)
            for q in (0, 1):
                row = 2 * (i % 4) + q
                lo_ref[20 * t + 16 + i // 4, row : row + 1] = ref[i, q, 4:5]
                hi_ref[20 * t + 16 + i // 4, row : row + 1] = ref[i, q, 3:4]


def level1_down_kernel(
    scal, a_ref, b_ref, c_ref, d_ref, yl_ref, yr_ref,
    out_ref, black_ref, wd0, wd1, fd0, fd1,
    cond0, cond1, rec0, rec1, v0, v1, dd, nat_f, nat_b, own,
):
    cond, rec, v, wd, fd = (cond0, cond1), (rec0, rec1), (v0, v1), (wd0, wd1), (fd0, fd1)
    gx, gy, gz = scal[0], scal[1], scal[2]
    lane = lanes(8)
    k = lane % 64
    inside = ((gz > 0) | (k >= 16)) & ((gz < 7) | (k < 48))
    keep = jnp.where(inside, 1.0, 0.0)
    row = rows_of(8)
    for i, ref in enumerate((a_ref, b_ref, c_ref, d_ref)):
        own[i] = ref[...]
    for block in range(3):
        here = keep
        if block == 0:
            here = jnp.where(row >= 3, keep, 0.0) * jnp.where(gy > 0, 1.0, 0.0)
        if block == 2:
            here = jnp.where(row < 5, keep, 0.0) * jnp.where(gy < 7, 1.0, 0.0)
        rows = pl.ds(8 * block, 8)

        def cells_of(slot, i, q):
            if block == 1:
                return own[slot, i, q]
            ref = yl_ref if block == 0 else yr_ref
            cells = ref[20 * slot + i]
            if (block == 0) == (q == 0):
                cells = pltpu.roll(cells, 4, 0)
            at = 2 * (i % 4) + q
            single = ref[20 * slot + 16 + i // 4, at : at + 1]
            return jnp.where(row == (3 if block == 0 else 4), single, cells)

        def body(j, carry):
            slots = [gx ^ j, gx ^ (j + 2)]
            for x in range(8):
                for q in (0, 1):
                    parts = []
                    for arr in (0, 8):
                        first, second = [cells_of(slot, arr + x, q) for slot in slots]
                        parts.append(jnp.where(lane < 64, first, turn(second, 64)))
                        parts.append(jnp.where(lane < 64, turn(first, 64), second))
                    for colour in (0, 1):
                        odd = (x + q + colour) % 2
                        fd[colour][8 * j + x, q, rows] = parts[odd]
                        cond[colour][8 * j + x, q, rows] = parts[2 + odd] * here
                        rec[colour][8 * j + x + 1, q, rows] = jnp.where(
                            here > 0.0, inverse_of(parts[2 + odd]), OFF
                        )
            return carry

        lax.fori_loop(0, 2, body, 0)
    set_up(L1, cond, rec, wd, fd, dd)
    descend(L1, v, wd, fd, dd, cond, nat_f, nat_b)
    keep_black(L1, v, black_ref)
    for h in (0, 1):
        index = 64 * h + 2 * (lane % 32) + (lane // 32) % 2
        for x in range(8):
            f = pick(nat_f[x, 8:16], index)
            b = pick(nat_b[x, 8:16], index)
            nat_f[x, 0:8] = jnp.where(lane < 64, f, b)
            for q in (0, 1):
                out_ref[8 * h + x, 4 * q : 4 * q + 4] = nat_f[x, pl.ds(q, 4, stride=2), :]


def level2_down_kernel(
    scal, in_ref,
    out_ref, black_ref, wd0, wd1, fd0, fd1,
    cond0, cond1, rec0, rec1, v0, v1, dd, nat_f, nat_b,
):
    cond, rec, v, wd, fd = (cond0, cond1), (rec0, rec1), (v0, v1), (wd0, wd1), (fd0, fd1)
    gy, gz = scal[1], scal[2]
    chip = gy // 2
    lane = lanes(8)
    k = lane % 32
    inside = ((gz > 0) | (k >= 8)) & ((gz < 7) | (k < 24))
    slots = [chip ^ j for j in range(4)]

    def body(x, a, q):
        mains = []
        for slot in slots:
            both = [in_ref[c, slot, x, 4 * q : 4 * q + 4] for c in (0, 1)]
            mains.append(jnp.concatenate(both, axis=0))
        parts = exchange(mains, 32)
        for colour in (0, 1):
            odd = (a + q + colour) % 2
            fd[colour][x, q] = parts[odd]
            cond[colour][x, q] = jnp.where(inside, parts[2 + odd], 0.0)
            rec[colour][x + 1, q] = jnp.where(inside, inverse_of(parts[2 + odd]), OFF)

    planes(0, 16, 4, body)
    set_up(L2, cond, rec, wd, fd, dd)
    descend(L2, v, wd, fd, dd, cond, nat_f, nat_b)
    keep_black(L2, v, black_ref)
    index = 32 * (lane // 32) + 8 + 2 * (lane % 8) + (lane // 8) % 2
    for x in range(8):
        packed = jnp.where(lane % 32 < 16, pick(nat_f[x], index), pick(nat_b[x], index))
        out_ref[x] = packed


def coarsest(f, b):
    lane, row = lanes(8), rows_of(8)
    x, k = lane // 32, lane % 32

    def near(values, colour, q):
        back = (x + q + colour) % 2 == 0
        across = values[1 - q]
        return [
            values[q],
            across,
            turn(values[q], -32),
            turn(values[q], 32),
            pltpu.roll(across, 1 if q == 0 else 7, 0),
            pick(values[q], (lane + jnp.where(back, 127, 1)) % 128),
        ]

    rec = [[inverse_of(cells) for cells in pair] for pair in b]
    weights, sources = [], []
    for colour in (0, 1):
        weights.append([])
        sources.append([])
        for q in (0, 1):
            back = (x + q + colour) % 2 == 0
            walls = [
                None, None, x == 3, x == 0, row == (0 if q == 0 else 7), k == jnp.where(back, 0, 31),
            ]
            faces, total = [], None
            for value, wall in zip(near(rec[1 - colour], colour, q), walls):
                if wall is not None:
                    value = jnp.where(wall, OFF, value)
                face = inverse_of(rec[colour][q] + value)
                total = face if total is None else total + face
                faces.append(face if wall is None else jnp.where(wall, 0.0, face))
            inverse = inverse_of(total)
            weights[-1].append([face * inverse for face in faces])
            sources[-1].append(f[colour][q] * (0.5 * inverse))

    def half(colour, other):
        made = []
        for q in (0, 1):
            total = sources[colour][q]
            for weight, value in zip(weights[colour][q], near(other, colour, q)):
                total = total + weight * value
            made.append(total)
        return made

    black = half(1, sources[0])

    def step(_, carry):
        return tuple(half(1, half(0, list(carry))))

    black = lax.fori_loop(0, ITERS - 2, step, tuple(black))
    red = half(0, list(black))
    return red, half(1, red)


def coarse_kernel(
    scal, own_ref, all_ref, out_ref,
    cond30, cond31, rec30, rec31, v30, v31, dd3, wd30, wd31, fd30, fd31, nat_f, nat_b,
    slabs, whole, nat4, nat3,
):
    cond3, rec3, v3, wd3, fd3 = (cond30, cond31), (rec30, rec31), (v30, v31), (wd30, wd31), (fd30, fd31)
    gz = scal[2]
    lane = lanes(8)
    slabs[gz] = own_ref[...]
    for j in range(4):
        slabs[(gz + 7 - j) % 8] = all_ref[0, j]
        slabs[(gz + 1 + j) % 8] = all_ref[1, j]

    for x in range(8):
        for c, cells in enumerate(exchange([slabs[r, x] for r in range(8)], 8)):
            whole[c % 4, x, 8 * (c // 4) : 8 * (c // 4) + 8] = cells

    def place3(x, a, q):
        for colour in (0, 1):
            odd = (a + q + colour) % 2
            fd3[colour][x, q] = whole[odd, x, pl.ds(q, 8, stride=2), :]
            cells = whole[2 + odd, x, pl.ds(q, 8, stride=2), :]
            cond3[colour][x, q] = cells
            rec3[colour][x + 1, q] = inverse_of(cells)

    planes(0, 8, 4, place3)
    set_up(L3, cond3, rec3, wd3, fd3, dd3)
    descend(L3, v3, wd3, fd3, dd3, cond3, nat_f, nat_b)
    f4 = [[None, None], [None, None]]
    b4 = [[None, None], [None, None]]
    for x in range(4):
        for arr, plane in enumerate((nat_f[x], nat_b[x])):
            for part in (0, 1):
                whole[arr, x, 8 * part : 8 * part + 8] = turn(plane, 64 * part)
        for made, arr in ((f4, 0), (b4, 1)):
            for q in (0, 1):
                cells = whole[arr, x, pl.ds(q, 8, stride=2), :]
                for colour in (0, 1):
                    mine = pick(cells, 2 * (lane % 32) + (x + q + colour) % 2)
                    before = made[colour][q]
                    made[colour][q] = mine if x == 0 else jnp.where(lane // 32 == x, mine, before)
    red, black = coarsest(f4, b4)
    for x in range(4):
        for q in (0, 1):
            even, odd = (red[q], black[q]) if (x + q) % 2 == 0 else (black[q], red[q])
            index = 32 * x + (lane % 64) // 2
            nat4[x, pl.ds(q, 8, stride=2), :] = jnp.where(lane % 2 == 0, pick(even, index), pick(odd, index))
    for x in range(4):
        nat_f[x] = jnp.where(lane < 64, nat4[x, 0:8], turn(nat4[x, 8:16], 64))

    def add(x, a, q):
        v3[1][x + 1, q] = v3[1][x + 1, q] + nat_f[x // 2]

    planes(0, 8, 4, add)
    ascend(L3, v3, wd3, fd3)
    place = 16 * gz - 8 + lane % 32
    z = jnp.clip(place, 0, 127)
    index = (z % 2) * 64 + z // 2
    for x in range(8):
        for q in (0, 1):
            even, odd = even_odd(v3, x, x, q)
            first = pick(jnp.where(lane < 64, even, turn(odd, 64)), index)
            second = pick(jnp.where(lane < 64, turn(even, 64), odd), index)
            nat3[x, pl.ds(q, 8, stride=2), :] = first
            nat3[x, pl.ds(16 + q, 8, stride=2), :] = second
        cells = nat3[x, 0:8]
        for j in (1, 2, 3):
            cells = jnp.where(lane // 32 == j, nat3[x, 8 * j : 8 * j + 8], cells)
        out_ref[x] = jnp.where(place == z, cells, 0.0)


def level2_up_kernel(scal, black_ref, wd0, wd1, fd0, fd1, add_ref, out_ref, v0, v1, nat):
    v, wd, fd = (v0, v1), (wd0, wd1), (fd0, fd1)
    gy = scal[1]
    correct(L2, v, black_ref, add_ref)
    ascend(L2, v, wd, fd)
    lane = lanes(8)
    k = lane % 64
    base = (gy + 1) // 2 - 1
    groups = [base, base + 1]

    def store(x, a, q):
        even, odd = even_odd(v, x, a, q)
        for i, mq in enumerate(groups):
            index = 32 * jnp.clip(mq, 0, 3) + k // 2
            cells = jnp.where(lane % 2 == 0, pick(even, index), pick(odd, index))
            nat[x, pl.ds(16 * i + q, 8, stride=2), :] = jnp.where((mq >= 0) & (mq < 4), cells, 0.0)

    planes(0, 16, 4, store)
    start = pl.multiple_of(8 - 8 * (gy % 2), 8)
    side = lanes(24) < 64
    for x in range(8):
        out_ref[x] = jnp.where(side, nat[x, pl.ds(start, 24), :], nat[8 + x, pl.ds(start, 24), :])


def level1_up_kernel(scal, black_ref, wd0, wd1, fd0, fd1, add_ref, out_ref, v0, v1, nat):
    v, wd, fd = (v0, v1), (wd0, wd1), (fd0, fd1)
    gx = scal[0]
    correct(L1, v, black_ref, add_ref)
    ascend(L1, v, wd, fd)
    lane = lanes(24)
    z = jnp.where(lane < 96, lane, lane - 128) + 32
    index = jnp.clip(z // 2, 0, 63)

    def store(i, carry):
        for u in range(4):
            x = 8 * gx - 4 + 4 * i + u
            inside = (x >= 0) & (x < 32)
            x = jnp.clip(x, 0, 31)
            there = 64 * (x // 16) + index
            for q in (0, 1):
                even, odd = even_odd(v, x % 16, u, q)
                cells = jnp.where(lane % 2 == 0, pick(even, there), pick(odd, there))
                nat[4 * i + u, pl.ds(q, 24, stride=2), :] = jnp.where(inside, cells, 0.0)
        return carry

    lax.fori_loop(0, 4, store, 0)
    for x in range(16):
        out_ref[x, 0:16] = nat[x, 16:32]
        out_ref[x, 16:20] = nat[x, 32:36]
        out_ref[x, 20:24] = nat[x, 12:16]


def level0_up_kernel(black_ref, wd0, wd1, fd0, fd1, add_ref, out_ref, v0, v1):
    v, wd, fd = (v0, v1), (wd0, wd1), (fd0, fd1)
    correct(L0, v, black_ref, add_ref)
    ascend(L0, v, wd, fd, [(4, 28), (6, 26), (6, 26), (8, 24)])
    lane = lanes(16)
    index = (lane % 2) * 64 + lane // 2

    def store(x, a, q):
        even, odd = even_odd(v, x, a, q)
        packed = jnp.where(lane < 64, even[0:16], turn(odd[0:16], 64))
        out_ref[x - 8, pl.ds(q, 16, stride=2), :] = pick(packed, index)

    planes(8, 24, 4, store)


def up_kernel(scal, own_ref, all_ref, *refs):
    set2, set1, set0 = refs[0:5], refs[5:10], refs[10:15]
    out_ref, add2, add1, add0, v0, v1, w0, w1, x0, x1, nat2, nat1, *rest = refs[15:]
    coarse_kernel(scal, own_ref, all_ref, add2, *rest)
    level2_up_kernel(scal, *set2, add2, add1, v0, v1, nat2)
    level1_up_kernel(scal, *set1, add1, add0, w0, w1, nat1)
    level0_up_kernel(*set0, add0, out_ref, x0, x1)


def arr(*shape):
    return jax.ShapeDtypeStruct(shape, F32)


def scratch(*shape):
    return pltpu.VMEM(shape, F32)


def level_scratch(level):
    shapes = [level.own()] * 2 + [level.wide()] * 4 + [level.own()]
    return [scratch(*s) for s in shapes]


def nat_scratch(level, count=None):
    return [scratch(count or level.count // 2, level.rows, 128)] * 2


def weights(level):
    return [(6,) + level.own()] * 2 + [level.own()] * 2


def call(kernel, outs, temps, *args, scal=None, limit=28):
    specs = [VMEM] * len(args)
    if scal is not None:
        specs = [SMEM] + specs
        args = (scal,) + args
    return pl.pallas_call(
        kernel,
        out_shape=outs,
        in_specs=specs,
        out_specs=jax.tree.map(lambda _: VMEM, outs),
        scratch_shapes=temps,
        compiler_params=pltpu.CompilerParams(vmem_limit_bytes=limit * 1024 * 1024),
    )(*args)


def ring(values, axis, step):
    count = lax.axis_size(axis)
    return lax.ppermute(values, axis, [(i, (i + step) % count) for i in range(count)])


def trade(values, axis, step):
    return lax.ppermute(values, axis, [(i, i ^ step) for i in range(lax.axis_size(axis))])


def both_cores(values):
    count = lax.axis_size("gy")
    return lax.all_gather(values, "gy", axis=0, axis_index_groups=[[i, i + 1] for i in range(0, count, 2)])


def along_z(values, step):
    rows, count = lax.axis_size("gy"), lax.axis_size("gz")
    pairs = []
    for i in range(rows):
        for k in range(count):
            pairs.append((i * count + k, i * count + (k + (-step if i % 2 else step)) % count))
    return lax.ppermute(values, ("gy", "gz"), pairs)


def on_device(right_side, coefficient):
    scal = jnp.stack([lax.axis_index("gx"), lax.axis_index("gy"), lax.axis_index("gz")]).astype(jnp.int32)
    half = arr(16, 2, 16, 128)
    strip = arr(2, 2, 16, 128)
    lo, hi, zl, zr = call(split_kernel, [half, half, strip, strip], [], right_side, coefficient)
    from_left, from_right = ring(zr, "gz", 1), ring(zl, "gz", -1)
    mains = (ring(hi, "gx", 1), lo, hi, ring(lo, "gx", -1))
    low, high = [jnp.concatenate([from_left[i : i + 1], from_right[i : i + 1]]) for i in (0, 1)]
    strips = (ring(high, "gx", 1), low, high, ring(low, "gx", -1))
    yl, yr = call(edge_kernel, [arr(72, 8, 128)] * 2, [], *mains, *strips)
    from_left, from_right = ring(yr, "gy", 1), ring(yl, "gy", -1)
    own, zl, zr, black0, *set0 = call(
        level0_down_kernel,
        [arr(16, 2, 8, 128), arr(4, 2, 8, 128), arr(4, 2, 8, 128), arr(*L0.own())]
        + [arr(*s) for s in weights(L0)],
        level_scratch(L0) + nat_scratch(L0, 8),
        *mains, *strips, from_left, from_right, scal=scal,
    )
    from_left, from_right = ring(zr, "gz", 1), ring(zl, "gz", -1)
    bundle = call(widen_kernel, arr(16, 2, 8, 128), [], own, from_left, from_right)
    column = [bundle] + [trade(bundle, "gx", s) for s in (1, 2, 3)]
    yl, yr = call(strip_kernel, [arr(80, 8, 128)] * 2, [], *column)
    own, black1, *set1 = call(
        level1_down_kernel,
        [arr(16, 8, 128), arr(*L1.own())] + [arr(*s) for s in weights(L1)],
        level_scratch(L1) + nat_scratch(L1) + [scratch(4, 16, 2, 8, 128)],
        *column, ring(yr, "gy", 1), ring(yl, "gy", -1), scal=scal,
    )
    own = own[None]
    sheet = jnp.concatenate([own] + [trade(own, "gy", 2 * s) for s in (1, 2, 3)])
    sheet = both_cores(sheet)
    own, black2, *set2 = call(
        level2_down_kernel,
        [arr(8, 8, 128), arr(*L2.own())] + [arr(*s) for s in weights(L2)],
        level_scratch(L2) + nat_scratch(L2),
        sheet, scal=scal,
    )
    slabs = both_cores(jnp.stack([along_z(own, s) for s in (1, 2, 3, 4)]))
    return call(
        up_kernel, arr(16, 32, 128),
        [scratch(8, 8, 128), scratch(8, 24, 128), scratch(16, 24, 128)]
        + [scratch(*level.wide()) for level in (L2, L2, L1, L1, L0, L0)]
        + [scratch(16, 32, 128), scratch(16, 48, 128)]
        + level_scratch(L3) + [scratch(*s) for s in weights(L3)] + nat_scratch(L3)
        + [scratch(8, 8, 8, 128), scratch(4, 8, 16, 128), scratch(4, 16, 128), scratch(8, 32, 128)],
        own, slabs, black2, *set2, black1, *set1, black0, *set0, scal=scal,
    )


def solution(mesh):
    spec = P("gx", "gy", "gz")
    return jax.shard_map(on_device, mesh=mesh, in_specs=(spec, spec), out_specs=spec, check_vma=False)
```

```python
import functools

import jax
import jax.numpy as jnp
from jax import lax
from jax.experimental import pallas as pl
from jax.experimental.pallas import tpu as pltpu
from jax.sharding import PartitionSpec as P

SWEEPS = 2
ITERS = 20
F32 = jnp.float32
OFF = 1e-20
VMEM = pl.BlockSpec(memory_space=pltpu.VMEM)
SMEM = pl.BlockSpec(memory_space=pltpu.SMEM)


class Level:
    def __init__(self, count, rows, group, fold):
        self.count, self.rows, self.group, self.fold = count, rows, group, fold

    def wide(self):
        return (self.count + 2, 2, self.rows, 128)

    def own(self):
        return (self.count, 2, self.rows, 128)


L0 = Level(32, 24, 128, None)
L1 = Level(16, 24, 64, "x")
L2 = Level(16, 8, 32, "y")
L3 = Level(8, 8, 64, "y")


def lanes(rows):
    return lax.broadcasted_iota(jnp.int32, (rows, 128), 1)


def rows_of(rows):
    return lax.broadcasted_iota(jnp.int32, (rows, 128), 0)


def pick(values, index):
    return jnp.take_along_axis(values, index, axis=1, mode="promise_in_bounds")


def turn(values, shift):
    shift = shift % 128
    return pltpu.roll(values, shift, 1) if shift else values


def inverse_of(values):
    return pl.reciprocal(values, approx=True)


def up(level, values):
    rolled = pltpu.roll(values, level.rows - 1, 0)
    if level.fold == "y":
        rolled = jnp.where(rows_of(level.rows) == level.rows - 1, turn(rolled, -level.group), rolled)
    return rolled


def down(level, values):
    rolled = pltpu.roll(values, 1, 0)
    if level.fold == "y":
        rolled = jnp.where(rows_of(level.rows) == 0, turn(rolled, level.group), rolled)
    return rolled


def goes_back(colour, a, q):
    return (colour == 0) == ((a + q) % 2 == 0)


class Window:
    def __init__(self, ref, first):
        self.ref, self.first, self.kept = ref, first, {}

    def __call__(self, offset, q):
        if (offset, q) not in self.kept:
            self.kept[offset, q] = self.ref[self.first + offset, q]
        return self.kept[offset, q]


def beside(level, other, at, q, colour, a):
    mid = other(at + 1, q)
    across = other(at + 1, 1 - q)
    return [
        other(at + 2, q),
        other(at, q),
        across if q == 0 else up(level, across),
        down(level, across) if q == 0 else across,
        mid,
        turn(mid, 1 if goes_back(colour, a, q) else -1),
    ]


def planes(first, last, unroll, body, *refs):
    pairs = (last - first) // 2
    unroll = min(unroll, pairs)
    while pairs % unroll:
        unroll -= 1

    def step(i, carry):
        start = first + 2 * unroll * i
        windows = [Window(ref, start) for ref in refs]
        for at in range(2 * unroll):
            for q in (0, 1):
                if refs:
                    body(start + at, at, q, windows)
                else:
                    body(start + at, at % 2, q)
        return carry

    if pairs == unroll:
        step(0, 0)
    else:
        lax.fori_loop(0, pairs // unroll, step, 0)


def fill_ends(level, values, rest=0.0):
    lane = lanes(level.rows)
    for q in (0, 1):
        if level.fold == "x":
            values[0, q] = jnp.where(lane < 64, rest, turn(values[level.count, q], 64))
            values[level.count + 1, q] = jnp.where(lane < 64, turn(values[1, q], 64), rest)
        else:
            values[0, q] = jnp.full((level.rows, 128), rest, F32)
            values[level.count + 1, q] = jnp.full((level.rows, 128), rest, F32)


def set_up(level, cond, rec, wd, fd, dd):
    rows = level.rows
    row, lane = rows_of(rows), lanes(rows)
    for colour in (0, 1):
        fill_ends(level, rec[colour], OFF)

    def body(x, at, q, windows):
        a = at % 2
        for colour in (0, 1):
            own_rec = windows[colour](at + 1, q)
            near = beside(level, windows[1 - colour], at, q, colour, a)
            walls = {}
            if level.fold == "y":
                if q == 0:
                    walls[3] = (row == 0) & (lane < level.group)
                else:
                    walls[2] = (row == rows - 1) & (lane >= 128 - level.group)
            if level.group < 128:
                end = 0 if goes_back(colour, a, q) else level.group - 1
                walls[5] = lane % level.group == end
            total = None
            faces = []
            for i, value in enumerate(near):
                if i in walls:
                    value = jnp.where(walls[i], OFF, value)
                face = inverse_of(own_rec + value)
                faces.append(face)
                total = face if total is None else total + face
            inverse = jnp.where(own_rec > 1e-10, inverse_of(total), 0.0)
            for i, face in enumerate(faces):
                weight = face * inverse
                wd[colour][i, x, q] = jnp.where(walls[i], 0.0, weight) if i in walls else weight
            fd[colour][x, q] = fd[colour][x, q] * (0.5 * inverse)
            if colour == 0:
                dd[x, q] = total

    planes(0, level.count, 4 if level.rows == 8 else 2, body, *rec)


def relaxed(level, colour, x, at, q, window, wd, fd):
    near = beside(level, window, at, q, colour, at % 2)
    weight = wd[colour]
    one = fd[colour][x, q] + weight[0, x, q] * near[0]
    two = weight[4, x, q] * near[4] + weight[1, x, q] * near[1]
    one = one + weight[2, x, q] * near[2]
    two = two + weight[3, x, q] * near[3]
    return one + (two + weight[5, x, q] * near[5])


def half_sweep(level, colour, v, wd, fd, first=0, last=None):
    def body(x, at, q, windows):
        v[colour][x + 1, q] = relaxed(level, colour, x, at, q, windows[0], wd, fd)

    planes(first, level.count if last is None else last, 8 if level.rows == 8 else 7, body, v[1 - colour])
    if level.fold == "x":
        fill_ends(level, v[colour])


def first_half(level, v, fd):
    for colour in (0, 1):
        fill_ends(level, v[colour])

    def body(x, a, q):
        v[0][x + 1, q] = fd[0][x, q]

    planes(0, level.count, 4, body)
    if level.fold == "x":
        fill_ends(level, v[0])


def descend(level, v, wd, fd, dd, cond, out_f, out_b, ranges=None):
    ranges = ranges or [(0, level.count)] * 4
    first_half(level, v, fd)
    half_sweep(level, 1, v, wd, fd, *ranges[0])
    half_sweep(level, 0, v, wd, fd, *ranges[1])
    half_sweep(level, 1, v, wd, fd, *ranges[2])
    first, last = ranges[3]

    def body(i, carry):
        window = Window(v[1], first + 4 * i)
        for u in (0, 1):
            left = jnp.zeros((level.rows, 128), F32)
            mean = jnp.zeros((level.rows, 128), F32)
            for a in (0, 1):
                for q in (0, 1):
                    at = 2 * u + a
                    x = first + 4 * i + at
                    left = left + dd[x, q] * (relaxed(level, 0, x, at, q, window, wd, fd) - v[0][x + 1, q])
                    mean = mean + (cond[0][x, q] + cond[1][x, q])
            out_f[2 * i + u] = left
            out_b[2 * i + u] = 0.125 * mean
        return carry

    lax.fori_loop(0, (last - first) // 4, body, 0)


def ascend(level, v, wd, fd, ranges=None):
    ranges = ranges or [(0, level.count)] * 4
    for step in range(2 * SWEEPS):
        half_sweep(level, step % 2, v, wd, fd, *ranges[step])


def correct(level, v, black, add):
    for colour in (0, 1):
        fill_ends(level, v[colour])

    def body(x, a, q):
        v[1][x + 1, q] = black[x, q] + add[x // 2]

    planes(0, level.count, 4, body)
    if level.fold == "x":
        fill_ends(level, v[1])


def keep_black(level, v, black):
    def body(x, a, q):
        black[x, q] = v[1][x + 1, q]

    planes(0, level.count, 4, body)


def even_odd(v, x, a, q):
    red, black = v[0][x + 1, q], v[1][x + 1, q]
    return (red, black) if (a + q) % 2 == 0 else (black, red)


def exchange(blocks, width):
    group = lanes(8) // width
    step = len(blocks) // 2
    while step:
        swapped = list(blocks)
        for i in range(len(blocks)):
            if not i & step:
                a, b = blocks[i], blocks[i + step]
                low = group & step == 0
                swapped[i] = jnp.where(low, a, turn(b, width * step))
                swapped[i + step] = jnp.where(low, turn(a, -width * step), b)
        blocks = swapped
        step //= 2
    return blocks


def split_kernel(f_ref, b_ref, lo_ref, hi_ref, zl_ref, zr_ref):
    lane = lanes(16)
    whole = 2 * (lane % 64) + lane // 64
    slot = lane // 8
    within = lane % 8
    first = 2 * (within % 4) + within // 4
    last = 120 + first
    for half, out in enumerate((lo_ref, hi_ref)):
        for q in (0, 1):
            left = jnp.zeros((16, 128), F32)
            right = jnp.zeros((16, 128), F32)
            for x in range(8):
                for arr, ref in enumerate((f_ref, b_ref)):
                    cells = ref[8 * half + x, pl.ds(q, 16, stride=2), :]
                    out[8 * arr + x, q] = pick(cells, whole)
                    here = slot == 2 * x + arr
                    left = jnp.where(here, pick(cells, first), left)
                    right = jnp.where(here, pick(cells, last), right)
            zl_ref[half, q] = left
            zr_ref[half, q] = turn(right, 60)


def edge_kernel(*refs):
    mains, strips, lo_ref, hi_ref = refs[0:4], refs[4:8], refs[8], refs[9]
    low = rows_of(8) < 4
    for t in range(4):
        for i in range(18):
            ref, at = (mains[t], i) if i < 16 else (strips[t], i - 16)
            lo_ref[18 * t + i] = jnp.where(low, ref[at, 0, 0:8], pltpu.roll(ref[at, 1, 0:8], 4, 0))
            hi_ref[18 * t + i] = jnp.where(low, pltpu.roll(ref[at, 1, 8:16], 4, 0), ref[at, 0, 8:16])


def level0_down_kernel(
    scal, m0, m1, m2, m3, s0, s1, s2, s3, yl_ref, yr_ref,
    own_ref, zl_ref, zr_ref, black_ref, wd0, wd1, fd0, fd1,
    cond0, cond1, rec0, rec1, v0, v1, dd, nat_f, nat_b,
):
    cond, rec, v, wd, fd = (cond0, cond1), (rec0, rec1), (v0, v1), (wd0, wd1), (fd0, fd1)
    gx, gy, gz = scal[0], scal[1], scal[2]
    lane, row = lanes(24), rows_of(24)
    inside = (lane < 68) | (lane >= 124)
    inside = inside & ((gz > 0) | (lane < 124)) & ((gz < 7) | (lane < 64) | (lane >= 124))
    inside = inside & ((gy > 0) | (row < 20)) & ((gy < 7) | (row < 16) | (row >= 20))
    keep = jnp.where(inside, 1.0, 0.0)
    low = rows_of(8) < 4
    for t, (main_ref, strip_ref) in enumerate(((m0, s0), (m1, s1), (m2, s2), (m3, s3))):
        here = keep
        if t == 0:
            here = keep * jnp.where(gx > 0, 1.0, 0.0)
        if t == 3:
            here = keep * jnp.where(gx < 3, 1.0, 0.0)

        def wide(i, q):
            right, left = yr_ref[18 * t + i], yl_ref[18 * t + i]
            edge = jnp.where(low, right, left) if q == 0 else pltpu.roll(jnp.where(low, left, right), 4, 0)
            own = main_ref[i, q] if i < 16 else strip_ref[i - 16, q]
            return jnp.concatenate([own, edge], axis=0)

        ends = [(wide(16, q), wide(17, q)) for q in (0, 1)]
        for x in range(8):
            for q in (0, 1):
                from_left, from_right = ends[q]
                for arr in (0, 1):
                    s = 2 * x + arr
                    main = wide(8 * arr + x, q)
                    edge = jnp.where(lane // 8 == s, from_right, from_left)
                    even = jnp.where(lane < 64, main, turn(edge, 64 - 8 * s))
                    odd = jnp.where(lane < 64, turn(main, 64), turn(edge, 60 - 8 * s))
                    cells = (even, odd) if (x + q) % 2 == 0 else (odd, even)
                    for colour in (0, 1):
                        if arr == 0:
                            fd[colour][8 * t + x, q] = cells[colour]
                        else:
                            on_grid = cells[colour] * here
                            cond[colour][8 * t + x, q] = on_grid
                            rec[colour][8 * t + x + 1, q] = jnp.where(
                                here > 0.0, inverse_of(cells[colour]), OFF
                            )
    set_up(L0, cond, rec, wd, fd, dd)
    descend(L0, v, wd, fd, dd, cond, nat_f, nat_b, [(2, 30), (2, 30), (4, 28), (8, 24)])
    keep_black(L0, v, black_ref)
    lane8 = lanes(8)
    k = lane8 % 64
    spread = 2 * jnp.clip(k - 16, 0, 31) + lane8 // 64
    near = 2 * (lane8 % 16) + (lane8 // 16) % 2
    for x in range(0, 8, 2):
        for q in (0, 1):
            left, right = [], []
            for a in (0, 1):
                f = nat_f[x + a, pl.ds(q, 8, stride=2), :]
                b = nat_b[x + a, pl.ds(q, 8, stride=2), :]
                own_ref[x + a, q] = pick(f, spread)
                own_ref[8 + x + a, q] = pick(b, spread)
                here = lane8 % 64 < 32
                left.append(jnp.where(here, pick(f, near), pick(b, near)))
                right.append(jnp.where(here, pick(f, near + 32), pick(b, near + 32)))
            zl_ref[x // 2, q] = jnp.where(lane8 < 64, left[0], left[1])
            zr_ref[x // 2, q] = jnp.where(lane8 < 64, right[0], right[1])


def widen_kernel(own_ref, left_ref, right_ref, out_ref):
    lane = lanes(8)
    k = lane % 64
    index = lane % 16 + 16 * (lane // 64)
    for x in range(8):
        for q in (0, 1):
            for arr in (0, 1):
                there = index + 64 * (x % 2) + 32 * arr
                edge = jnp.where(k < 16, pick(left_ref[x // 2, q], there), pick(right_ref[x // 2, q], there))
                out_ref[8 * arr + x, q] = jnp.where((k >= 16) & (k < 48), own_ref[8 * arr + x, q], edge)


def strip_kernel(a_ref, b_ref, c_ref, d_ref, lo_ref, hi_ref):
    low = rows_of(8) < 4
    for t, ref in enumerate((a_ref, b_ref, c_ref, d_ref)):
        for i in range(16):
            zero, one = ref[i, 0], ref[i, 1]
            lo_ref[20 * t + i] = jnp.where(low, zero, pltpu.roll(one, 4, 0))
            hi_ref[20 * t + i] = jnp.where(low, pltpu.roll(zero, 4, 0), one)
            for q in (0, 1):
                row = 2 * (i % 4) + q
                lo_ref[20 * t + 16 + i // 4, row : row + 1] = ref[i, q, 4:5]
                hi_ref[20 * t + 16 + i // 4, row : row + 1] = ref[i, q, 3:4]


def level1_down_kernel(
    scal, a_ref, b_ref, c_ref, d_ref, yl_ref, yr_ref,
    out_ref, black_ref, wd0, wd1, fd0, fd1,
    cond0, cond1, rec0, rec1, v0, v1, dd, nat_f, nat_b, own,
):
    cond, rec, v, wd, fd = (cond0, cond1), (rec0, rec1), (v0, v1), (wd0, wd1), (fd0, fd1)
    gx, gy, gz = scal[0], scal[1], scal[2]
    lane = lanes(8)
    k = lane % 64
    inside = ((gz > 0) | (k >= 16)) & ((gz < 7) | (k < 48))
    keep = jnp.where(inside, 1.0, 0.0)
    row = rows_of(8)
    for i, ref in enumerate((a_ref, b_ref, c_ref, d_ref)):
        own[i] = ref[...]
    for block in range(3):
        here = keep
        if block == 0:
            here = jnp.where(row >= 3, keep, 0.0) * jnp.where(gy > 0, 1.0, 0.0)
        if block == 2:
            here = jnp.where(row < 5, keep, 0.0) * jnp.where(gy < 7, 1.0, 0.0)
        rows = pl.ds(8 * block, 8)

        def cells_of(slot, i, q):
            if block == 1:
                return own[slot, i, q]
            ref = yl_ref if block == 0 else yr_ref
            cells = ref[20 * slot + i]
            if (block == 0) == (q == 0):
                cells = pltpu.roll(cells, 4, 0)
            at = 2 * (i % 4) + q
            single = ref[20 * slot + 16 + i // 4, at : at + 1]
            return jnp.where(row == (3 if block == 0 else 4), single, cells)

        def body(j, carry):
            slots = [gx ^ j, gx ^ (j + 2)]
            for x in range(8):
                for q in (0, 1):
                    parts = []
                    for arr in (0, 8):
                        first, second = [cells_of(slot, arr + x, q) for slot in slots]
                        parts.append(jnp.where(lane < 64, first, turn(second, 64)))
                        parts.append(jnp.where(lane < 64, turn(first, 64), second))
                    for colour in (0, 1):
                        odd = (x + q + colour) % 2
                        fd[colour][8 * j + x, q, rows] = parts[odd]
                        cond[colour][8 * j + x, q, rows] = parts[2 + odd] * here
                        rec[colour][8 * j + x + 1, q, rows] = jnp.where(
                            here > 0.0, inverse_of(parts[2 + odd]), OFF
                        )
            return carry

        lax.fori_loop(0, 2, body, 0)
    set_up(L1, cond, rec, wd, fd, dd)
    descend(L1, v, wd, fd, dd, cond, nat_f, nat_b)
    keep_black(L1, v, black_ref)
    for h in (0, 1):
        index = 64 * h + 2 * (lane % 32) + (lane // 32) % 2
        for x in range(8):
            f = pick(nat_f[x, 8:16], index)
            b = pick(nat_b[x, 8:16], index)
            nat_f[x, 0:8] = jnp.where(lane < 64, f, b)
            for q in (0, 1):
                out_ref[8 * h + x, 4 * q : 4 * q + 4] = nat_f[x, pl.ds(q, 4, stride=2), :]


def level2_down_kernel(
    scal, in_ref,
    out_ref, black_ref, wd0, wd1, fd0, fd1,
    cond0, cond1, rec0, rec1, v0, v1, dd, nat_f, nat_b,
):
    cond, rec, v, wd, fd = (cond0, cond1), (rec0, rec1), (v0, v1), (wd0, wd1), (fd0, fd1)
    gy, gz = scal[1], scal[2]
    chip = gy // 2
    lane = lanes(8)
    k = lane % 32
    inside = ((gz > 0) | (k >= 8)) & ((gz < 7) | (k < 24))
    slots = [chip ^ j for j in range(4)]

    def body(x, a, q):
        mains = []
        for slot in slots:
            both = [in_ref[c, slot, x, 4 * q : 4 * q + 4] for c in (0, 1)]
            mains.append(jnp.concatenate(both, axis=0))
        parts = exchange(mains, 32)
        for colour in (0, 1):
            odd = (a + q + colour) % 2
            fd[colour][x, q] = parts[odd]
            cond[colour][x, q] = jnp.where(inside, parts[2 + odd], 0.0)
            rec[colour][x + 1, q] = jnp.where(inside, inverse_of(parts[2 + odd]), OFF)

    planes(0, 16, 4, body)
    set_up(L2, cond, rec, wd, fd, dd)
    descend(L2, v, wd, fd, dd, cond, nat_f, nat_b)
    keep_black(L2, v, black_ref)
    index = 32 * (lane // 32) + 8 + 2 * (lane % 8) + (lane // 8) % 2
    for x in range(8):
        packed = jnp.where(lane % 32 < 16, pick(nat_f[x], index), pick(nat_b[x], index))
        out_ref[x] = packed


def coarsest(f, b):
    lane, row = lanes(8), rows_of(8)
    x, k = lane // 32, lane % 32

    def near(values, colour, q):
        back = (x + q + colour) % 2 == 0
        across = values[1 - q]
        return [
            values[q],
            across,
            turn(values[q], -32),
            turn(values[q], 32),
            pltpu.roll(across, 1 if q == 0 else 7, 0),
            pick(values[q], (lane + jnp.where(back, 127, 1)) % 128),
        ]

    rec = [[inverse_of(cells) for cells in pair] for pair in b]
    weights, sources = [], []
    for colour in (0, 1):
        weights.append([])
        sources.append([])
        for q in (0, 1):
            back = (x + q + colour) % 2 == 0
            walls = [
                None, None, x == 3, x == 0, row == (0 if q == 0 else 7), k == jnp.where(back, 0, 31),
            ]
            faces, total = [], None
            for value, wall in zip(near(rec[1 - colour], colour, q), walls):
                if wall is not None:
                    value = jnp.where(wall, OFF, value)
                face = inverse_of(rec[colour][q] + value)
                total = face if total is None else total + face
                faces.append(face if wall is None else jnp.where(wall, 0.0, face))
            inverse = inverse_of(total)
            weights[-1].append([face * inverse for face in faces])
            sources[-1].append(f[colour][q] * (0.5 * inverse))

    def half(colour, other):
        made = []
        for q in (0, 1):
            total = sources[colour][q]
            for weight, value in zip(weights[colour][q], near(other, colour, q)):
                total = total + weight * value
            made.append(total)
        return made

    black = half(1, sources[0])

    def step(_, carry):
        return tuple(half(1, half(0, list(carry))))

    black = lax.fori_loop(0, ITERS - 2, step, tuple(black))
    red = half(0, list(black))
    return red, half(1, red)


def coarse_kernel(
    scal, own_ref, all_ref, out_ref,
    cond30, cond31, rec30, rec31, v30, v31, dd3, wd30, wd31, fd30, fd31, nat_f, nat_b,
    slabs, whole, nat4, nat3,
):
    cond3, rec3, v3, wd3, fd3 = (cond30, cond31), (rec30, rec31), (v30, v31), (wd30, wd31), (fd30, fd31)
    gz = scal[2]
    lane = lanes(8)
    slabs[gz] = own_ref[...]
    for j in range(4):
        slabs[(gz + 7 - j) % 8] = all_ref[0, j]
        slabs[(gz + 1 + j) % 8] = all_ref[1, j]

    for x in range(8):
        for c, cells in enumerate(exchange([slabs[r, x] for r in range(8)], 8)):
            whole[c % 4, x, 8 * (c // 4) : 8 * (c // 4) + 8] = cells

    def place3(x, a, q):
        for colour in (0, 1):
            odd = (a + q + colour) % 2
            fd3[colour][x, q] = whole[odd, x, pl.ds(q, 8, stride=2), :]
            cells = whole[2 + odd, x, pl.ds(q, 8, stride=2), :]
            cond3[colour][x, q] = cells
            rec3[colour][x + 1, q] = inverse_of(cells)

    planes(0, 8, 4, place3)
    set_up(L3, cond3, rec3, wd3, fd3, dd3)
    descend(L3, v3, wd3, fd3, dd3, cond3, nat_f, nat_b)
    f4 = [[None, None], [None, None]]
    b4 = [[None, None], [None, None]]
    for x in range(4):
        for arr, plane in enumerate((nat_f[x], nat_b[x])):
            for part in (0, 1):
                whole[arr, x, 8 * part : 8 * part + 8] = turn(plane, 64 * part)
        for made, arr in ((f4, 0), (b4, 1)):
            for q in (0, 1):
                cells = whole[arr, x, pl.ds(q, 8, stride=2), :]
                for colour in (0, 1):
                    mine = pick(cells, 2 * (lane % 32) + (x + q + colour) % 2)
                    before = made[colour][q]
                    made[colour][q] = mine if x == 0 else jnp.where(lane // 32 == x, mine, before)
    red, black = coarsest(f4, b4)
    for x in range(4):
        for q in (0, 1):
            even, odd = (red[q], black[q]) if (x + q) % 2 == 0 else (black[q], red[q])
            index = 32 * x + (lane % 64) // 2
            nat4[x, pl.ds(q, 8, stride=2), :] = jnp.where(lane % 2 == 0, pick(even, index), pick(odd, index))
    for x in range(4):
        nat_f[x] = jnp.where(lane < 64, nat4[x, 0:8], turn(nat4[x, 8:16], 64))

    def add(x, a, q):
        v3[1][x + 1, q] = v3[1][x + 1, q] + nat_f[x // 2]

    planes(0, 8, 4, add)
    ascend(L3, v3, wd3, fd3)
    place = 16 * gz - 8 + lane % 32
    z = jnp.clip(place, 0, 127)
    index = (z % 2) * 64 + z // 2
    for x in range(8):
        for q in (0, 1):
            even, odd = even_odd(v3, x, x, q)
            first = pick(jnp.where(lane < 64, even, turn(odd, 64)), index)
            second = pick(jnp.where(lane < 64, turn(even, 64), odd), index)
            nat3[x, pl.ds(q, 8, stride=2), :] = first
            nat3[x, pl.ds(16 + q, 8, stride=2), :] = second
        cells = nat3[x, 0:8]
        for j in (1, 2, 3):
            cells = jnp.where(lane // 32 == j, nat3[x, 8 * j : 8 * j + 8], cells)
        out_ref[x] = jnp.where(place == z, cells, 0.0)


def level2_up_kernel(scal, black_ref, wd0, wd1, fd0, fd1, add_ref, out_ref, v0, v1, nat):
    v, wd, fd = (v0, v1), (wd0, wd1), (fd0, fd1)
    gy = scal[1]
    correct(L2, v, black_ref, add_ref)
    ascend(L2, v, wd, fd)
    lane = lanes(8)
    k = lane % 64
    base = (gy + 1) // 2 - 1
    groups = [base, base + 1]

    def store(x, a, q):
        even, odd = even_odd(v, x, a, q)
        for i, mq in enumerate(groups):
            index = 32 * jnp.clip(mq, 0, 3) + k // 2
            cells = jnp.where(lane % 2 == 0, pick(even, index), pick(odd, index))
            nat[x, pl.ds(16 * i + q, 8, stride=2), :] = jnp.where((mq >= 0) & (mq < 4), cells, 0.0)

    planes(0, 16, 4, store)
    start = pl.multiple_of(8 - 8 * (gy % 2), 8)
    side = lanes(24) < 64
    for x in range(8):
        out_ref[x] = jnp.where(side, nat[x, pl.ds(start, 24), :], nat[8 + x, pl.ds(start, 24), :])


def level1_up_kernel(scal, black_ref, wd0, wd1, fd0, fd1, add_ref, out_ref, v0, v1, nat):
    v, wd, fd = (v0, v1), (wd0, wd1), (fd0, fd1)
    gx = scal[0]
    correct(L1, v, black_ref, add_ref)
    ascend(L1, v, wd, fd)
    lane = lanes(24)
    z = jnp.where(lane < 96, lane, lane - 128) + 32
    index = jnp.clip(z // 2, 0, 63)

    def store(i, carry):
        for u in range(4):
            x = 8 * gx - 4 + 4 * i + u
            inside = (x >= 0) & (x < 32)
            x = jnp.clip(x, 0, 31)
            there = 64 * (x // 16) + index
            for q in (0, 1):
                even, odd = even_odd(v, x % 16, u, q)
                cells = jnp.where(lane % 2 == 0, pick(even, there), pick(odd, there))
                nat[4 * i + u, pl.ds(q, 24, stride=2), :] = jnp.where(inside, cells, 0.0)
        return carry

    lax.fori_loop(0, 4, store, 0)
    for x in range(16):
        out_ref[x, 0:16] = nat[x, 16:32]
        out_ref[x, 16:20] = nat[x, 32:36]
        out_ref[x, 20:24] = nat[x, 12:16]


def level0_up_kernel(black_ref, wd0, wd1, fd0, fd1, add_ref, out_ref, v0, v1):
    v, wd, fd = (v0, v1), (wd0, wd1), (fd0, fd1)
    correct(L0, v, black_ref, add_ref)
    ascend(L0, v, wd, fd, [(4, 28), (6, 26), (6, 26), (8, 24)])
    lane = lanes(16)
    index = (lane % 2) * 64 + lane // 2

    def store(x, a, q):
        even, odd = even_odd(v, x, a, q)
        packed = jnp.where(lane < 64, even[0:16], turn(odd[0:16], 64))
        out_ref[x - 8, pl.ds(q, 16, stride=2), :] = pick(packed, index)

    planes(8, 24, 4, store)


def up_kernel(scal, own_ref, all_ref, *refs):
    set2, set1, set0 = refs[0:5], refs[5:10], refs[10:15]
    out_ref, add2, add1, add0, v0, v1, w0, w1, x0, x1, nat2, nat1, *rest = refs[15:]
    coarse_kernel(scal, own_ref, all_ref, add2, *rest)
    level2_up_kernel(scal, *set2, add2, add1, v0, v1, nat2)
    level1_up_kernel(scal, *set1, add1, add0, w0, w1, nat1)
    level0_up_kernel(*set0, add0, out_ref, x0, x1)


def arr(*shape):
    return jax.ShapeDtypeStruct(shape, F32)


def scratch(*shape):
    return pltpu.VMEM(shape, F32)


def level_scratch(level):
    shapes = [level.own()] * 2 + [level.wide()] * 4 + [level.own()]
    return [scratch(*s) for s in shapes]


def nat_scratch(level, count=None):
    return [scratch(count or level.count // 2, level.rows, 128)] * 2


def weights(level):
    return [(6,) + level.own()] * 2 + [level.own()] * 2


def call(kernel, outs, temps, *args, scal=None, limit=28):
    specs = [VMEM] * len(args)
    if scal is not None:
        specs = [SMEM] + specs
        args = (scal,) + args
    return pl.pallas_call(
        kernel,
        out_shape=outs,
        in_specs=specs,
        out_specs=jax.tree.map(lambda _: VMEM, outs),
        scratch_shapes=temps,
        compiler_params=pltpu.CompilerParams(vmem_limit_bytes=limit * 1024 * 1024),
    )(*args)


def ring(values, axis, step):
    count = lax.axis_size(axis)
    return lax.ppermute(values, axis, [(i, (i + step) % count) for i in range(count)])


def trade(values, axis, step):
    return lax.ppermute(values, axis, [(i, i ^ step) for i in range(lax.axis_size(axis))])


def both_cores(values):
    count = lax.axis_size("gy")
    return lax.all_gather(values, "gy", axis=0, axis_index_groups=[[i, i + 1] for i in range(0, count, 2)])


def along_z(values, step):
    rows, count = lax.axis_size("gy"), lax.axis_size("gz")
    pairs = []
    for i in range(rows):
        for k in range(count):
            pairs.append((i * count + k, i * count + (k + (-step if i % 2 else step)) % count))
    return lax.ppermute(values, ("gy", "gz"), pairs)


def on_device(right_side, coefficient):
    scal = jnp.stack([lax.axis_index("gx"), lax.axis_index("gy"), lax.axis_index("gz")]).astype(jnp.int32)
    half = arr(16, 2, 16, 128)
    strip = arr(2, 2, 16, 128)
    lo, hi, zl, zr = call(split_kernel, [half, half, strip, strip], [], right_side, coefficient)
    from_left, from_right = ring(zr, "gz", 1), ring(zl, "gz", -1)
    mains = (ring(hi, "gx", 1), lo, hi, ring(lo, "gx", -1))
    low, high = [jnp.concatenate([from_left[i : i + 1], from_right[i : i + 1]]) for i in (0, 1)]
    strips = (ring(high, "gx", 1), low, high, ring(low, "gx", -1))
    yl, yr = call(edge_kernel, [arr(72, 8, 128)] * 2, [], *mains, *strips)
    from_left, from_right = ring(yr, "gy", 1), ring(yl, "gy", -1)
    own, zl, zr, black0, *set0 = call(
        level0_down_kernel,
        [arr(16, 2, 8, 128), arr(4, 2, 8, 128), arr(4, 2, 8, 128), arr(*L0.own())]
        + [arr(*s) for s in weights(L0)],
        level_scratch(L0) + nat_scratch(L0, 8),
        *mains, *strips, from_left, from_right, scal=scal,
    )
    from_left, from_right = ring(zr, "gz", 1), ring(zl, "gz", -1)
    bundle = call(widen_kernel, arr(16, 2, 8, 128), [], own, from_left, from_right)
    column = [bundle] + [trade(bundle, "gx", s) for s in (1, 2, 3)]
    yl, yr = call(strip_kernel, [arr(80, 8, 128)] * 2, [], *column)
    own, black1, *set1 = call(
        level1_down_kernel,
        [arr(16, 8, 128), arr(*L1.own())] + [arr(*s) for s in weights(L1)],
        level_scratch(L1) + nat_scratch(L1) + [scratch(4, 16, 2, 8, 128)],
        *column, ring(yr, "gy", 1), ring(yl, "gy", -1), scal=scal,
    )
    own = own[None]
    sheet = jnp.concatenate([own] + [trade(own, "gy", 2 * s) for s in (1, 2, 3)])
    sheet = both_cores(sheet)
    own, black2, *set2 = call(
        level2_down_kernel,
        [arr(8, 8, 128), arr(*L2.own())] + [arr(*s) for s in weights(L2)],
        level_scratch(L2) + nat_scratch(L2),
        sheet, scal=scal,
    )
    slabs = both_cores(jnp.stack([along_z(own, s) for s in (1, 2, 3, 4)]))
    return call(
        up_kernel, arr(16, 32, 128),
        [scratch(8, 8, 128), scratch(8, 24, 128), scratch(16, 24, 128)]
        + [scratch(*level.wide()) for level in (L2, L2, L1, L1, L0, L0)]
        + [scratch(16, 32, 128), scratch(16, 48, 128)]
        + level_scratch(L3) + [scratch(*s) for s in weights(L3)] + nat_scratch(L3)
        + [scratch(8, 8, 8, 128), scratch(4, 8, 16, 128), scratch(4, 16, 128), scratch(8, 32, 128)],
        own, slabs, black2, *set2, black1, *set1, black0, *set0, scal=scal,
    )


def solution(mesh):
    spec = P("gx", "gy", "gz")
    return jax.shard_map(on_device, mesh=mesh, in_specs=(spec, spec), out_specs=spec, check_vma=False)
```

```python
import functools

import jax
import jax.numpy as jnp
from jax import lax
from jax.experimental import pallas as pl
from jax.experimental.pallas import tpu as pltpu
from jax.sharding import PartitionSpec as P

SWEEPS = 2
ITERS = 20
F32 = jnp.float32
OFF = 1e-20
VMEM = pl.BlockSpec(memory_space=pltpu.VMEM)
SMEM = pl.BlockSpec(memory_space=pltpu.SMEM)


class Level:
    def __init__(self, count, rows, group, fold):
        self.count, self.rows, self.group, self.fold = count, rows, group, fold

    def wide(self):
        return (self.count + 2, 2, self.rows, 128)

    def own(self):
        return (self.count, 2, self.rows, 128)


L0 = Level(32, 24, 128, None)
L1 = Level(16, 24, 64, "x")
L2 = Level(16, 8, 32, "y")
L3 = Level(8, 8, 64, "y")


def lanes(rows):
    return lax.broadcasted_iota(jnp.int32, (rows, 128), 1)


def rows_of(rows):
    return lax.broadcasted_iota(jnp.int32, (rows, 128), 0)


def pick(values, index):
    return jnp.take_along_axis(values, index, axis=1, mode="promise_in_bounds")


def turn(values, shift):
    shift = shift % 128
    return pltpu.roll(values, shift, 1) if shift else values


def inverse_of(values):
    return pl.reciprocal(values, approx=True)


def up(level, values):
    rolled = pltpu.roll(values, level.rows - 1, 0)
    if level.fold == "y":
        rolled = jnp.where(rows_of(level.rows) == level.rows - 1, turn(rolled, -level.group), rolled)
    return rolled


def down(level, values):
    rolled = pltpu.roll(values, 1, 0)
    if level.fold == "y":
        rolled = jnp.where(rows_of(level.rows) == 0, turn(rolled, level.group), rolled)
    return rolled


def goes_back(colour, a, q):
    return (colour == 0) == ((a + q) % 2 == 0)


class Window:
    def __init__(self, ref, first):
        self.ref, self.first, self.kept = ref, first, {}

    def __call__(self, offset, q):
        if (offset, q) not in self.kept:
            self.kept[offset, q] = self.ref[self.first + offset, q]
        return self.kept[offset, q]


def beside(level, other, at, q, colour, a):
    mid = other(at + 1, q)
    across = other(at + 1, 1 - q)
    return [
        other(at + 2, q),
        other(at, q),
        across if q == 0 else up(level, across),
        down(level, across) if q == 0 else across,
        mid,
        turn(mid, 1 if goes_back(colour, a, q) else -1),
    ]


def planes(first, last, unroll, body, *refs):
    pairs = (last - first) // 2
    unroll = min(unroll, pairs)
    while pairs % unroll:
        unroll -= 1

    def step(i, carry):
        start = first + 2 * unroll * i
        windows = [Window(ref, start) for ref in refs]
        for at in range(2 * unroll):
            for q in (0, 1):
                if refs:
                    body(start + at, at, q, windows)
                else:
                    body(start + at, at % 2, q)
        return carry

    if pairs == unroll:
        step(0, 0)
    else:
        lax.fori_loop(0, pairs // unroll, step, 0)


def fill_ends(level, values, rest=0.0):
    lane = lanes(level.rows)
    for q in (0, 1):
        if level.fold == "x":
            values[0, q] = jnp.where(lane < 64, rest, turn(values[level.count, q], 64))
            values[level.count + 1, q] = jnp.where(lane < 64, turn(values[1, q], 64), rest)
        else:
            values[0, q] = jnp.full((level.rows, 128), rest, F32)
            values[level.count + 1, q] = jnp.full((level.rows, 128), rest, F32)


def set_up(level, cond, rec, wd, fd, dd):
    rows = level.rows
    row, lane = rows_of(rows), lanes(rows)
    for colour in (0, 1):
        fill_ends(level, rec[colour], OFF)

    def body(x, at, q, windows):
        a = at % 2
        for colour in (0, 1):
            own_rec = windows[colour](at + 1, q)
            near = beside(level, windows[1 - colour], at, q, colour, a)
            walls = {}
            if level.fold == "y":
                if q == 0:
                    walls[3] = (row == 0) & (lane < level.group)
                else:
                    walls[2] = (row == rows - 1) & (lane >= 128 - level.group)
            if level.group < 128:
                end = 0 if goes_back(colour, a, q) else level.group - 1
                walls[5] = lane % level.group == end
            total = None
            faces = []
            for i, value in enumerate(near):
                if i in walls:
                    value = jnp.where(walls[i], OFF, value)
                face = inverse_of(own_rec + value)
                faces.append(face)
                total = face if total is None else total + face
            inverse = jnp.where(own_rec > 1e-10, inverse_of(total), 0.0)
            for i, face in enumerate(faces):
                weight = face * inverse
                wd[colour][i, x, q] = jnp.where(walls[i], 0.0, weight) if i in walls else weight
            fd[colour][x, q] = fd[colour][x, q] * (0.5 * inverse)
            if colour == 0:
                dd[x, q] = total

    planes(0, level.count, 4 if level.rows == 8 else 2, body, *rec)


def relaxed(level, colour, x, at, q, window, wd, fd):
    near = beside(level, window, at, q, colour, at % 2)
    weight = wd[colour]
    one = fd[colour][x, q] + weight[0, x, q] * near[0]
    two = weight[4, x, q] * near[4] + weight[1, x, q] * near[1]
    one = one + weight[2, x, q] * near[2]
    two = two + weight[3, x, q] * near[3]
    return one + (two + weight[5, x, q] * near[5])


def half_sweep(level, colour, v, wd, fd, first=0, last=None):
    def body(x, at, q, windows):
        v[colour][x + 1, q] = relaxed(level, colour, x, at, q, windows[0], wd, fd)

    planes(first, level.count if last is None else last, 8 if level.rows == 8 else 7, body, v[1 - colour])
    if level.fold == "x":
        fill_ends(level, v[colour])


def first_half(level, v, fd):
    for colour in (0, 1):
        fill_ends(level, v[colour])

    def body(x, a, q):
        v[0][x + 1, q] = fd[0][x, q]

    planes(0, level.count, 4, body)
    if level.fold == "x":
        fill_ends(level, v[0])


def descend(level, v, wd, fd, dd, cond, out_f, out_b, ranges=None):
    ranges = ranges or [(0, level.count)] * 4
    first_half(level, v, fd)
    half_sweep(level, 1, v, wd, fd, *ranges[0])
    half_sweep(level, 0, v, wd, fd, *ranges[1])
    half_sweep(level, 1, v, wd, fd, *ranges[2])
    first, last = ranges[3]

    def body(i, carry):
        window = Window(v[1], first + 8 * i)
        for u in range(4):
            left = jnp.zeros((level.rows, 128), F32)
            mean = jnp.zeros((level.rows, 128), F32)
            for a in (0, 1):
                for q in (0, 1):
                    at = 2 * u + a
                    x = first + 8 * i + at
                    left = left + dd[x, q] * (relaxed(level, 0, x, at, q, window, wd, fd) - v[0][x + 1, q])
                    mean = mean + (cond[0][x, q] + cond[1][x, q])
            out_f[4 * i + u] = left
            out_b[4 * i + u] = 0.125 * mean
        return carry

    lax.fori_loop(0, (last - first) // 8, body, 0)


def ascend(level, v, wd, fd, ranges=None):
    ranges = ranges or [(0, level.count)] * 4
    for step in range(2 * SWEEPS):
        half_sweep(level, step % 2, v, wd, fd, *ranges[step])


def correct(level, v, black, add):
    for colour in (0, 1):
        fill_ends(level, v[colour])

    def body(x, a, q):
        v[1][x + 1, q] = black[x, q] + add[x // 2]

    planes(0, level.count, 4, body)
    if level.fold == "x":
        fill_ends(level, v[1])


def keep_black(level, v, black):
    def body(x, a, q):
        black[x, q] = v[1][x + 1, q]

    planes(0, level.count, 4, body)


def even_odd(v, x, a, q):
    red, black = v[0][x + 1, q], v[1][x + 1, q]
    return (red, black) if (a + q) % 2 == 0 else (black, red)


def exchange(blocks, width):
    group = lanes(8) // width
    step = len(blocks) // 2
    while step:
        swapped = list(blocks)
        for i in range(len(blocks)):
            if not i & step:
                a, b = blocks[i], blocks[i + step]
                low = group & step == 0
                swapped[i] = jnp.where(low, a, turn(b, width * step))
                swapped[i + step] = jnp.where(low, turn(a, -width * step), b)
        blocks = swapped
        step //= 2
    return blocks


def split_kernel(f_ref, b_ref, lo_ref, hi_ref, zl_ref, zr_ref):
    lane = lanes(16)
    whole = 2 * (lane % 64) + lane // 64
    slot = lane // 8
    within = lane % 8
    first = 2 * (within % 4) + within // 4
    last = 120 + first
    for half, out in enumerate((lo_ref, hi_ref)):
        for q in (0, 1):
            left = jnp.zeros((16, 128), F32)
            right = jnp.zeros((16, 128), F32)
            for x in range(8):
                for arr, ref in enumerate((f_ref, b_ref)):
                    cells = ref[8 * half + x, pl.ds(q, 16, stride=2), :]
                    out[8 * arr + x, q] = pick(cells, whole)
                    here = slot == 2 * x + arr
                    left = jnp.where(here, pick(cells, first), left)
                    right = jnp.where(here, pick(cells, last), right)
            zl_ref[half, q] = left
            zr_ref[half, q] = turn(right, 60)


def edge_kernel(*refs):
    mains, strips, lo_ref, hi_ref = refs[0:4], refs[4:8], refs[8], refs[9]
    low = rows_of(8) < 4
    for t in range(4):
        for i in range(18):
            ref, at = (mains[t], i) if i < 16 else (strips[t], i - 16)
            lo_ref[18 * t + i] = jnp.where(low, ref[at, 0, 0:8], pltpu.roll(ref[at, 1, 0:8], 4, 0))
            hi_ref[18 * t + i] = jnp.where(low, pltpu.roll(ref[at, 1, 8:16], 4, 0), ref[at, 0, 8:16])


def level0_down_kernel(
    scal, m0, m1, m2, m3, s0, s1, s2, s3, yl_ref, yr_ref,
    own_ref, zl_ref, zr_ref, black_ref, wd0, wd1, fd0, fd1,
    cond0, cond1, rec0, rec1, v0, v1, dd, nat_f, nat_b,
):
    cond, rec, v, wd, fd = (cond0, cond1), (rec0, rec1), (v0, v1), (wd0, wd1), (fd0, fd1)
    gx, gy, gz = scal[0], scal[1], scal[2]
    lane, row = lanes(24), rows_of(24)
    inside = (lane < 68) | (lane >= 124)
    inside = inside & ((gz > 0) | (lane < 124)) & ((gz < 7) | (lane < 64) | (lane >= 124))
    inside = inside & ((gy > 0) | (row < 20)) & ((gy < 7) | (row < 16) | (row >= 20))
    keep = jnp.where(inside, 1.0, 0.0)
    low = rows_of(8) < 4
    for t, (main_ref, strip_ref) in enumerate(((m0, s0), (m1, s1), (m2, s2), (m3, s3))):
        here = keep
        if t == 0:
            here = keep * jnp.where(gx > 0, 1.0, 0.0)
        if t == 3:
            here = keep * jnp.where(gx < 3, 1.0, 0.0)

        def wide(i, q):
            right, left = yr_ref[18 * t + i], yl_ref[18 * t + i]
            edge = jnp.where(low, right, left) if q == 0 else pltpu.roll(jnp.where(low, left, right), 4, 0)
            own = main_ref[i, q] if i < 16 else strip_ref[i - 16, q]
            return jnp.concatenate([own, edge], axis=0)

        ends = [(wide(16, q), wide(17, q)) for q in (0, 1)]
        for x in range(8):
            for q in (0, 1):
                from_left, from_right = ends[q]
                for arr in (0, 1):
                    s = 2 * x + arr
                    main = wide(8 * arr + x, q)
                    edge = jnp.where(lane // 8 == s, from_right, from_left)
                    even = jnp.where(lane < 64, main, turn(edge, 64 - 8 * s))
                    odd = jnp.where(lane < 64, turn(main, 64), turn(edge, 60 - 8 * s))
                    cells = (even, odd) if (x + q) % 2 == 0 else (odd, even)
                    for colour in (0, 1):
                        if arr == 0:
                            fd[colour][8 * t + x, q] = cells[colour]
                        else:
                            on_grid = cells[colour] * here
                            cond[colour][8 * t + x, q] = on_grid
                            rec[colour][8 * t + x + 1, q] = jnp.where(
                                here > 0.0, inverse_of(cells[colour]), OFF
                            )
    set_up(L0, cond, rec, wd, fd, dd)
    descend(L0, v, wd, fd, dd, cond, nat_f, nat_b, [(2, 30), (2, 30), (4, 28), (8, 24)])
    keep_black(L0, v, black_ref)
    lane8 = lanes(8)
    k = lane8 % 64
    spread = 2 * jnp.clip(k - 16, 0, 31) + lane8 // 64
    near = 2 * (lane8 % 16) + (lane8 // 16) % 2
    for x in range(0, 8, 2):
        for q in (0, 1):
            left, right = [], []
            for a in (0, 1):
                f = nat_f[x + a, pl.ds(q, 8, stride=2), :]
                b = nat_b[x + a, pl.ds(q, 8, stride=2), :]
                own_ref[x + a, q] = pick(f, spread)
                own_ref[8 + x + a, q] = pick(b, spread)
                here = lane8 % 64 < 32
                left.append(jnp.where(here, pick(f, near), pick(b, near)))
                right.append(jnp.where(here, pick(f, near + 32), pick(b, near + 32)))
            zl_ref[x // 2, q] = jnp.where(lane8 < 64, left[0], left[1])
            zr_ref[x // 2, q] = jnp.where(lane8 < 64, right[0], right[1])


def widen_kernel(own_ref, left_ref, right_ref, out_ref):
    lane = lanes(8)
    k = lane % 64
    index = lane % 16 + 16 * (lane // 64)
    for x in range(8):
        for q in (0, 1):
            for arr in (0, 1):
                there = index + 64 * (x % 2) + 32 * arr
                edge = jnp.where(k < 16, pick(left_ref[x // 2, q], there), pick(right_ref[x // 2, q], there))
                out_ref[8 * arr + x, q] = jnp.where((k >= 16) & (k < 48), own_ref[8 * arr + x, q], edge)


def strip_kernel(a_ref, b_ref, c_ref, d_ref, lo_ref, hi_ref):
    low = rows_of(8) < 4
    for t, ref in enumerate((a_ref, b_ref, c_ref, d_ref)):
        for i in range(16):
            zero, one = ref[i, 0], ref[i, 1]
            lo_ref[20 * t + i] = jnp.where(low, zero, pltpu.roll(one, 4, 0))
            hi_ref[20 * t + i] = jnp.where(low, pltpu.roll(zero, 4, 0), one)
            for q in (0, 1):
                row = 2 * (i % 4) + q
                lo_ref[20 * t + 16 + i // 4, row : row + 1] = ref[i, q, 4:5]
                hi_ref[20 * t + 16 + i // 4, row : row + 1] = ref[i, q, 3:4]


def level1_down_kernel(
    scal, a_ref, b_ref, c_ref, d_ref, yl_ref, yr_ref,
    out_ref, black_ref, wd0, wd1, fd0, fd1,
    cond0, cond1, rec0, rec1, v0, v1, dd, nat_f, nat_b, own,
):
    cond, rec, v, wd, fd = (cond0, cond1), (rec0, rec1), (v0, v1), (wd0, wd1), (fd0, fd1)
    gx, gy, gz = scal[0], scal[1], scal[2]
    lane = lanes(8)
    k = lane % 64
    inside = ((gz > 0) | (k >= 16)) & ((gz < 7) | (k < 48))
    keep = jnp.where(inside, 1.0, 0.0)
    row = rows_of(8)
    for i, ref in enumerate((a_ref, b_ref, c_ref, d_ref)):
        own[i] = ref[...]
    for block in range(3):
        here = keep
        if block == 0:
            here = jnp.where(row >= 3, keep, 0.0) * jnp.where(gy > 0, 1.0, 0.0)
        if block == 2:
            here = jnp.where(row < 5, keep, 0.0) * jnp.where(gy < 7, 1.0, 0.0)
        rows = pl.ds(8 * block, 8)

        def cells_of(slot, i, q):
            if block == 1:
                return own[slot, i, q]
            ref = yl_ref if block == 0 else yr_ref
            cells = ref[20 * slot + i]
            if (block == 0) == (q == 0):
                cells = pltpu.roll(cells, 4, 0)
            at = 2 * (i % 4) + q
            single = ref[20 * slot + 16 + i // 4, at : at + 1]
            return jnp.where(row == (3 if block == 0 else 4), single, cells)

        def body(j, carry):
            slots = [gx ^ j, gx ^ (j + 2)]
            for x in range(8):
                for q in (0, 1):
                    parts = []
                    for arr in (0, 8):
                        first, second = [cells_of(slot, arr + x, q) for slot in slots]
                        parts.append(jnp.where(lane < 64, first, turn(second, 64)))
                        parts.append(jnp.where(lane < 64, turn(first, 64), second))
                    for colour in (0, 1):
                        odd = (x + q + colour) % 2
                        fd[colour][8 * j + x, q, rows] = parts[odd]
                        cond[colour][8 * j + x, q, rows] = parts[2 + odd] * here
                        rec[colour][8 * j + x + 1, q, rows] = jnp.where(
                            here > 0.0, inverse_of(parts[2 + odd]), OFF
                        )
            return carry

        lax.fori_loop(0, 2, body, 0)
    set_up(L1, cond, rec, wd, fd, dd)
    descend(L1, v, wd, fd, dd, cond, nat_f, nat_b)
    keep_black(L1, v, black_ref)
    for h in (0, 1):
        index = 64 * h + 2 * (lane % 32) + (lane // 32) % 2
        for x in range(8):
            f = pick(nat_f[x, 8:16], index)
            b = pick(nat_b[x, 8:16], index)
            nat_f[x, 0:8] = jnp.where(lane < 64, f, b)
            for q in (0, 1):
                out_ref[8 * h + x, 4 * q : 4 * q + 4] = nat_f[x, pl.ds(q, 4, stride=2), :]


def level2_down_kernel(
    scal, in_ref,
    out_ref, black_ref, wd0, wd1, fd0, fd1,
    cond0, cond1, rec0, rec1, v0, v1, dd, nat_f, nat_b,
):
    cond, rec, v, wd, fd = (cond0, cond1), (rec0, rec1), (v0, v1), (wd0, wd1), (fd0, fd1)
    gy, gz = scal[1], scal[2]
    chip = gy // 2
    lane = lanes(8)
    k = lane % 32
    inside = ((gz > 0) | (k >= 8)) & ((gz < 7) | (k < 24))
    slots = [chip ^ j for j in range(4)]

    def body(x, a, q):
        mains = []
        for slot in slots:
            both = [in_ref[c, slot, x, 4 * q : 4 * q + 4] for c in (0, 1)]
            mains.append(jnp.concatenate(both, axis=0))
        parts = exchange(mains, 32)
        for colour in (0, 1):
            odd = (a + q + colour) % 2
            fd[colour][x, q] = parts[odd]
            cond[colour][x, q] = jnp.where(inside, parts[2 + odd], 0.0)
            rec[colour][x + 1, q] = jnp.where(inside, inverse_of(parts[2 + odd]), OFF)

    planes(0, 16, 4, body)
    set_up(L2, cond, rec, wd, fd, dd)
    descend(L2, v, wd, fd, dd, cond, nat_f, nat_b)
    keep_black(L2, v, black_ref)
    index = 32 * (lane // 32) + 8 + 2 * (lane % 8) + (lane // 8) % 2
    for x in range(8):
        packed = jnp.where(lane % 32 < 16, pick(nat_f[x], index), pick(nat_b[x], index))
        out_ref[x] = packed


def coarsest(f, b):
    lane, row = lanes(8), rows_of(8)
    x, k = lane // 32, lane % 32

    def near(values, colour, q):
        back = (x + q + colour) % 2 == 0
        across = values[1 - q]
        return [
            values[q],
            across,
            turn(values[q], -32),
            turn(values[q], 32),
            pltpu.roll(across, 1 if q == 0 else 7, 0),
            pick(values[q], (lane + jnp.where(back, 127, 1)) % 128),
        ]

    rec = [[inverse_of(cells) for cells in pair] for pair in b]
    weights, sources = [], []
    for colour in (0, 1):
        weights.append([])
        sources.append([])
        for q in (0, 1):
            back = (x + q + colour) % 2 == 0
            walls = [
                None, None, x == 3, x == 0, row == (0 if q == 0 else 7), k == jnp.where(back, 0, 31),
            ]
            faces, total = [], None
            for value, wall in zip(near(rec[1 - colour], colour, q), walls):
                if wall is not None:
                    value = jnp.where(wall, OFF, value)
                face = inverse_of(rec[colour][q] + value)
                total = face if total is None else total + face
                faces.append(face if wall is None else jnp.where(wall, 0.0, face))
            inverse = inverse_of(total)
            weights[-1].append([face * inverse for face in faces])
            sources[-1].append(f[colour][q] * (0.5 * inverse))

    def half(colour, other):
        made = []
        for q in (0, 1):
            total = sources[colour][q]
            for weight, value in zip(weights[colour][q], near(other, colour, q)):
                total = total + weight * value
            made.append(total)
        return made

    black = half(1, sources[0])

    def step(_, carry):
        return tuple(half(1, half(0, list(carry))))

    black = lax.fori_loop(0, ITERS - 2, step, tuple(black))
    red = half(0, list(black))
    return red, half(1, red)


def coarse_kernel(
    scal, own_ref, all_ref, out_ref,
    cond30, cond31, rec30, rec31, v30, v31, dd3, wd30, wd31, fd30, fd31, nat_f, nat_b,
    slabs, whole, nat4, nat3,
):
    cond3, rec3, v3, wd3, fd3 = (cond30, cond31), (rec30, rec31), (v30, v31), (wd30, wd31), (fd30, fd31)
    gz = scal[2]
    lane = lanes(8)
    slabs[gz] = own_ref[...]
    for j in range(4):
        slabs[gz ^ (1 + j)] = all_ref[0, j]
        if j < 3:
            slabs[gz ^ (5 + j)] = all_ref[1, j]

    for x in range(8):
        for c, cells in enumerate(exchange([slabs[r, x] for r in range(8)], 8)):
            whole[c % 4, x, 8 * (c // 4) : 8 * (c // 4) + 8] = cells

    def place3(x, a, q):
        for colour in (0, 1):
            odd = (a + q + colour) % 2
            fd3[colour][x, q] = whole[odd, x, pl.ds(q, 8, stride=2), :]
            cells = whole[2 + odd, x, pl.ds(q, 8, stride=2), :]
            cond3[colour][x, q] = cells
            rec3[colour][x + 1, q] = inverse_of(cells)

    planes(0, 8, 4, place3)
    set_up(L3, cond3, rec3, wd3, fd3, dd3)
    descend(L3, v3, wd3, fd3, dd3, cond3, nat_f, nat_b)
    f4 = [[None, None], [None, None]]
    b4 = [[None, None], [None, None]]
    for x in range(4):
        for arr, plane in enumerate((nat_f[x], nat_b[x])):
            for part in (0, 1):
                whole[arr, x, 8 * part : 8 * part + 8] = turn(plane, 64 * part)
        for made, arr in ((f4, 0), (b4, 1)):
            for q in (0, 1):
                cells = whole[arr, x, pl.ds(q, 8, stride=2), :]
                for colour in (0, 1):
                    mine = pick(cells, 2 * (lane % 32) + (x + q + colour) % 2)
                    before = made[colour][q]
                    made[colour][q] = mine if x == 0 else jnp.where(lane // 32 == x, mine, before)
    red, black = coarsest(f4, b4)
    for x in range(4):
        for q in (0, 1):
            even, odd = (red[q], black[q]) if (x + q) % 2 == 0 else (black[q], red[q])
            index = 32 * x + (lane % 64) // 2
            nat4[x, pl.ds(q, 8, stride=2), :] = jnp.where(lane % 2 == 0, pick(even, index), pick(odd, index))
    for x in range(4):
        nat_f[x] = jnp.where(lane < 64, nat4[x, 0:8], turn(nat4[x, 8:16], 64))

    def add(x, a, q):
        v3[1][x + 1, q] = v3[1][x + 1, q] + nat_f[x // 2]

    planes(0, 8, 4, add)
    ascend(L3, v3, wd3, fd3)
    place = 16 * gz - 8 + lane % 32
    z = jnp.clip(place, 0, 127)
    index = (z % 2) * 64 + z // 2
    for x in range(8):
        for q in (0, 1):
            even, odd = even_odd(v3, x, x, q)
            first = pick(jnp.where(lane < 64, even, turn(odd, 64)), index)
            second = pick(jnp.where(lane < 64, turn(even, 64), odd), index)
            nat3[x, pl.ds(q, 8, stride=2), :] = first
            nat3[x, pl.ds(16 + q, 8, stride=2), :] = second
        cells = nat3[x, 0:8]
        for j in (1, 2, 3):
            cells = jnp.where(lane // 32 == j, nat3[x, 8 * j : 8 * j + 8], cells)
        out_ref[x] = jnp.where(place == z, cells, 0.0)


def level2_up_kernel(scal, black_ref, wd0, wd1, fd0, fd1, add_ref, out_ref, v0, v1, nat):
    v, wd, fd = (v0, v1), (wd0, wd1), (fd0, fd1)
    gy = scal[1]
    correct(L2, v, black_ref, add_ref)
    ascend(L2, v, wd, fd)
    lane = lanes(8)
    k = lane % 64
    base = (gy + 1) // 2 - 1
    groups = [base, base + 1]

    def store(x, a, q):
        even, odd = even_odd(v, x, a, q)
        for i, mq in enumerate(groups):
            index = 32 * jnp.clip(mq, 0, 3) + k // 2
            cells = jnp.where(lane % 2 == 0, pick(even, index), pick(odd, index))
            nat[x, pl.ds(16 * i + q, 8, stride=2), :] = jnp.where((mq >= 0) & (mq < 4), cells, 0.0)

    planes(0, 16, 4, store)
    start = pl.multiple_of(8 - 8 * (gy % 2), 8)
    side = lanes(24) < 64
    for x in range(8):
        out_ref[x] = jnp.where(side, nat[x, pl.ds(start, 24), :], nat[8 + x, pl.ds(start, 24), :])


def level1_up_kernel(scal, black_ref, wd0, wd1, fd0, fd1, add_ref, out_ref, v0, v1, nat):
    v, wd, fd = (v0, v1), (wd0, wd1), (fd0, fd1)
    gx = scal[0]
    correct(L1, v, black_ref, add_ref)
    ascend(L1, v, wd, fd)
    lane = lanes(24)
    z = jnp.where(lane < 96, lane, lane - 128) + 32
    index = jnp.clip(z // 2, 0, 63)

    def store(i, carry):
        for u in range(4):
            x = 8 * gx - 4 + 4 * i + u
            inside = (x >= 0) & (x < 32)
            x = jnp.clip(x, 0, 31)
            there = 64 * (x // 16) + index
            for q in (0, 1):
                even, odd = even_odd(v, x % 16, u, q)
                cells = jnp.where(lane % 2 == 0, pick(even, there), pick(odd, there))
                nat[4 * i + u, pl.ds(q, 24, stride=2), :] = jnp.where(inside, cells, 0.0)
        return carry

    lax.fori_loop(0, 4, store, 0)
    for x in range(16):
        out_ref[x, 0:16] = nat[x, 16:32]
        out_ref[x, 16:20] = nat[x, 32:36]
        out_ref[x, 20:24] = nat[x, 12:16]


def level0_up_kernel(black_ref, wd0, wd1, fd0, fd1, add_ref, out_ref, v0, v1):
    v, wd, fd = (v0, v1), (wd0, wd1), (fd0, fd1)
    correct(L0, v, black_ref, add_ref)
    ascend(L0, v, wd, fd, [(4, 28), (6, 26), (6, 26), (8, 24)])
    lane = lanes(16)
    index = (lane % 2) * 64 + lane // 2

    def store(x, a, q):
        even, odd = even_odd(v, x, a, q)
        packed = jnp.where(lane < 64, even[0:16], turn(odd[0:16], 64))
        out_ref[x - 8, pl.ds(q, 16, stride=2), :] = pick(packed, index)

    planes(8, 24, 4, store)


def up_kernel(scal, own_ref, all_ref, *refs):
    set2, set1, set0 = refs[0:5], refs[5:10], refs[10:15]
    out_ref, add2, add1, add0, v0, v1, w0, w1, x0, x1, nat2, nat1, *rest = refs[15:]
    coarse_kernel(scal, own_ref, all_ref, add2, *rest)
    level2_up_kernel(scal, *set2, add2, add1, v0, v1, nat2)
    level1_up_kernel(scal, *set1, add1, add0, w0, w1, nat1)
    level0_up_kernel(*set0, add0, out_ref, x0, x1)


def arr(*shape):
    return jax.ShapeDtypeStruct(shape, F32)


def scratch(*shape):
    return pltpu.VMEM(shape, F32)


def level_scratch(level):
    shapes = [level.own()] * 2 + [level.wide()] * 4 + [level.own()]
    return [scratch(*s) for s in shapes]


def nat_scratch(level, count=None):
    return [scratch(count or level.count // 2, level.rows, 128)] * 2


def weights(level):
    return [(6,) + level.own()] * 2 + [level.own()] * 2


def call(kernel, outs, temps, *args, scal=None, limit=28):
    specs = [VMEM] * len(args)
    if scal is not None:
        specs = [SMEM] + specs
        args = (scal,) + args
    return pl.pallas_call(
        kernel,
        out_shape=outs,
        in_specs=specs,
        out_specs=jax.tree.map(lambda _: VMEM, outs),
        scratch_shapes=temps,
        compiler_params=pltpu.CompilerParams(vmem_limit_bytes=limit * 1024 * 1024),
    )(*args)


def ring(values, axis, step):
    count = lax.axis_size(axis)
    return lax.ppermute(values, axis, [(i, (i + step) % count) for i in range(count)])


def trade(values, axis, step):
    return lax.ppermute(values, axis, [(i, i ^ step) for i in range(lax.axis_size(axis))])


def both_cores(values):
    count = lax.axis_size("gy")
    return lax.all_gather(values, "gy", axis=0, axis_index_groups=[[i, i + 1] for i in range(0, count, 2)])


def along_z(values, step):
    rows, count = lax.axis_size("gy"), lax.axis_size("gz")
    pairs = []
    for i in range(rows):
        for k in range(count):
            pairs.append((i * count + k, i * count + (k ^ (step | 4 * (i % 2)))))
    return lax.ppermute(values, ("gy", "gz"), pairs)


def on_device(right_side, coefficient):
    scal = jnp.stack([lax.axis_index("gx"), lax.axis_index("gy"), lax.axis_index("gz")]).astype(jnp.int32)
    half = arr(16, 2, 16, 128)
    strip = arr(2, 2, 16, 128)
    lo, hi, zl, zr = call(split_kernel, [half, half, strip, strip], [], right_side, coefficient)
    from_left, from_right = ring(zr, "gz", 1), ring(zl, "gz", -1)
    mains = (ring(hi, "gx", 1), lo, hi, ring(lo, "gx", -1))
    low, high = [jnp.concatenate([from_left[i : i + 1], from_right[i : i + 1]]) for i in (0, 1)]
    strips = (ring(high, "gx", 1), low, high, ring(low, "gx", -1))
    yl, yr = call(edge_kernel, [arr(72, 8, 128)] * 2, [], *mains, *strips)
    from_left, from_right = ring(yr, "gy", 1), ring(yl, "gy", -1)
    own, zl, zr, black0, *set0 = call(
        level0_down_kernel,
        [arr(16, 2, 8, 128), arr(4, 2, 8, 128), arr(4, 2, 8, 128), arr(*L0.own())]
        + [arr(*s) for s in weights(L0)],
        level_scratch(L0) + nat_scratch(L0, 8),
        *mains, *strips, from_left, from_right, scal=scal,
    )
    from_left, from_right = ring(zr, "gz", 1), ring(zl, "gz", -1)
    bundle = call(widen_kernel, arr(16, 2, 8, 128), [], own, from_left, from_right)
    column = [bundle] + [trade(bundle, "gx", s) for s in (1, 2, 3)]
    yl, yr = call(strip_kernel, [arr(80, 8, 128)] * 2, [], *column)
    own, black1, *set1 = call(
        level1_down_kernel,
        [arr(16, 8, 128), arr(*L1.own())] + [arr(*s) for s in weights(L1)],
        level_scratch(L1) + nat_scratch(L1) + [scratch(4, 16, 2, 8, 128)],
        *column, ring(yr, "gy", 1), ring(yl, "gy", -1), scal=scal,
    )
    own = own[None]
    sheet = jnp.concatenate([own] + [trade(own, "gy", 2 * s) for s in (1, 2, 3)])
    sheet = both_cores(sheet)
    own, black2, *set2 = call(
        level2_down_kernel,
        [arr(8, 8, 128), arr(*L2.own())] + [arr(*s) for s in weights(L2)],
        level_scratch(L2) + nat_scratch(L2),
        sheet, scal=scal,
    )
    slabs = both_cores(jnp.stack([along_z(own, s) for s in (1, 2, 3, 4)]))
    return call(
        up_kernel, arr(16, 32, 128),
        [scratch(8, 8, 128), scratch(8, 24, 128), scratch(16, 24, 128)]
        + [scratch(*level.wide()) for level in (L2, L2, L1, L1, L0, L0)]
        + [scratch(16, 32, 128), scratch(16, 48, 128)]
        + level_scratch(L3) + [scratch(*s) for s in weights(L3)] + nat_scratch(L3)
        + [scratch(8, 8, 8, 128), scratch(4, 8, 16, 128), scratch(4, 16, 128), scratch(8, 32, 128)],
        own, slabs, black2, *set2, black1, *set1, black0, *set0, scal=scal,
    )


def solution(mesh):
    spec = P("gx", "gy", "gz")
    return jax.shard_map(on_device, mesh=mesh, in_specs=(spec, spec), out_specs=spec, check_vma=False)
```
